32 devices in a mesh: dp: 8 (over y, x, core), tensor: 4 (over z).
Axes of the slice: x: 2, y: 2, z: 4, core: 2. Of those that a mesh axis runs over, the one named last changes fastest.
Arguments:
- tokens: bfloat16 [8192, 1024], P('dp'), may hold values from -6 to 6
- memory: bfloat16 [8, 1024, 1024], P('dp'), may hold values from -6 to 6
- segments: int32 [8, 2048], P('dp'), may hold values from 0 to 3, never falling along the last dimension, each value on 1 to 1024 neighbouring positions
- value_routes: int32 [8, 2048, 4, 2], P('dp', None, 'tensor'), may hold values from 0 to 4, all different within a row
- output_routes: int32 [8192, 4, 2], P('dp', 'tensor'), may hold values from 0 to 4, all different within a row
- first_gain: float32 [1024], replicated, may hold values from 0.5 to 1.5
- first_bias: float32 [1024], replicated, may hold values from -4 to 4
- second_gain: float32 [1024], replicated, may hold values from 0.5 to 1.5
- second_bias: float32 [1024], replicated, may hold values from -4 to 4
- query_head_weight: bfloat16 [4, 1024, 112], P('tensor'), may hold values from -0.1875 to 0.1875
- key_weight: bfloat16 [4, 1024, 112], P('tensor'), may hold values from -0.1875 to 0.1875
- position_weight: bfloat16 [4, 1024, 112], P('tensor'), may hold values from -0.1875 to 0.1875
- value_weight: bfloat16 [4, 1024, 560], P('tensor'), may hold values from -0.1875 to 0.1875
- value_select: bfloat16 [4, 1024, 5], P('tensor'), may hold values from -0.375 to 0.375
- output_expert_selector: bfloat16 [4, 1024, 5], P('tensor'), may hold values from -0.375 to 0.375
- output_expert_weight: bfloat16 [4, 560, 1024], P('tensor'), may hold values from -3 to 3
- content_bias: float32 [4, 112], P('tensor'), may hold values from -6 to 6
- position_bias: float32 [4, 112], P('tensor'), may hold values from -6 to 6
- up_projection_weight: bfloat16 [1024, 4096], P(None, 'tensor'), may hold values from -0.1875 to 0.1875
- down_projection_weight: bfloat16 [4096, 1024], P('tensor'), may hold values from -0.125 to 0.125
- cotangent: bfloat16 [8192, 1024], P(('dp', 'tensor')), may hold values from -6 to 6
Outputs:
- result: bfloat16 [8192, 1024], P(('dp', 'tensor'))
- tokens_gradient: float32 [8192, 1024], P(('dp', 'tensor'))
- first_gain_gradient: float32 [1024], replicated
- first_bias_gradient: float32 [1024], replicated
- second_gain_gradient: float32 [1024], replicated
- second_bias_gradient: float32 [1024], replicated
- query_weight_gradient: float32 [4, 1024, 112], P('tensor', 'dp')
- key_weight_gradient: float32 [4, 1024, 112], P('tensor', 'dp')
- position_weight_gradient: float32 [4, 1024, 112], P('tensor', 'dp')
- value_weight_gradient: float32 [4, 1024, 560], P('tensor', 'dp')
- value_select_gradient: float32 [4, 1024, 5], P('tensor', 'dp')
- output_select_gradient: float32 [4, 1024, 5], P('tensor', 'dp')
- output_weight_gradient: float32 [4, 560, 1024], P('tensor', None, 'dp')
- content_bias_gradient: float32 [4, 112], replicated
- position_bias_gradient: float32 [4, 112], replicated
- up_weight_gradient: float32 [1024, 4096], P('dp', 'tensor')
- down_weight_gradient: float32 [4096, 1024], P('tensor', 'dp')
The draws below stay inside these ranges and needn't reach their ends.
Inputs may be any that keep to these rules, and one draw needn't show every extreme that they name: `value_routes`: each row names 2 different value experts of its head. `output_routes`: each row names 2 different output experts of its head. `segments`: numbers never fall along a row.
All inputs are finite; a program needn't handle non-finite values.
Results may differ from the reference program's by a relative error of at most 0.023.
Values may be sent and summed in bfloat16 or wider, within the bound.
No kernel may reach another device: no remote copies, remote signals or barrier semaphores. Data moves between devices by JAX's collectives and lax.ppermute only.
A program may use at most 192 MiB of HBM per device.

```python
import math
from functools import partial
import jax
import jax.numpy as jnp
import numpy as np
from jax import lax

D = 1024
H = 4
DH = 112
E = 5
TOP = 2
FF = 4096
LEN = 1024
MEM = 1024
BLOCK = 512
KEYS = 2048
SEQS = 8
TOKENS = 8192


def spiked(array, stream_key, source, target, shards_of, factor):
    def block_of(dim):
        return (jnp.arange(array.shape[dim]) // (array.shape[dim] // shards_of)).reshape((-1,) + (1,) * (array.ndim - 1 - dim))

    first = jax.random.permutation(stream_key, shards_of)[block_of(target)]
    far = (block_of(target) + shards_of // 2) % shards_of
    return jnp.where((block_of(source) == first) | (block_of(source) == far), factor * array, array)


def levels(rng, dims, shards, least, high):
    factor_of, own = 1.0, jax.random.fold_in(rng, 6)
    for axis_at, blocks in shards:
        draws = jnp.exp(jax.random.uniform(jax.random.fold_in(own, axis_at), (blocks,), jnp.float32, least / len(shards), high / len(shards)))
        factor_of = factor_of * jnp.repeat(draws, dims[axis_at] // blocks).reshape([-1 if axis == axis_at else 1 for axis in range(len(dims))])
    return factor_of


def distinct(rng, rows, number_of, top, lift):
    ranking = jax.random.permutation(jax.random.fold_in(rng, 1), number_of)
    boost = ranking
    for power in range(3):
        boost = boost * boost // number_of
    boost = boost * lift // number_of
    lots = jax.random.randint(jax.random.fold_in(rng, 2), (rows, number_of), 0, 4096) + boost
    holders = jax.random.permutation(jax.random.fold_in(rng, 3), rows)[jnp.arange(number_of) % rows]
    lots = jnp.where(jnp.arange(rows)[:, None] == holders[None, :], 1 << 14, lots)
    priority = lots * number_of + jnp.arange(number_of)
    return lax.top_k(priority.astype(jnp.int32), top)[1].astype(jnp.int32)


def profile(count, total, reach, slope):
    weights = [(1 << 20) // math.isqrt(standing ** slope) + 1 for standing in range(2, count + 1)]
    rest, given = total - reach - (count - 1), [1] * (count - 1)
    while rest > 0:
        movable = [i for i in range(count - 1) if given[i] < reach]
        pool, remaining = sum([weights[i] for i in movable]), rest
        for i in movable:
            more = min(reach - given[i], max(1, remaining * weights[i] // pool), rest)
            given[i] = given[i] + more
            rest = rest - more
    return np.array([reach] + given)


def uneven(rng, count, total, reach, skew):
    if count == 2:
        one = jax.random.randint(rng, (), max(1, total - reach), min(reach, total - 1) + 1)
        return jnp.stack([one, total - one])
    sizes = jnp.asarray(profile(count, total, reach, skew), jnp.int32)
    pairs = (count - 1) // 2
    donor, taker = sizes[1:1 + 2 * pairs:2], sizes[2:2 + 2 * pairs:2]
    slack = jnp.minimum(donor - 1, reach - taker)
    moved = jax.random.randint(jax.random.fold_in(rng, 1), (pairs,), 0, 1 << 20) % (slack + 1)
    sizes = sizes.at[1:1 + 2 * pairs:2].set(donor - moved).at[2:2 + 2 * pairs:2].set(taker + moved)
    return sizes[jax.random.permutation(jax.random.fold_in(rng, 2), count)]


def bell_draw(stream_key, shape, deviation, bound, cuts=(), kind=jnp.bfloat16):
    drawn = deviation * jax.random.normal(stream_key, shape, jnp.float32)
    if cuts:
        drawn = drawn * levels(stream_key, shape, cuts, -0.22, 0.18)
    return jnp.clip(drawn, -bound, bound).astype(kind)


def heavy_noise(stream_key, extent, deviation, limit, cuts, heavy, held_as=jnp.bfloat16):
    result = deviation * jax.random.normal(stream_key, extent, jnp.float32)
    if cuts:
        result = result * levels(stream_key, extent, cuts, -0.22, 0.18)
    return jnp.clip(spiked(result, jax.random.fold_in(stream_key, 3), *heavy), -limit, limit).astype(held_as)


def setup_inputs(seed: int = 0) -> dict:
    keys = jax.random.split(jax.random.key(seed), 22)
    tokens = bell_draw(keys[0], (TOKENS, D), 1.0, 6.0, ((0, 8),))
    memory = bell_draw(keys[1], (SEQS, MEM, D), 1.0, 6.0, ((0, 8),))
    segments = jax.vmap(lambda own: jnp.searchsorted(jnp.cumsum(uneven(own, 4, KEYS, KEYS // 2, 0)), jnp.arange(KEYS), side="right"))(jax.random.split(keys[2], SEQS)).reshape((SEQS, KEYS)).astype(jnp.int32)
    value_routes = distinct(keys[3], SEQS * KEYS * H, E, TOP, 0).reshape((SEQS, KEYS, H, TOP))
    output_routes = distinct(keys[4], TOKENS * H, E, TOP, 0).reshape((TOKENS, H, TOP))
    first_gain = jnp.clip(1.0 + 0.1 * jax.random.normal(keys[5], (D,), jnp.float32), 0.5, 1.5)
    first_bias = bell_draw(keys[6], (D,), 0.3, 4.0, (), jnp.float32)
    second_gain = jnp.clip(1.0 + 0.1 * jax.random.normal(keys[7], (D,), jnp.float32), 0.5, 1.5)
    second_bias = bell_draw(keys[8], (D,), 0.3, 4.0, (), jnp.float32)
    query_head_weight = bell_draw(keys[9], (H, D, DH), D ** -0.5, 0.1875, ((0, 4),))
    key_weight = bell_draw(keys[10], (H, D, DH), D ** -0.5, 0.1875, ((0, 4),))
    position_weight = bell_draw(keys[11], (H, D, DH), D ** -0.5, 0.1875, ((0, 4),))
    value_weight = bell_draw(keys[12], (H, D, E * DH), D ** -0.5, 0.1875, ((0, 4),))
    value_select = bell_draw(keys[13], (H, D, E), (D // 4) ** -0.5, 0.375, ((0, 4),))
    output_expert_selector = bell_draw(keys[14], (H, D, E), (D // 4) ** -0.5, 0.375, ((0, 4),))
    output_expert_weight = bell_draw(keys[15], (H, E * DH, D), 4 ** -0.5, 3.0, ((0, 4),))
    content_bias = bell_draw(keys[16], (H, DH), 0.7, 6.0, ((0, 4),), jnp.float32)
    position_bias = bell_draw(keys[17], (H, DH), 0.7, 6.0, ((0, 4),), jnp.float32)
    up_projection_weight = bell_draw(keys[18], (D, FF), D ** -0.5, 0.1875, ((1, 4),))
    down_projection_weight = bell_draw(keys[19], (FF, D), (FF // 2) ** -0.5, 0.125, ((0, 4),))
    cotangent = heavy_noise(keys[20], (TOKENS, D), 1.0, 6.0, ((0, 32),), (0, 1, 32, 2.75))
    return {"tokens": tokens, "memory": memory, "segments": segments, "value_routes": value_routes, "output_routes": output_routes, "first_gain": first_gain, "first_bias": first_bias, "second_gain": second_gain, "second_bias": second_bias, "query_head_weight": query_head_weight, "key_weight": key_weight, "position_weight": position_weight, "value_weight": value_weight, "value_select": value_select, "output_expert_selector": output_expert_selector, "output_expert_weight": output_expert_weight, "content_bias": content_bias, "position_bias": position_bias, "up_projection_weight": up_projection_weight, "down_projection_weight": down_projection_weight, "cotangent": cotangent}


@jax.custom_vjp
def low(v):
    return lax.optimization_barrier(v.astype(jnp.bfloat16)).astype(jnp.float32)

@jax.custom_vjp
def low_back(v):
    return v

def low_keep(v):
    return (low(v), None)

def low_pass(kept, grad):
    return (grad,)

def back_keep(v):
    return (v, None)

def back_low(kept, grad):
    return (low(grad),)
low.defvjp(low_keep, low_pass)
low_back.defvjp(back_keep, back_low)
EPSILON = 1e-05
PRECISION_MAX = lax.Precision.HIGHEST

def norm_rows(values, gain, bias):
    center = values - lax.optimization_barrier(jnp.mean(values, axis=-1, keepdims=True))
    spread = lax.optimization_barrier(jnp.mean(center * center, axis=-1, keepdims=True))
    return center * lax.rsqrt(spread + EPSILON) * gain + bias

def position_table(places, width):
    half = width // 2
    place = jnp.arange(places).astype(jnp.float32)
    rates = jnp.exp(jnp.arange(half).astype(jnp.float32) * (-2.0 * math.log(10000.0) / width))
    angles = place[:, None] * rates[None, :]
    return jnp.concatenate([jnp.sin(angles), jnp.cos(angles)], axis=1)

def expert_mask(routes, experts):
    hits = routes[..., :, None] == jnp.arange(experts, dtype=jnp.int32)
    return lax.optimization_barrier(jnp.sum(hits.astype(jnp.float32), axis=-2))

def attend_block(pieces, key_vecs, value_vecs, rel_keys, seg_keys):
    query_c, query_p, seg_query, begin = pieces
    width = key_vecs.shape[0]
    content = jnp.dot(query_c, key_vecs.T, precision=PRECISION_MAX)
    shifted = jnp.dot(query_p, rel_keys.T, precision=PRECISION_MAX)
    places = begin + jnp.arange(query_c.shape[0], dtype=jnp.int32)
    offsets = places[:, None] - jnp.arange(width, dtype=jnp.int32)[None, :]
    position = jnp.take_along_axis(shifted, jnp.clip(offsets, 0, width - 1), axis=1)
    scores = low_back(content + position)
    allowed = (offsets >= 0) & (seg_query[:, None] == seg_keys[None, :])
    scores = jnp.where(allowed, scores, -1e+30)
    probs = jax.nn.softmax(scores, axis=-1)
    return jnp.dot(low(probs), value_vecs, precision=PRECISION_MAX)

def attend_sequence(pieces, table_low, rel_weight):
    query_c, query_p, key_vecs, value_vecs, seg_row = pieces
    rel_keys = low_back(low(jnp.dot(table_low, rel_weight, precision=PRECISION_MAX)))
    blocks = LEN // BLOCK
    begins = MEM + BLOCK * jnp.arange(blocks, dtype=jnp.int32)
    seg_query = seg_row[MEM:].reshape(blocks, BLOCK)
    step_fn = jax.checkpoint(partial(attend_block, key_vecs=key_vecs, value_vecs=value_vecs, rel_keys=rel_keys, seg_keys=seg_row))
    outputs = lax.map(step_fn, (query_c.reshape(blocks, BLOCK, -1), query_p.reshape(blocks, BLOCK, -1), seg_query, begins))
    return outputs.reshape(LEN, -1)

def layer(tokens, first_gain, first_bias, second_gain, second_bias, query_head_weight, key_weight, position_weight, value_weight, value_select, output_expert_selector, output_expert_weight, content_bias, position_bias, up_projection_weight, down_projection_weight, memory, segments, value_routes, output_routes):
    seq_total = tokens.shape[0] // LEN
    key_rows = jnp.concatenate([memory, tokens.reshape(seq_total, LEN, D)], axis=1)
    normed = low(norm_rows(key_rows, first_gain, first_bias))
    normalized_token = normed[:, MEM:]
    table_low = low(position_table(KEYS, D))
    scale = DH ** (-0.5)
    attention_mix = jnp.zeros((seq_total, LEN, D), jnp.float32)
    for index_of_head in range(H):
        query_rows = low_back(jnp.einsum('hpi,im->hpm', normalized_token, query_head_weight[index_of_head], precision=PRECISION_MAX))
        query_c = low_back(low((query_rows + content_bias[index_of_head]) * scale))
        query_p = low_back(low((query_rows + position_bias[index_of_head]) * scale))
        key_vecs = low_back(low(jnp.einsum('skd,dc->skc', normed, key_weight[index_of_head], precision=PRECISION_MAX)))
        every_value = low_back(jnp.einsum('skd,dc->skc', normed, value_weight[index_of_head], precision=PRECISION_MAX))
        value_logit = low_back(jnp.einsum('skd,de->ske', normed, value_select[index_of_head], precision=PRECISION_MAX))
        value_gate = jax.nn.sigmoid(value_logit) * expert_mask(value_routes[:, :, index_of_head], E)
        value_vecs = low(lax.optimization_barrier(jnp.sum(value_gate[..., None] * every_value.reshape(seq_total, KEYS, E, DH), axis=2)))
        output_logit = low_back(jnp.einsum('jbw,wy->jby', normalized_token, output_expert_selector[index_of_head], precision=PRECISION_MAX))
        out_gate = jax.nn.sigmoid(output_logit) * expert_mask(output_routes[:, index_of_head].reshape(seq_total, LEN, TOP), E)
        step_fn = jax.checkpoint(partial(attend_sequence, table_low=table_low, rel_weight=position_weight[index_of_head]))
        heads_out = low_back(lax.map(step_fn, (query_c, query_p, key_vecs, value_vecs, segments)))
        mixed_heads = low_back(low((out_gate[..., None] * heads_out[..., None, :]).reshape(seq_total, LEN, E * DH)))
        attention_mix = attention_mix + jnp.einsum('zek,kw->zew', mixed_heads, output_expert_weight[index_of_head], precision=PRECISION_MAX)
    attention_mix = low_back(attention_mix)
    middle_state = tokens.reshape(seq_total, LEN, D) + attention_mix
    up_input = low(norm_rows(middle_state, second_gain, second_bias))
    preactivation = low_back(jnp.einsum('gtz,za->gta', up_input, up_projection_weight, precision=PRECISION_MAX))
    hidden_state = low_back(low(jax.nn.gelu(preactivation, approximate=False)))
    layer_output = middle_state + jnp.einsum('oqy,ym->oqm', hidden_state, down_projection_weight, precision=PRECISION_MAX)
    return layer_output.reshape(seq_total * LEN, D)

def reference(tokens, memory, segments, value_routes, output_routes, first_gain, first_bias, second_gain, second_bias, query_head_weight, key_weight, position_weight, value_weight, value_select, output_expert_selector, output_expert_weight, content_bias, position_bias, up_projection_weight, down_projection_weight, cotangent):
    layer_fn = partial(layer, memory=memory.astype(jnp.float32), segments=segments, value_routes=value_routes, output_routes=output_routes)
    primals = [tokens, first_gain, first_bias, second_gain, second_bias, query_head_weight, key_weight, position_weight, value_weight, value_select, output_expert_selector, output_expert_weight, content_bias, position_bias, up_projection_weight, down_projection_weight]
    primals = [item.astype(jnp.float32) for item in primals]
    layer_output, pullback = jax.vjp(layer_fn, *primals)
    grads = pullback(cotangent.astype(jnp.float32))
    return (layer_output.astype(jnp.bfloat16), grads[0], grads[1], grads[2], grads[3], grads[4], grads[5], grads[6], grads[7], grads[8], grads[9], grads[10], grads[11], grads[12], grads[13], grads[14], grads[15])
```

```python
import functools
import math

import jax
import jax.numpy as jnp
from jax import lax
from jax.experimental import pallas as pl
from jax.experimental.pallas import tpu as pltpu
from jax.sharding import PartitionSpec as P

EPSILON = 1e-05
ROOT_HALF = 0.7071067811865476
INVERSE_ROOT_TAU = 0.3989422804014327
ROWS = 256
GROUP = 8
MIB = 1024 * 1024
BF16 = jnp.bfloat16
F32 = jnp.float32


def mm(left, right):
    return jnp.dot(left, right, preferred_element_type=F32)


def mm_nt(left, right):
    return lax.dot_general(left, right, (((1,), (1,)), ((), ())), preferred_element_type=F32)


def mm_tn(left, right):
    return lax.dot_general(left, right, (((0,), (0,)), ((), ())), preferred_element_type=F32)


def norm_parts(values):
    center = values - jnp.mean(values, axis=-1, keepdims=True)
    inv_std = lax.rsqrt(jnp.mean(center * center, axis=-1, keepdims=True) + EPSILON)
    return center * inv_std, inv_std


def norm_back(upstream, normal, inv_std, gain):
    scaled = upstream * gain
    return inv_std * (
        scaled
        - jnp.mean(scaled, axis=-1, keepdims=True)
        - normal * jnp.mean(scaled * normal, axis=-1, keepdims=True)
    )


def params(vmem_mib):
    return pltpu.CompilerParams(vmem_limit_bytes=vmem_mib * MIB)


def cost(flops, moved, transcendentals=0):
    return pl.CostEstimate(
        flops=int(flops), bytes_accessed=int(moved), transcendentals=int(transcendentals)
    )


def struct(shape, dtype):
    return jax.ShapeDtypeStruct(shape, dtype)


def whole(*shape):
    return pl.BlockSpec(shape, lambda *_: (0,) * len(shape))


def picked(routes, experts):
    lane = lax.broadcasted_iota(jnp.int32, (routes.shape[0], experts), 1)
    return (lane == routes[:, 0:1]) | (lane == routes[:, 1:2])


def project_kernel(
    experts,
    head_dim,
    mem_steps,
    scale,
    mem_ref,
    tok_ref,
    gain_ref,
    bias_ref,
    w_ref,
    vroute_ref,
    oroute_ref,
    cb_ref,
    pb_ref,
    normed_ref,
    key_ref,
    val_ref,
    every_ref,
    vgate_ref,
    qc_ref,
    qp_ref,
    ogate_ref,
):
    step = pl.program_id(0)
    first = head_dim
    select = first + experts * head_dim
    query = select + experts
    pick = query + head_dim
    total = pick + experts

    def rows_part(rows_ref, columns):
        normal, _ = norm_parts(rows_ref[...].astype(F32))
        normed = (normal * gain_ref[...] + bias_ref[...]).astype(BF16)
        normed_ref[...] = normed
        out = mm(normed, w_ref[:, :columns])
        key_ref[...] = out[:, :head_dim].astype(BF16)
        gate = jnp.where(
            picked(vroute_ref[...], experts), jax.nn.sigmoid(out[:, select : select + experts]), 0.0
        )
        vgate_ref[...] = gate
        every_ref[...] = out[:, first:select].astype(BF16)
        value = gate[:, 0:1] * out[:, first : first + head_dim]
        for e in range(1, experts):
            begin = first + e * head_dim
            value = value + gate[:, e : e + 1] * out[:, begin : begin + head_dim]
        val_ref[...] = value.astype(BF16)
        return out

    @pl.when(step < mem_steps)
    def _():
        rows_part(mem_ref, query)

    @pl.when(step >= mem_steps)
    def _():
        out = rows_part(tok_ref, total)
        q = out[:, query : query + head_dim]
        qc_ref[...] = ((q + cb_ref[...]) * scale).astype(BF16)
        qp_ref[...] = ((q + pb_ref[...]) * scale).astype(BF16)
        ogate_ref[...] = jnp.where(
            picked(oroute_ref[...], experts), jax.nn.sigmoid(out[:, pick:total]), 0.0
        )


def project(memory, tokens, gain, bias, w_all, vroutes, oroutes, cb, pb, experts, head_dim):
    mem, width = memory.shape
    toks = tokens.shape[0]
    mem_steps, tok_steps = mem // ROWS, toks // ROWS
    keys = mem + toks
    cols = w_all.shape[1]
    mem_row = lambda i: (jnp.minimum(i, mem_steps - 1), 0)
    tok_row = lambda i: (jnp.maximum(i - mem_steps, 0), 0)
    row = lambda i: (i, 0)
    return pl.pallas_call(
        functools.partial(project_kernel, experts, head_dim, mem_steps, head_dim ** (-0.5)),
        grid=(mem_steps + tok_steps,),
        in_specs=[
            pl.BlockSpec((ROWS, width), mem_row),
            pl.BlockSpec((ROWS, width), tok_row),
            whole(1, width),
            whole(1, width),
            whole(width, cols),
            pl.BlockSpec((ROWS, vroutes.shape[1]), row),
            pl.BlockSpec((ROWS, oroutes.shape[1]), tok_row),
            whole(1, head_dim),
            whole(1, head_dim),
        ],
        out_specs=[
            pl.BlockSpec((ROWS, width), row),
            pl.BlockSpec((ROWS, head_dim), row),
            pl.BlockSpec((ROWS, head_dim), row),
            pl.BlockSpec((ROWS, experts * head_dim), row),
            pl.BlockSpec((ROWS, experts), row),
            pl.BlockSpec((ROWS, head_dim), tok_row),
            pl.BlockSpec((ROWS, head_dim), tok_row),
            pl.BlockSpec((ROWS, experts), tok_row),
        ],
        out_shape=[
            struct((keys, width), BF16),
            struct((keys, head_dim), BF16),
            struct((keys, head_dim), BF16),
            struct((keys, experts * head_dim), BF16),
            struct((keys, experts), F32),
            struct((toks, head_dim), BF16),
            struct((toks, head_dim), BF16),
            struct((toks, experts), F32),
        ],
        compiler_params=params(40),
        cost_estimate=cost(2 * keys * width * cols, 4 * keys * width * 2),
        name="project",
    )(memory, tokens, gain, bias, w_all, vroutes, oroutes, cb, pb)


def attend_kernel(
    span,
    z_ref,
    qc_ref,
    qp_ref,
    key_ref,
    val_ref,
    rel_ref,
    segk_ref,
    segq_ref,
    ogate_ref,
    heads_ref,
    probs_ref,
    pack_ref,
):
    begin = pl.program_id(0) * ROWS
    wide = span + ROWS
    head_dim = qc_ref.shape[1]
    keys = key_ref[pl.ds(begin, wide), :]
    vals = val_ref[pl.ds(begin, wide), :]
    content = mm_nt(qc_ref[...], keys)
    reverse = mm_nt(qp_ref[...], rel_ref[...])
    reverse = jnp.concatenate([reverse, jnp.zeros((ROWS, ROWS), F32)], axis=1)
    scores = content + pltpu.roll(reverse, 1, 1, stride=1, stride_axis=0)
    column = lax.broadcasted_iota(jnp.int32, (ROWS, wide), 1)
    place = lax.broadcasted_iota(jnp.int32, (ROWS, wide), 0)
    ahead = column - place
    allowed = (segk_ref[0] == segq_ref[...]) & (ahead <= span) & (ahead >= 1)
    scores = jnp.where(allowed, scores, -1e30)
    expo = jnp.exp(scores - jnp.max(scores, axis=1, keepdims=True))
    expo = jnp.where(allowed, expo, 0.0)
    probs = (expo * (1.0 / jnp.sum(expo, axis=1, keepdims=True))).astype(BF16)
    probs_ref[...] = probs
    heads = mm(probs, vals)
    heads_ref[...] = heads
    pack_ref[0, :, :head_dim] = heads.astype(BF16)
    pack_ref[0, :, head_dim:] = ogate_ref[...].astype(BF16)


def attend(rank, qc, qp, key_vecs, value_vecs, rel_reverse, seg_keys, seg_query, ogate):
    toks, head_dim = qc.shape
    keys = key_vecs.shape[0]
    span = rel_reverse.shape[0]
    steps = toks // ROWS
    wide = span + ROWS
    experts = ogate.shape[1]
    row = lambda i, z: (i, 0)
    return pl.pallas_call(
        functools.partial(attend_kernel, span),
        grid_spec=pltpu.PrefetchScalarGridSpec(
            num_scalar_prefetch=1,
            grid=(steps,),
            in_specs=[
                pl.BlockSpec((ROWS, head_dim), row),
                pl.BlockSpec((ROWS, head_dim), row),
                whole(keys, head_dim),
                whole(keys, head_dim),
                whole(span, head_dim),
                pl.BlockSpec((1, 1, wide), lambda i, z: (i, 0, 0)),
                pl.BlockSpec((ROWS, 1), row),
                pl.BlockSpec((ROWS, experts), row),
            ],
            out_specs=[
                pl.BlockSpec((ROWS, head_dim), row),
                pl.BlockSpec((ROWS, wide), row),
                pl.BlockSpec((1, ROWS, head_dim + experts), lambda i, z: (i ^ z[0], 0, 0)),
            ],
        ),
        out_shape=[
            struct((toks, head_dim), F32),
            struct((toks, wide), BF16),
            struct((steps, ROWS, head_dim + experts), BF16),
        ],
        compiler_params=params(40),
        cost_estimate=cost(6 * toks * wide * head_dim, 6 * MIB, toks * wide),
        name="attend",
    )(rank, qc, qp, key_vecs, value_vecs, rel_reverse, seg_keys, seg_query, ogate)


def attend_back_kernel(
    span,
    experts,
    scale,
    z_ref,
    qc_ref,
    qp_ref,
    key_ref,
    val_ref,
    rel_ref,
    probs_ref,
    heads_ref,
    back_ref,
    ogate_ref,
    every_ref,
    vgate_ref,
    key_grad_ref,
    value_grad_ref,
    value_logit_ref,
    rel_grad_ref,
    bias_ref,
    pack_ref,
    keys_scr,
    values_scr,
    rel_scr,
    query_scr,
):
    step = pl.program_id(0)
    steps = pl.num_programs(0)
    begin = step * ROWS
    wide = span + ROWS
    head_dim = qc_ref.shape[1]
    mem = keys_scr.shape[0] - steps * ROWS

    @pl.when(step == 0)
    def _():
        keys_scr[...] = jnp.zeros_like(keys_scr)
        values_scr[...] = jnp.zeros_like(values_scr)
        rel_scr[...] = jnp.zeros_like(rel_scr)
        bias_ref[...] = jnp.zeros_like(bias_ref)

    window = pl.ds(begin, wide)
    keys = key_ref[window, :]
    vals = val_ref[window, :]
    out_grad = back_ref[0, :, :head_dim]
    probs = probs_ref[...]
    delta = jnp.sum(out_grad.astype(F32) * heads_ref[...], axis=1, keepdims=True)
    probs_grad = mm_nt(out_grad, vals)
    score_grad = (probs.astype(F32) * (probs_grad - delta)).astype(BF16)
    content_grad = mm(score_grad, keys).astype(BF16).astype(F32) * scale
    keys_scr[window, :] += mm_tn(score_grad, qc_ref[...])
    values_scr[window, :] += mm_tn(probs, out_grad)
    flip = (
        lax.broadcasted_iota(jnp.int32, (ROWS, ROWS), 0)
        + lax.broadcasted_iota(jnp.int32, (ROWS, ROWS), 1)
        == ROWS - 1
    ).astype(BF16)
    turned = mm(flip, score_grad)
    turned = pltpu.roll(turned, span, 1, stride=1, stride_axis=0)[:, :span].astype(BF16)
    place_grad = mm(turned, rel_ref[...]).astype(BF16)
    position_grad = mm(flip, place_grad) * scale
    rel_scr[...] += mm_tn(turned, mm(flip, qp_ref[...]).astype(BF16))
    bias_ref[0:1, :] += jnp.sum(content_grad, axis=0, keepdims=True)
    bias_ref[1:2, :] += jnp.sum(position_grad, axis=0, keepdims=True)
    gate = ogate_ref[...]
    slot = step ^ z_ref[0]
    query_scr[slot, :, :head_dim] = content_grad + position_grad
    query_scr[slot, :, head_dim:] = (
        back_ref[0, :, head_dim:].astype(F32) * gate * (1.0 - gate)
    )

    @pl.when(step == steps - 1)
    def _():
        rel_grad_ref[...] = rel_scr[...].astype(BF16)

        @pl.loop(0, (mem + steps * ROWS) // ROWS)
        def _(block):
            rows = pl.ds(block * ROWS, ROWS)
            key_grad = keys_scr[rows, :].astype(BF16)
            value_grad = values_scr[rows, :]
            gates = vgate_ref[rows, :]
            key_grad_ref[rows, :] = key_grad
            value_grad_ref[rows, :] = value_grad
            sums = [
                jnp.sum(
                    value_grad
                    * every_ref[rows, e * head_dim : (e + 1) * head_dim].astype(F32),
                    axis=1,
                    keepdims=True,
                )
                for e in range(experts)
            ]
            lane = lax.broadcasted_iota(jnp.int32, (ROWS, experts), 1)
            logit = jnp.zeros((ROWS, experts), F32)
            for e in range(experts):
                logit = jnp.where(lane == e, sums[e], logit)
            logit = (logit * gates * (1.0 - gates)).astype(BF16)
            value_logit_ref[rows, :] = logit

            @pl.when(block * ROWS >= mem)
            def _():
                slot = (block - mem // ROWS) ^ z_ref[0]
                pack_ref[slot, 0, :, :head_dim] = key_grad
                pack_ref[slot, 0, :, head_dim:] = logit
                pack_ref[slot, 1, :, :head_dim] = value_grad.astype(BF16)
                pack_ref[slot, 1, :, head_dim:] = gates.astype(BF16)
                pack_ref[slot, 2] = query_scr[slot].astype(BF16)


def attend_back(
    rank, qc, qp, key_vecs, value_vecs, rel_reverse, probs, heads, back, ogate, every, vgate
):
    toks, head_dim = qc.shape
    keys = key_vecs.shape[0]
    span = rel_reverse.shape[0]
    steps = toks // ROWS
    wide = span + ROWS
    experts = ogate.shape[1]
    row = lambda i, z: (i, 0)
    return pl.pallas_call(
        functools.partial(attend_back_kernel, span, experts, head_dim ** (-0.5)),
        grid_spec=pltpu.PrefetchScalarGridSpec(
            num_scalar_prefetch=1,
            grid=(steps,),
            in_specs=[
                pl.BlockSpec((ROWS, head_dim), row),
                pl.BlockSpec((ROWS, head_dim), row),
                whole(keys, head_dim),
                whole(keys, head_dim),
                whole(span, head_dim),
                pl.BlockSpec((ROWS, wide), row),
                pl.BlockSpec((ROWS, head_dim), row),
                pl.BlockSpec((1, ROWS, head_dim + experts), lambda i, z: (i ^ z[0], 0, 0)),
                pl.BlockSpec((ROWS, experts), row),
                whole(keys, experts * head_dim),
                whole(keys, experts),
            ],
            out_specs=[
                whole(keys, head_dim),
                whole(keys, head_dim),
                whole(keys, experts),
                whole(span, head_dim),
                whole(2, head_dim),
                whole(steps, 3, ROWS, head_dim + experts),
            ],
            scratch_shapes=[
                pltpu.VMEM((keys, head_dim), F32),
                pltpu.VMEM((keys, head_dim), F32),
                pltpu.VMEM((span, head_dim), F32),
                pltpu.VMEM((steps, ROWS, head_dim + experts), F32),
            ],
        ),
        out_shape=[
            struct((keys, head_dim), BF16),
            struct((keys, head_dim), F32),
            struct((keys, experts), BF16),
            struct((span, head_dim), BF16),
            struct((2, head_dim), F32),
            struct((steps, 3, ROWS, head_dim + experts), BF16),
        ],
        compiler_params=params(48),
        cost_estimate=cost(14 * toks * wide * head_dim, 12 * MIB),
        name="attend_back",
    )(rank, qc, qp, key_vecs, value_vecs, rel_reverse, probs, heads, back, ogate, every, vgate)


def mix_kernel(
    experts,
    where_ref,
    pack_ref,
    own_ref,
    even_ref,
    odd_ref,
    tok_ref,
    gain_ref,
    bias_ref,
    mixed_ref,
    full_ref,
    middle_ref,
    up_ref,
    attn_scr,
):
    step = pl.program_id(0)
    steps = pl.num_programs(0)
    heads = pack_ref.shape[0]
    head_dim = pack_ref.shape[2] - experts

    @pl.when(step == 0)
    def _():
        for m in range(heads):
            out = pack_ref[m, :, :head_dim].astype(F32)
            for e in range(experts):
                gate = pack_ref[m, :, head_dim + e : head_dim + e + 1].astype(F32)
                mixed_ref[m, :, e * head_dim : (e + 1) * head_dim] = (gate * out).astype(BF16)

    turned = where_ref[1] == 1
    full_ref[0] = own_ref[...]
    total = mm(mixed_ref[0], own_ref[...])
    for m in range(1, heads):
        even, odd = even_ref[0, m - 1], odd_ref[0, m - 1]
        weight = jnp.concatenate(
            [jnp.where(turned, odd, even), jnp.where(turned, even, odd)], axis=1
        )
        full_ref[m] = weight
        total = total + mm(mixed_ref[m], weight)
    block = where_ref[0] ^ step
    size = total.shape[1]
    attn_scr[:, pl.ds(pl.multiple_of(block * size, size), size)] = total

    @pl.when(step == steps - 1)
    def _():
        middle = tok_ref[...].astype(F32) + attn_scr[...]
        middle_ref[...] = middle
        normal, _ = norm_parts(middle)
        up_ref[...] = (normal * gain_ref[...] + bias_ref[...]).astype(BF16)


def mix(where, pack, own_weight, even, odd, tokens, gain, bias, experts):
    heads, rows, lanes = pack.shape
    depth, width = own_weight.shape
    steps = even.shape[0]
    size = width // steps
    return pl.pallas_call(
        functools.partial(mix_kernel, experts),
        grid_spec=pltpu.PrefetchScalarGridSpec(
            num_scalar_prefetch=1,
            grid=(steps,),
            in_specs=[
                whole(heads, rows, lanes),
                pl.BlockSpec((depth, size), lambda s, w: (0, w[0] ^ s)),
                pl.BlockSpec((1,) + even.shape[1:], lambda s, w: (s, 0, 0, 0)),
                pl.BlockSpec((1,) + odd.shape[1:], lambda s, w: (s, 0, 0, 0)),
                pl.BlockSpec((rows, width), lambda s, w: (w[2], 0)),
                whole(1, width),
                whole(1, width),
            ],
            out_specs=[
                whole(heads, rows, depth),
                pl.BlockSpec((heads, depth, size), lambda s, w: (0, 0, w[0] ^ s)),
                whole(rows, width),
                whole(rows, width),
            ],
            scratch_shapes=[pltpu.VMEM((rows, width), F32)],
        ),
        out_shape=[
            struct((heads, rows, depth), BF16),
            struct((heads, depth, width), BF16),
            struct((rows, width), F32),
            struct((rows, width), BF16),
        ],
        compiler_params=params(40),
        cost_estimate=cost(2 * rows * heads * depth * width, 14 * MIB),
        name="mix",
    )(where, pack, own_weight, even, odd, tokens, gain, bias)


def mix_back_kernel(
    experts,
    ug0_ref,
    ug1_ref,
    ug2_ref,
    ug3_ref,
    cot_ref,
    middle_ref,
    gain_ref,
    pack_ref,
    full_ref,
    middle_grad_ref,
    attn_grad_ref,
    sums_ref,
    back_ref,
):
    step = pl.program_id(0)
    head_dim = pack_ref.shape[2] - experts

    @pl.when(step == 0)
    def _():
        upstream = (
            ug0_ref[...].astype(F32)
            + ug1_ref[...].astype(F32)
            + ug2_ref[...].astype(F32)
            + ug3_ref[...].astype(F32)
        )
        normal, inv_std = norm_parts(middle_ref[...])
        sums_ref[0:1, :] = jnp.sum(upstream * normal, axis=0, keepdims=True)
        sums_ref[1:2, :] = jnp.sum(upstream, axis=0, keepdims=True)
        grad = cot_ref[...].astype(F32) + norm_back(upstream, normal, inv_std, gain_ref[...])
        middle_grad_ref[...] = grad
        attn_grad_ref[...] = grad.astype(BF16)

    mixed_grad = mm_nt(attn_grad_ref[...], full_ref[0]).astype(BF16).astype(F32)
    out = pack_ref[0, :, :head_dim].astype(F32)
    total = jnp.zeros_like(out)
    lane = lax.broadcasted_iota(jnp.int32, (out.shape[0], experts), 1)
    gates = jnp.zeros((out.shape[0], experts), F32)
    for e in range(experts):
        part = mixed_grad[:, e * head_dim : (e + 1) * head_dim]
        total = total + pack_ref[0, :, head_dim + e : head_dim + e + 1].astype(F32) * part
        gates = jnp.where(lane == e, jnp.sum(part * out, axis=1, keepdims=True), gates)
    back_ref[0, :, :head_dim] = total.astype(BF16)
    back_ref[0, :, head_dim:] = gates.astype(BF16)


def mix_back(grads, cot, middle, gain, pack, full, experts):
    heads, rows, lanes = pack.shape
    depth, width = full.shape[1:]
    return pl.pallas_call(
        functools.partial(mix_back_kernel, experts),
        grid=(heads,),
        in_specs=[whole(rows, width)] * 6
        + [
            whole(1, width),
            pl.BlockSpec((1, rows, lanes), lambda m: (m, 0, 0)),
            pl.BlockSpec((1, depth, width), lambda m: (m, 0, 0)),
        ],
        out_specs=[
            whole(rows, width),
            whole(rows, width),
            whole(2, width),
            pl.BlockSpec((1, rows, lanes), lambda m: (m, 0, 0)),
        ],
        out_shape=[
            struct((rows, width), F32),
            struct((rows, width), BF16),
            struct((2, width), F32),
            struct((heads, rows, lanes), BF16),
        ],
        compiler_params=params(40),
        cost_estimate=cost(2 * rows * heads * depth * width, 12 * MIB),
        name="mix_back",
    )(*grads, cot, middle, gain, pack, full)


def feed_kernel(
    up_ref, cot_ref, wu_ref, wd_ref, hidden_ref, pre_grad_ref, out_ref, up_grad_ref, out_scr, up_scr
):
    step = pl.program_id(0)
    steps = pl.num_programs(0)

    @pl.when(step == 0)
    def _():
        out_scr[...] = jnp.zeros_like(out_scr)
        up_scr[...] = jnp.zeros_like(up_scr)

    pre = mm(up_ref[...], wu_ref[...])
    hidden_grad = mm_nt(cot_ref[...], wd_ref[...]).astype(BF16).astype(F32)
    phi = 0.5 * (1.0 + lax.erf(pre * ROOT_HALF))
    hidden = (pre * phi).astype(BF16)
    slope = phi + pre * jnp.exp(-0.5 * pre * pre) * INVERSE_ROOT_TAU
    pre_grad = (hidden_grad * slope).astype(BF16)
    hidden_ref[...] = hidden
    pre_grad_ref[...] = pre_grad
    out_scr[...] += mm(hidden, wd_ref[...])
    up_scr[...] += mm_nt(pre_grad, wu_ref[...])

    @pl.when(step == steps - 1)
    def _():
        out_ref[...] = out_scr[...].astype(out_ref.dtype)
        up_grad_ref[...] = up_scr[...].astype(up_grad_ref.dtype)


def feed(up_in, cot, w_up, w_down):
    rows, width = up_in.shape
    hidden = w_up.shape[1]
    size = 256
    return pl.pallas_call(
        feed_kernel,
        grid=(hidden // size,),
        in_specs=[
            whole(rows, width),
            whole(rows, width),
            pl.BlockSpec((width, size), lambda i: (0, i)),
            pl.BlockSpec((size, width), lambda i: (i, 0)),
        ],
        out_specs=[
            pl.BlockSpec((rows, size), lambda i: (0, i)),
            pl.BlockSpec((rows, size), lambda i: (0, i)),
            whole(rows, width),
            whole(rows, width),
        ],
        out_shape=[
            struct((rows, hidden), BF16),
            struct((rows, hidden), BF16),
            struct((rows, width), BF16),
            struct((rows, width), BF16),
        ],
        scratch_shapes=[pltpu.VMEM((rows, width), F32), pltpu.VMEM((rows, width), F32)],
        compiler_params=params(32),
        cost_estimate=cost(8 * rows * width * hidden, 8 * MIB, 2 * rows * hidden),
        name="feed",
    )(up_in, cot, w_up, w_down)


def feed_weights_kernel(count, *refs):
    lefts, rights = refs[: 2 * count], refs[2 * count : 4 * count]
    out_ref, scr = refs[4 * count], refs[4 * count + 1]
    step = pl.program_id(0)
    half = pl.num_programs(0) // 2

    for which in range(2):

        @pl.when(step == which * half)
        def _():
            for m in range(count):
                rows = lefts[which * count + m].shape[0]
                scr[:, m * rows : (m + 1) * rows] = lefts[which * count + m][...].T

        @pl.when(step // half == which)
        def _():
            right = jnp.concatenate(
                [rights[which * count + m][...] for m in range(count)], axis=0
            )
            out_ref[...] = mm(scr[...], right).astype(BF16)


def feed_weights(ups, cots, pre_grads, hiddens):
    count = len(ups)
    rows, width = ups[0].shape
    hidden = hiddens[0].shape[1]
    size = 512
    half = hidden // size
    left = [whole(rows, width)] * (2 * count)
    right = [
        pl.BlockSpec((rows, size), lambda i: (0, jnp.minimum(i, half - 1)))
    ] * count + [pl.BlockSpec((rows, size), lambda i: (0, jnp.maximum(i - half, 0)))] * count
    return pl.pallas_call(
        functools.partial(feed_weights_kernel, count),
        grid=(2 * half,),
        in_specs=left + right,
        out_specs=pl.BlockSpec((width, size), lambda i: (0, i)),
        out_shape=struct((width, 2 * hidden), BF16),
        scratch_shapes=[pltpu.VMEM((width, count * rows), BF16)],
        compiler_params=params(40),
        cost_estimate=cost(4 * count * rows * width * hidden, 12 * MIB),
        name="feed_weights",
    )(*ups, *cots, *pre_grads, *hiddens)


def weights_kernel(
    experts,
    mem_steps,
    normed_ref,
    key_ref,
    value_ref,
    gate_ref,
    logit_ref,
    query_ref,
    out_ref,
    colsum_ref,
    grads_scr,
):
    step = pl.program_id(0)
    head_dim = key_ref.shape[1]
    select = head_dim * (1 + experts)
    query = select + experts

    @pl.when(step == 0)
    def _():
        out_ref[...] = jnp.zeros_like(out_ref)
        colsum_ref[...] = jnp.zeros_like(colsum_ref)

    value_grad = value_ref[...]
    grads_scr[:, :head_dim] = key_ref[...]
    for e in range(experts):
        grads_scr[:, head_dim * (1 + e) : head_dim * (2 + e)] = (
            gate_ref[:, e : e + 1] * value_grad
        ).astype(BF16)
    grads_scr[:, select:query] = logit_ref[...]

    def add(columns):
        grads = grads_scr[:, :columns]
        out_ref[:, :columns] += mm_tn(normed_ref[...], grads)
        colsum_ref[:, :columns] += jnp.sum(grads.astype(F32), axis=0, keepdims=True)

    @pl.when(step < mem_steps)
    def _():
        add(query)

    @pl.when(step >= mem_steps)
    def _():
        grads_scr[:, query:] = query_ref[0, 0]
        add(grads_scr.shape[1])


def weight_grads(rank, normed, key_grad, value_grad, gates, logit, pack, experts, mem_steps):
    keys, width = normed.shape
    head_dim = key_grad.shape[1]
    lanes = pack.shape[3]
    cols = head_dim * (1 + experts) + experts + lanes
    row = lambda i, z: (i, 0)

    def body(z_ref, *refs):
        weights_kernel(experts, mem_steps, *refs)

    return pl.pallas_call(
        body,
        grid_spec=pltpu.PrefetchScalarGridSpec(
            num_scalar_prefetch=1,
            grid=(keys // ROWS,),
            in_specs=[
                pl.BlockSpec((ROWS, width), row),
                pl.BlockSpec((ROWS, head_dim), row),
                pl.BlockSpec((ROWS, head_dim), row),
                pl.BlockSpec((ROWS, experts), row),
                pl.BlockSpec((ROWS, experts), row),
                pl.BlockSpec(
                    (1, 1, ROWS, lanes),
                    lambda i, z: (jnp.maximum(i - mem_steps, 0) ^ z[0], 2, 0, 0),
                ),
            ],
            out_specs=[whole(width, cols), whole(1, cols)],
            scratch_shapes=[pltpu.VMEM((ROWS, cols), BF16)],
        ),
        out_shape=[struct((width, cols), F32), struct((1, cols), F32)],
        compiler_params=params(40),
        cost_estimate=cost(2 * keys * width * cols, 10 * MIB),
        name="weight_grads",
    )(rank, normed, key_grad, value_grad, gates, logit, pack)


def token_kernel(
    experts, z_ref, pack0_ref, pack1_ref, pack2_ref, pack3_ref, w_ref, tok_ref, mid_ref, gain_ref,
    out_ref, grads_scr, total_scr,
):
    step = pl.program_id(0)
    steps = pl.num_programs(0)
    lanes = pack0_ref.shape[2]
    head_dim = lanes - experts
    select = head_dim * (1 + experts)
    query = select + experts

    @pl.when(step == 0)
    def _():
        total_scr[...] = jnp.zeros_like(total_scr)

    for m, pack_ref in enumerate((pack0_ref, pack1_ref, pack2_ref, pack3_ref)):

        @pl.when(step == m)
        def _():
            grads_scr[:, :head_dim] = pack_ref[0, :, :head_dim]
            value_grad = pack_ref[1, :, :head_dim].astype(F32)
            for e in range(experts):
                gate = pack_ref[1, :, head_dim + e : head_dim + e + 1].astype(F32)
                grads_scr[:, head_dim * (1 + e) : head_dim * (2 + e)] = (
                    gate * value_grad
                ).astype(BF16)
            grads_scr[:, select:query] = pack_ref[0, :, head_dim:]
            grads_scr[:, query:] = pack_ref[2]

    total_scr[...] += mm_nt(grads_scr[...], w_ref[0])

    @pl.when(step == steps - 1)
    def _():
        normal, inv_std = norm_parts(tok_ref[...].astype(F32))
        out_ref[...] = mid_ref[...] + norm_back(total_scr[...], normal, inv_std, gain_ref[...])


def token_grads(rank, packs, weights, tokens, middle_grad, gain, experts):
    rows, width = middle_grad.shape
    heads, _, cols = weights.shape
    shape = packs[0].shape
    return pl.pallas_call(
        functools.partial(token_kernel, experts),
        grid_spec=pltpu.PrefetchScalarGridSpec(
            num_scalar_prefetch=1,
            grid=(heads,),
            in_specs=[whole(*shape)] * heads
            + [
                pl.BlockSpec((1, width, cols), lambda m, z: (m ^ z[0], 0, 0)),
                pl.BlockSpec((rows, width), lambda m, z: (z[0], 0)),
                whole(rows, width),
                whole(1, width),
            ],
            out_specs=whole(rows, width),
            scratch_shapes=[pltpu.VMEM((rows, cols), BF16), pltpu.VMEM((rows, width), F32)],
        ),
        out_shape=struct((rows, width), F32),
        compiler_params=params(40),
        cost_estimate=cost(2 * rows * width * cols * heads, 10 * MIB),
        name="token_grads",
    )(rank, *packs, weights, tokens, middle_grad, gain)


def swap(array, axis, mask):
    size = lax.axis_size(axis)
    return lax.ppermute(array, axis, [(i, i ^ mask) for i in range(size)])


def halve(parts, dim, bit, mask):
    keep = lax.dynamic_index_in_dim(parts, bit, dim, keepdims=False)
    send = lax.dynamic_index_in_dim(parts, 1 - bit, dim, keepdims=False)
    return keep.astype(F32) + swap(send.astype(BF16), "dp", mask).astype(F32)


def scatter_rows(array):
    size = lax.axis_size("dp")
    at = lax.axis_index("dp")
    rows = array.shape[0] // size
    tail = array.shape[1:]
    bits = [(at >> b) & 1 for b in range(size.bit_length() - 1)]
    part = halve(array.reshape((size // 2, 2, rows) + tail), 1, bits[0], 1)
    half = rows // 2
    done = []
    for begin, order in ((0, (1, 2)), (half, (2, 1))):
        piece = part[:, begin : begin + half].reshape((size // 8, 2, 2, half) + tail)
        first, second = order
        piece = halve(piece, 3 - first, bits[first], 1 << first)
        piece = halve(piece, 1, bits[second], 1 << second)
        for b in range(3, len(bits)):
            piece = halve(piece.reshape((size >> (b + 1), 2, half) + tail), 1, bits[b], 1 << b)
        done.append(piece.reshape((half,) + tail))
    return jnp.concatenate(done, axis=0)


def sum_everywhere(array):
    for axis in ("dp", "tensor"):
        for b in range(lax.axis_size(axis).bit_length() - 1):
            array = array + swap(array, axis, 1 << b)
    return array


def spread_columns(weight, at):
    depth, width = weight.shape
    size = width // GROUP
    own = lax.dynamic_slice_in_dim(weight, at * size, size, 1)
    far = jnp.stack([swap(own, "tensor", m) for m in range(1, lax.axis_size("tensor"))])
    by_x = swap(far, "dp", 2)
    by_y = swap(far, "dp", 4)
    cut = depth // 32 * 16
    both = jnp.concatenate(
        [swap(by_x[:, :cut], "dp", 4), swap(by_y[:, cut:], "dp", 2)], axis=1
    )
    even = jnp.stack([far, by_x, by_y, both])
    odd = swap(even, "dp", 1)
    return even, odd


def on_device(
    tokens,
    memory,
    segments,
    value_routes,
    output_routes,
    first_gain,
    first_bias,
    second_gain,
    second_bias,
    query_head_weight,
    key_weight,
    position_weight,
    value_weight,
    value_select,
    output_expert_selector,
    output_expert_weight,
    content_bias,
    position_bias,
    up_projection_weight,
    down_projection_weight,
    cotangent,
):
    mem_len = memory.shape[1]
    toks, width = tokens.shape
    keys = mem_len + toks
    head_dim = query_head_weight.shape[2]
    experts = value_select.shape[2]
    parts = lax.axis_size("tensor")
    rank = lax.axis_index("tensor")
    at = lax.axis_index("dp")
    others = range(1, parts)
    rank_ref = rank.reshape(1).astype(jnp.int32)
    row = lambda v: v.reshape(1, -1)

    own_out = output_expert_weight[0]
    even, odd = spread_columns(own_out, at % GROUP)
    cots = [cotangent] + [swap(cotangent, "tensor", m) for m in others]
    w_all = jnp.concatenate(
        [
            key_weight[0],
            value_weight[0],
            value_select[0],
            query_head_weight[0],
            output_expert_selector[0],
        ],
        axis=1,
    )
    piece = width // lax.axis_size("dp")
    w_heads = lax.all_gather(
        lax.dynamic_slice_in_dim(w_all, at * piece, piece, 0), ("tensor", "dp"), axis=0, tiled=True
    ).reshape(parts, width, -1)

    span = mem_len
    fine = 32
    rates = jnp.exp(jnp.arange(width // 2).astype(F32) * (-2.0 * math.log(10000.0) / width))
    coarse_at = (span - 1 - fine * jnp.arange(span // fine)).astype(F32)[:, None] * rates[None, :]
    fine_at = jnp.arange(fine).astype(F32)[:, None] * rates[None, :]
    sin_a, cos_a = jnp.sin(coarse_at)[:, None, :], jnp.cos(coarse_at)[:, None, :]
    sin_b, cos_b = jnp.sin(fine_at)[None, :, :], jnp.cos(fine_at)[None, :, :]
    sin_table = jnp.concatenate(
        [sin_a * cos_b - cos_a * sin_b, cos_a * cos_b + sin_a * sin_b], axis=2
    )
    sin_table = sin_table.reshape(span, width).astype(BF16)
    rel_reverse = mm(sin_table, position_weight[0]).astype(BF16)

    normed, key_vecs, value_vecs, every, vgate, qc, qp, ogate = project(
        memory[0],
        tokens,
        row(first_gain),
        row(first_bias),
        w_all,
        value_routes[0, :, 0],
        output_routes[:, 0],
        content_bias,
        position_bias,
        experts,
        head_dim,
    )
    steps = toks // ROWS
    seg = segments[0]
    seg_keys = jnp.stack([seg[i * ROWS : i * ROWS + span + ROWS] for i in range(steps)])[:, None]
    heads, probs, pack = attend(
        rank_ref, qc, qp, key_vecs, value_vecs, rel_reverse, seg_keys, seg[mem_len:, None], ogate
    )

    pack = jnp.stack([pack[0]] + [swap(pack[m], "tensor", m) for m in others])
    group_at = at % GROUP
    where = jnp.stack([group_at // 2, group_at % 2, rank]).astype(jnp.int32)
    mixed, full, middle, up_in = mix(
        where, pack, own_out, even, odd, tokens, row(second_gain), row(second_bias), experts
    )

    ups = [up_in] + [swap(up_in, "tensor", m) for m in others]
    fed = [feed(u, c, up_projection_weight, down_projection_weight) for u, c in zip(ups, cots)]
    hiddens, pre_grads, outs, up_grads = zip(*fed)
    up_grads = [up_grads[0]] + [swap(up_grads[m], "tensor", m) for m in others]
    outs = [outs[0]] + [swap(outs[m], "tensor", m) for m in others]
    result = middle
    for out in outs:
        result = result + out.astype(F32)
    result = result.astype(BF16)
    feed_grads = lax.psum_scatter(
        feed_weights(ups, cots, pre_grads, hiddens), "dp", scatter_dimension=0, tiled=True
    )
    hidden = up_projection_weight.shape[1]
    up_total = feed_grads[:, :hidden].astype(F32)
    down_total = feed_grads[:, hidden:].T.astype(F32)

    middle_grad, attn_grad, sums_two, back = mix_back(
        up_grads, cotangent, middle, row(second_gain), pack, full, experts
    )
    back = jnp.stack([back[0]] + [swap(back[m], "tensor", m) for m in others])
    attn_grads = jnp.concatenate([attn_grad] + [swap(attn_grad, "tensor", m) for m in others])
    mine = lax.dynamic_update_slice_in_dim

    key_grad, value_grad, value_logit, rel_grad, bias_sums, packs = attend_back(
        rank_ref, qc, qp, key_vecs, value_vecs, rel_reverse, probs, heads, back, ogate, every, vgate
    )
    grads, colsum = weight_grads(
        rank_ref,
        normed,
        key_grad,
        value_grad,
        vgate,
        value_logit,
        packs,
        experts,
        mem_len // ROWS,
    )
    own_packs = [packs[0]] + [swap(packs[m], "tensor", m) for m in others]
    tokens_grad = token_grads(
        rank_ref, own_packs, w_heads, tokens, middle_grad, row(first_gain), experts
    )
    rel_weight_grad = mm_tn(sin_table, rel_grad)

    share = toks // parts
    out_mixed = []
    for m in range(parts):
        begin = (rank ^ m) * share
        gate = lax.dynamic_slice_in_dim(ogate, begin, share, 0)
        out = lax.dynamic_slice_in_dim(heads, begin, share, 0)
        out_mixed.append(
            (gate[:, :, None] * out[:, None, :]).reshape(share, experts * head_dim).astype(BF16)
        )
    out_weight_grad = mm_tn(attn_grads, jnp.concatenate(out_mixed))

    wide = w_all.astype(F32)
    bias_one = jnp.sum(wide * colsum, axis=1)
    gain_one = (
        jnp.sum(grads * wide, axis=1) - first_bias * bias_one
    ) / first_gain

    kept = scatter_rows(
        jnp.concatenate([grads, rel_weight_grad, out_weight_grad], axis=1)
    )
    slot = (jnp.arange(parts) == rank).astype(F32)[:, None]
    flat = jnp.concatenate(
        [
            gain_one,
            bias_one,
            sums_two.reshape(-1),
            (slot * bias_sums[0][None]).reshape(-1),
            (slot * bias_sums[1][None]).reshape(-1),
        ]
    )
    small = sum_everywhere(flat.reshape(-1, 128)).reshape(-1)
    last = 4 * width + parts * head_dim
    select = head_dim * (1 + experts)
    query = select + experts
    pick = query + head_dim
    cols = pick + experts
    return (
        result,
        tokens_grad,
        small[:width],
        small[width : 2 * width],
        small[2 * width : 3 * width],
        small[3 * width : 4 * width],
        kept[None, :, query:pick],
        kept[None, :, :head_dim],
        kept[None, :, cols : cols + head_dim],
        kept[None, :, head_dim:select],
        kept[None, :, select:query],
        kept[None, :, pick:cols],
        kept[:, cols + head_dim :].T[None],
        small[4 * width : last].reshape(parts, head_dim),
        small[last:].reshape(parts, head_dim),
        up_total,
        down_total,
    )


def solution(mesh):
    placed = (
        P("dp", None),
        P("dp", None, None),
        P("dp", None),
        P("dp", None, "tensor", None),
        P("dp", "tensor", None),
        P(),
        P(),
        P(),
        P(),
        P("tensor", None, None),
        P("tensor", None, None),
        P("tensor", None, None),
        P("tensor", None, None),
        P("tensor", None, None),
        P("tensor", None, None),
        P("tensor", None, None),
        P("tensor", None),
        P("tensor", None),
        P(None, "tensor"),
        P("tensor", None),
        P(("dp", "tensor"), None),
    )
    return jax.shard_map(
        on_device,
        mesh=mesh,
        in_specs=placed,
        out_specs=(
            P(("dp", "tensor"), None),
            P(("dp", "tensor"), None),
            P(),
            P(),
            P(),
            P(),
            P("tensor", "dp", None),
            P("tensor", "dp", None),
            P("tensor", "dp", None),
            P("tensor", "dp", None),
            P("tensor", "dp", None),
            P("tensor", "dp", None),
            P("tensor", None, "dp"),
            P(),
            P(),
            P("dp", "tensor"),
            P("tensor", "dp"),
        ),
        check_vma=False,
    )
```

```python
import functools
import math

import jax
import jax.numpy as jnp
from jax import lax
from jax.experimental import pallas as pl
from jax.experimental.pallas import tpu as pltpu
from jax.sharding import PartitionSpec as P

EPSILON = 1e-05
ROOT_HALF = 0.7071067811865476
INVERSE_ROOT_TAU = 0.3989422804014327
ROWS = 256
GROUP = 8
MIB = 1024 * 1024
BF16 = jnp.bfloat16
F32 = jnp.float32


def mm(left, right):
    return jnp.dot(left, right, preferred_element_type=F32)


def mm_nt(left, right):
    return lax.dot_general(left, right, (((1,), (1,)), ((), ())), preferred_element_type=F32)


def mm_tn(left, right):
    return lax.dot_general(left, right, (((0,), (0,)), ((), ())), preferred_element_type=F32)


def norm_parts(values):
    center = values - jnp.mean(values, axis=-1, keepdims=True)
    inv_std = lax.rsqrt(jnp.mean(center * center, axis=-1, keepdims=True) + EPSILON)
    return center * inv_std, inv_std


def norm_back(upstream, normal, inv_std, gain):
    scaled = upstream * gain
    return inv_std * (
        scaled
        - jnp.mean(scaled, axis=-1, keepdims=True)
        - normal * jnp.mean(scaled * normal, axis=-1, keepdims=True)
    )


def params():
    return pltpu.CompilerParams(vmem_limit_bytes=63 * MIB)


def cost(microseconds):
    return pl.CostEstimate(
        flops=int(microseconds * 1.15e9), bytes_accessed=MIB, transcendentals=0
    )


def struct(shape, dtype):
    return jax.ShapeDtypeStruct(shape, dtype)


def whole(*shape):
    return pl.BlockSpec(shape, lambda *_: (0,) * len(shape))

LANES = 128


def lane_of(rows):
    return lax.broadcasted_iota(jnp.int32, (rows, LANES), 1)


def picked(routes, head_dim):
    rows = routes.shape[1]
    routes = jnp.concatenate([routes, jnp.zeros((6, rows), jnp.int32)], axis=0).astype(F32).T
    lane = (lane_of(rows) - head_dim).astype(F32)
    return (lane == routes[:, 0:1]) | (lane == routes[:, 1:2])


def after(array, *deps):
    def body(*refs):
        del refs

    spec = pl.BlockSpec(memory_space=pl.ANY)
    return pl.pallas_call(
        body,
        in_specs=[spec] * (1 + len(deps)),
        out_specs=spec,
        out_shape=struct(array.shape, array.dtype),
        input_output_aliases={0: 0},
        name="after",
    )(array, *deps)


def together(*arrays):
    def body(*refs):
        del refs

    spec = pl.BlockSpec(memory_space=pl.ANY)
    return pl.pallas_call(
        body,
        in_specs=[spec] * len(arrays),
        out_specs=[spec] * len(arrays),
        out_shape=[struct(a.shape, a.dtype) for a in arrays],
        input_output_aliases={i: i for i in range(len(arrays))},
        name="together",
    )(*arrays)


def project_kernel(
    experts,
    head_dim,
    mem_steps,
    scale,
    mem_ref,
    tok_ref,
    gain_ref,
    bias_ref,
    key_w_ref,
    vsel_ref,
    value_w_ref,
    query_w_ref,
    osel_ref,
    vroute_ref,
    oroute_ref,
    cb_ref,
    pb_ref,
    w_out_ref,
    normed_ref,
    key_ref,
    val_ref,
    every_ref,
    vgate_ref,
    qc_ref,
    qp_ref,
    ogate_ref,
    w_ref,
):
    step = pl.program_id(0)
    query = (1 + experts) * LANES

    @pl.when(step == 0)
    def _():
        w_ref[...] = jnp.zeros_like(w_ref)
        w_ref[:head_dim, :] = key_w_ref[...]
        w_ref[head_dim : head_dim + experts, :] = vsel_ref[...]
        for e in range(experts):
            w_ref[(1 + e) * LANES : (1 + e) * LANES + head_dim, :] = value_w_ref[
                e * head_dim : (e + 1) * head_dim, :
            ]
        w_ref[query : query + head_dim, :] = query_w_ref[...]
        w_ref[query + head_dim : query + head_dim + experts, :] = osel_ref[...]

    size = w_out_ref.shape[0]
    w_out_ref[...] = w_ref[pl.ds(pl.multiple_of(step * size, size), size), :]

    def rows_part(rows_ref, columns, last):
        blocks = [slice(i * ROWS, (i + 1) * ROWS) for i in range(rows_ref.shape[0] // ROWS)]
        normed, outs = [], []
        for rows in blocks:
            normal, _ = norm_parts(rows_ref[rows, :].astype(F32))
            normed.append((normal * gain_ref[...] + bias_ref[...]).astype(BF16))
            outs.append(mm_nt(normed[-1], w_ref[:columns, :]))
        lane = lane_of(ROWS)
        real = lane < head_dim
        for rows, norm, out in zip(blocks, normed, outs):
            normed_ref[rows, :] = norm
            first = out[:, :LANES]
            key_ref[rows, :] = jnp.where(real, first, 0.0).astype(BF16)
            every_ref[rows, :] = out[:, LANES:query].astype(BF16)
            gate = jnp.where(picked(vroute_ref[:, rows], head_dim), jax.nn.sigmoid(first), 0.0)
            vgate_ref[rows, :] = gate
            value = jnp.zeros((ROWS, LANES), F32)
            for e in range(experts):
                value = value + gate[:, head_dim + e : head_dim + e + 1] * (
                    out[:, (1 + e) * LANES : (2 + e) * LANES]
                )
            val_ref[rows, :] = value.astype(BF16)
            if last:
                q = out[:, query:]
                qc_ref[rows, :] = jnp.where(real, (q + cb_ref[...]) * scale, 0.0).astype(BF16)
                qp_ref[rows, :] = jnp.where(real, (q + pb_ref[...]) * scale, 0.0).astype(BF16)
                ogate_ref[rows, :] = jnp.where(
                    picked(oroute_ref[:, rows], head_dim), jax.nn.sigmoid(q), 0.0
                )

    @pl.when(step < mem_steps)
    def _():
        rows_part(mem_ref, query, False)

    @pl.when(step >= mem_steps)
    def _():
        rows_part(tok_ref, query + LANES, True)


def project(memory, tokens, gain, bias, weights, vroutes, oroutes, cb, pb, experts, head_dim):
    mem, width = memory.shape
    toks = tokens.shape[0]
    big = 2 * ROWS
    mem_steps, tok_steps = mem // big, toks // big
    steps = mem_steps + tok_steps
    keys = mem + toks
    cols = width
    mem_row = lambda i: (jnp.minimum(i, mem_steps - 1), 0)
    tok_row = lambda i: (jnp.maximum(i - mem_steps, 0), 0)
    row = lambda i: (i, 0)
    return pl.pallas_call(
        functools.partial(project_kernel, experts, head_dim, mem_steps, head_dim ** (-0.5)),
        grid=(steps,),
        in_specs=[
            pl.BlockSpec((big, width), mem_row),
            pl.BlockSpec((big, width), tok_row),
            whole(1, width),
            whole(1, width),
        ]
        + [whole(*w.shape) for w in weights]
        + [
            pl.BlockSpec((vroutes.shape[0], big), lambda i: (0, i)),
            pl.BlockSpec((oroutes.shape[0], big), lambda i: (0, jnp.maximum(i - mem_steps, 0))),
            whole(1, LANES),
            whole(1, LANES),
        ],
        out_specs=[
            pl.BlockSpec((cols // steps, width), row),
            pl.BlockSpec((big, width), row),
            pl.BlockSpec((big, LANES), row),
            pl.BlockSpec((big, LANES), row),
            pl.BlockSpec((big, experts * LANES), row),
            pl.BlockSpec((big, LANES), row),
            pl.BlockSpec((big, LANES), tok_row),
            pl.BlockSpec((big, LANES), tok_row),
            pl.BlockSpec((big, LANES), tok_row),
        ],
        out_shape=[
            struct((cols, width), BF16),
            struct((keys, width), BF16),
            struct((keys, LANES), BF16),
            struct((keys, LANES), BF16),
            struct((keys, experts * LANES), BF16),
            struct((keys, LANES), F32),
            struct((toks, LANES), BF16),
            struct((toks, LANES), BF16),
            struct((toks, LANES), F32),
        ],
        scratch_shapes=[pltpu.VMEM((cols, width), BF16)],
        compiler_params=params(),
        cost_estimate=cost(12),
        name="project",
    )(memory, tokens, gain, bias, *weights, vroutes, oroutes, cb, pb)


def attend_kernel(
    span,
    head_dim,
    count,
    z_ref,
    qc_ref,
    qp_ref,
    key_ref,
    val_ref,
    rel_ref,
    segk_ref,
    segq_ref,
    ogate_ref,
    heads_ref,
    probs_ref,
    *pack_refs,
):
    step = pl.program_id(0)
    wide = span + ROWS
    column = lax.broadcasted_iota(jnp.int32, (ROWS, ROWS), 1)
    causal = column <= lax.broadcasted_iota(jnp.int32, (ROWS, ROWS), 0)
    for b in range(count):
        rows = slice(b * ROWS, (b + 1) * ROWS)
        window = pl.ds((step * count + b) * ROWS, wide)
        content = mm_nt(qc_ref[rows, :], key_ref[window, :])
        reverse = mm_nt(qp_ref[rows, :], rel_ref[...])
        reverse = jnp.concatenate([reverse, jnp.zeros((ROWS, ROWS), F32)], axis=1)
        scores = content + pltpu.roll(reverse, 1, 1, stride=1, stride_axis=0)
        same = segk_ref[b] == segq_ref[rows, :]
        allowed = jnp.concatenate([same[:, :span], same[:, span:] & causal], axis=1)
        scores = jnp.where(allowed, scores, -1e30)
        expo = jnp.exp(scores - jnp.max(scores, axis=1, keepdims=True))
        probs = (expo * (1.0 / jnp.sum(expo, axis=1, keepdims=True))).astype(BF16)
        probs_ref[rows, :] = probs
        heads = mm(probs, val_ref[window, :])
        heads_ref[rows, :] = heads
        packed = jnp.where(lane_of(ROWS) < head_dim, heads, ogate_ref[rows, :]).astype(BF16)
        slot = (step * count + b) ^ z_ref[0]
        for m, pack_ref in enumerate(pack_refs):

            @pl.when(slot == m)
            def _():
                pack_ref[...] = packed


def attend(rank, qc, qp, key_vecs, value_vecs, rel_reverse, seg_keys, seg_query, ogate, head_dim):
    toks = qc.shape[0]
    keys = key_vecs.shape[0]
    span = rel_reverse.shape[0]
    steps = toks // ROWS
    count = 2
    big = count * ROWS
    wide = span + ROWS
    row = lambda i, z: (i, 0)
    return pl.pallas_call(
        functools.partial(attend_kernel, span, head_dim, count),
        grid_spec=pltpu.PrefetchScalarGridSpec(
            num_scalar_prefetch=1,
            grid=(steps // count,),
            in_specs=[
                pl.BlockSpec((big, LANES), row),
                pl.BlockSpec((big, LANES), row),
                whole(keys, LANES),
                whole(keys, LANES),
                whole(span, LANES),
                pl.BlockSpec((count, 1, wide), lambda i, z: (i, 0, 0)),
                pl.BlockSpec((big, 1), row),
                pl.BlockSpec((big, LANES), row),
            ],
            out_specs=[
                pl.BlockSpec((big, LANES), row),
                pl.BlockSpec((big, wide), row),
            ]
            + [whole(ROWS, LANES)] * steps,
        ),
        out_shape=[struct((toks, LANES), F32), struct((toks, wide), BF16)]
        + [struct((ROWS, LANES), BF16)] * steps,
        compiler_params=params(),
        cost_estimate=cost(8),
        name="attend",
    )(rank, qc, qp, key_vecs, value_vecs, rel_reverse, seg_keys, seg_query, ogate)


def attend_back_kernel(
    span,
    experts,
    head_dim,
    parts,
    z_ref,
    qc_ref,
    qp_ref,
    key_ref,
    val_ref,
    rel_ref,
    probs_ref,
    heads_ref,
    ogate_ref,
    every_ref,
    vgate_ref,
    *refs,
):
    back_refs, refs = refs[:parts], refs[parts:]
    key_grad_ref, value_grad_ref, query_grad_ref, rel_grad_ref, bias_ref = refs[:5]
    pack_refs, refs = refs[5 : 5 + parts], refs[5 + parts :]
    keys_scr, values_scr, rel_scr, query_scr, back_scr = refs
    step = pl.program_id(0)
    steps = pl.num_programs(0)
    wide = span + ROWS
    mem = keys_scr.shape[0] - steps * ROWS
    scale = head_dim ** (-0.5)
    real = lane_of(ROWS) < head_dim

    @pl.when(step == 0)
    def _():
        keys_scr[...] = jnp.zeros_like(keys_scr)
        values_scr[...] = jnp.zeros_like(values_scr)
        rel_scr[...] = jnp.zeros_like(rel_scr)
        bias_ref[...] = jnp.zeros_like(bias_ref)

    slot = step ^ z_ref[0]
    for m, back_ref in enumerate(back_refs):

        @pl.when(slot == m)
        def _():
            back_scr[...] = back_ref[...]

    window = pl.ds(step * ROWS, wide)
    keys = key_ref[window, :]
    vals = val_ref[window, :]
    back = back_scr[...].astype(F32)
    out_grad = jnp.where(real, back, 0.0)
    delta = jnp.sum(out_grad * heads_ref[...], axis=1, keepdims=True)
    out_grad = out_grad.astype(BF16)
    probs = probs_ref[...]
    probs_grad = mm_nt(out_grad, vals)
    score_grad = (probs.astype(F32) * (probs_grad - delta)).astype(BF16)
    content_grad = mm(score_grad, keys).astype(BF16).astype(F32) * scale
    keys_scr[window, :] += mm_tn(score_grad, qc_ref[...])
    values_scr[window, :] += mm_tn(probs, out_grad)
    flip = (
        lax.broadcasted_iota(jnp.int32, (ROWS, ROWS), 0)
        + lax.broadcasted_iota(jnp.int32, (ROWS, ROWS), 1)
        == ROWS - 1
    ).astype(BF16)
    turned = mm(flip, score_grad)
    turned = pltpu.roll(turned, span, 1, stride=1, stride_axis=0)[:, :span].astype(BF16)
    place_grad = mm(turned, rel_ref[...]).astype(BF16)
    position_grad = mm(flip, place_grad) * scale
    rel_scr[...] += mm_tn(turned, mm(flip, qp_ref[...]).astype(BF16))
    bias_ref[0:1, :] += jnp.sum(content_grad, axis=0, keepdims=True)
    bias_ref[1:2, :] += jnp.sum(position_grad, axis=0, keepdims=True)
    gate = ogate_ref[...]
    query_grad = jnp.where(real, content_grad + position_grad, back * gate * (1.0 - gate))
    query_grad = query_grad.astype(BF16)
    query_grad_ref[...] = query_grad
    query_scr[pl.ds(step * ROWS, ROWS), :] = query_grad

    @pl.when(step == steps - 1)
    def _():
        rel_grad_ref[...] = rel_scr[...].astype(BF16)

        @pl.loop(0, (mem + steps * ROWS) // ROWS)
        def _(block):
            rows = pl.ds(block * ROWS, ROWS)
            value_grad = values_scr[rows, :]
            gates = vgate_ref[rows, :]
            value_grad_ref[rows, :] = value_grad
            logit = keys_scr[rows, :]
            lane = lane_of(ROWS)
            for e in range(experts):
                part = every_ref[rows, e * LANES : (e + 1) * LANES].astype(F32)
                total = jnp.sum(value_grad * part, axis=1, keepdims=True)
                logit = jnp.where(lane == head_dim + e, total, logit)
            key_grad = jnp.where(real, logit, logit * gates * (1.0 - gates)).astype(BF16)
            key_grad_ref[rows, :] = key_grad

            @pl.when(block * ROWS >= mem)
            def _():
                place = block - mem // ROWS
                value_pack = jnp.where(real, value_grad, gates).astype(BF16)
                for m, pack_ref in enumerate(pack_refs):

                    @pl.when((place ^ z_ref[0]) == m)
                    def _():
                        pack_ref[0] = key_grad
                        pack_ref[1] = value_pack
                        pack_ref[2] = query_scr[pl.ds(place * ROWS, ROWS), :]


def attend_back(
    rank,
    qc,
    qp,
    key_vecs,
    value_vecs,
    rel_reverse,
    probs,
    heads,
    ogate,
    every,
    vgate,
    backs,
    head_dim,
):
    toks = qc.shape[0]
    keys = key_vecs.shape[0]
    span = rel_reverse.shape[0]
    steps = toks // ROWS
    wide = span + ROWS
    experts = every.shape[1] // LANES
    row = lambda i, z: (i, 0)
    return pl.pallas_call(
        functools.partial(attend_back_kernel, span, experts, head_dim, steps),
        grid_spec=pltpu.PrefetchScalarGridSpec(
            num_scalar_prefetch=1,
            grid=(steps,),
            in_specs=[
                pl.BlockSpec((ROWS, LANES), row),
                pl.BlockSpec((ROWS, LANES), row),
                whole(keys, LANES),
                whole(keys, LANES),
                whole(span, LANES),
                pl.BlockSpec((ROWS, wide), row),
                pl.BlockSpec((ROWS, LANES), row),
                pl.BlockSpec((ROWS, LANES), row),
                whole(keys, experts * LANES),
                whole(keys, LANES),
            ]
            + [whole(ROWS, LANES)] * steps,
            out_specs=[
                whole(keys, LANES),
                whole(keys, LANES),
                pl.BlockSpec((ROWS, LANES), row),
                whole(span, LANES),
                whole(2, LANES),
            ]
            + [whole(3, ROWS, LANES)] * steps,
            scratch_shapes=[
                pltpu.VMEM((keys, LANES), F32),
                pltpu.VMEM((keys, LANES), F32),
                pltpu.VMEM((span, LANES), F32),
                pltpu.VMEM((toks, LANES), BF16),
                pltpu.VMEM((ROWS, LANES), BF16),
            ],
        ),
        out_shape=[
            struct((keys, LANES), BF16),
            struct((keys, LANES), F32),
            struct((toks, LANES), BF16),
            struct((span, LANES), BF16),
            struct((2, LANES), F32),
        ]
        + [struct((3, ROWS, LANES), BF16)] * steps,
        compiler_params=params(),
        cost_estimate=cost(15),
        name="attend_back",
    )(rank, qc, qp, key_vecs, value_vecs, rel_reverse, probs, heads, ogate, every, vgate, *backs)


def mix_kernel(experts, head_dim, heads, where_ref, *refs):
    pack_refs, refs = refs[:heads], refs[heads:]
    own_ref, even_ref, odd_ref, tok_ref, gain_ref, bias_ref = refs[:6]
    full_ref, middle_ref, up_ref, mixed_scr, attn_scr = refs[6:]
    step = pl.program_id(0)
    steps = pl.num_programs(0)

    @pl.when(step == 0)
    def _():
        real = lane_of(ROWS) < head_dim
        for m in range(heads):
            pack = pack_refs[m][...].astype(F32)
            out = jnp.where(real, pack, 0.0)
            for e in range(experts):
                gate = pack[:, head_dim + e : head_dim + e + 1]
                mixed_scr[m, :, e * LANES : (e + 1) * LANES] = (gate * out).astype(BF16)

    turned = where_ref[1] == 1
    total = None
    for m in range(heads):
        if m == 0:
            weight = own_ref[...]
        else:
            even, odd = even_ref[0, m - 1], odd_ref[0, m - 1]
            weight = jnp.concatenate(
                [jnp.where(turned, odd, even), jnp.where(turned, even, odd)], axis=1
            )
        for e in range(experts):
            full_ref[m, e * LANES : e * LANES + head_dim, :] = weight[
                e * head_dim : (e + 1) * head_dim
            ]
            full_ref[m, e * LANES + head_dim : (e + 1) * LANES, :] = jnp.zeros(
                (LANES - head_dim, weight.shape[1]), BF16
            )
        part = mm(mixed_scr[m], full_ref[m])
        total = part if total is None else total + part
    block = where_ref[0] ^ step
    size = total.shape[1]
    attn_scr[:, pl.ds(pl.multiple_of(block * size, size), size)] = total

    @pl.when(step == steps - 1)
    def _():
        middle = tok_ref[...].astype(F32) + attn_scr[...]
        middle_ref[...] = middle
        normal, _ = norm_parts(middle)
        up_ref[...] = (normal * gain_ref[...] + bias_ref[...]).astype(BF16)


def mix(where, packs, own_weight, even, odd, tokens, gain, bias, experts, head_dim):
    heads = len(packs)
    rows = packs[0].shape[0]
    depth, width = own_weight.shape
    steps = even.shape[0]
    size = width // steps
    return pl.pallas_call(
        functools.partial(mix_kernel, experts, head_dim, heads),
        grid_spec=pltpu.PrefetchScalarGridSpec(
            num_scalar_prefetch=1,
            grid=(steps,),
            in_specs=[whole(rows, LANES)] * heads
            + [
                pl.BlockSpec((depth, size), lambda s, w: (0, w[0] ^ s)),
                pl.BlockSpec((1,) + even.shape[1:], lambda s, w: (s, 0, 0, 0)),
                pl.BlockSpec((1,) + odd.shape[1:], lambda s, w: (s, 0, 0, 0)),
                pl.BlockSpec((rows, width), lambda s, w: (w[2], 0)),
                whole(1, width),
                whole(1, width),
            ],
            out_specs=[
                pl.BlockSpec((heads, experts * LANES, size), lambda s, w: (0, 0, w[0] ^ s)),
                whole(rows, width),
                whole(rows, width),
            ],
            scratch_shapes=[
                pltpu.VMEM((heads, rows, experts * LANES), BF16),
                pltpu.VMEM((rows, width), F32),
            ],
        ),
        out_shape=[
            struct((heads, experts * LANES, width), BF16),
            struct((rows, width), F32),
            struct((rows, width), BF16),
        ],
        compiler_params=params(),
        cost_estimate=cost(9),
        name="mix",
    )(where, *packs, own_weight, even, odd, tokens, gain, bias)


def mix_back_kernel(experts, head_dim, heads, *refs):
    grad0_ref, grad1_ref, cot_ref, middle_ref, gain_ref, full_ref = refs[:6]
    pack_refs, refs = refs[6 : 6 + heads], refs[6 + heads :]
    middle_grad_ref, attn_grad_ref, sums_ref = refs[:3]
    back_refs = refs[3 : 3 + heads]
    step = pl.program_id(0)

    @pl.when(step == 0)
    def _():
        upstream = grad0_ref[...].astype(F32) + grad1_ref[...].astype(F32)
        normal, inv_std = norm_parts(middle_ref[...])
        sums_ref[0:1, :] = jnp.sum(upstream * normal, axis=0, keepdims=True)
        sums_ref[1:2, :] = jnp.sum(upstream, axis=0, keepdims=True)
        grad = cot_ref[...].astype(F32) + norm_back(upstream, normal, inv_std, gain_ref[...])
        middle_grad_ref[...] = grad
        attn_grad_ref[...] = grad.astype(BF16)

    mixed_grad = mm_nt(attn_grad_ref[...], full_ref[0]).astype(BF16).astype(F32)
    lane = lane_of(ROWS)
    real = lane < head_dim
    for m in range(heads):

        @pl.when(step == m)
        def _():
            pack = pack_refs[m][...].astype(F32)
            total = jnp.zeros((ROWS, LANES), F32)
            gates = jnp.zeros((ROWS, LANES), F32)
            for e in range(experts):
                part = mixed_grad[:, e * LANES : (e + 1) * LANES]
                total = total + pack[:, head_dim + e : head_dim + e + 1] * part
                inner = jnp.sum(part * pack, axis=1, keepdims=True)
                gates = jnp.where(lane == head_dim + e, inner, gates)
            back_refs[m][...] = jnp.where(real, total, gates).astype(BF16)


def mix_back(own_grad, far_grad, cot, middle, gain, full, packs, experts, head_dim):
    heads, depth, width = full.shape
    rows = middle.shape[0]
    return pl.pallas_call(
        functools.partial(mix_back_kernel, experts, head_dim, heads),
        grid=(heads,),
        in_specs=[whole(rows, width)] * 4
        + [whole(1, width), pl.BlockSpec((1, depth, width), lambda m: (m, 0, 0))]
        + [whole(rows, LANES)] * heads,
        out_specs=[whole(rows, width), whole(rows, width), whole(2, width)]
        + [whole(rows, LANES)] * heads,
        out_shape=[
            struct((rows, width), F32),
            struct((rows, width), BF16),
            struct((2, width), F32),
        ]
        + [struct((rows, LANES), BF16)] * heads,
        compiler_params=params(),
        cost_estimate=cost(10),
        name="mix_back",
    )(own_grad, far_grad, cot, middle, gain, full, *packs)


def feed_kernel(half, up_ref, cot_ref, wu_ref, wd_ref, far_u_ref, far_d_ref, *refs):
    refs = refs[-6:]
    hidden_ref, pre_grad_ref, out_ref, up_grad_ref, out_scr, up_scr = refs
    step = pl.program_id(0)
    steps = pl.num_programs(0)
    width = up_ref.shape[1]
    count = wu_ref.shape[1] // ROWS

    @pl.when(step == 0)
    def _():
        out_scr[...] = jnp.zeros_like(out_scr)
        up_scr[...] = jnp.zeros_like(up_scr)

    def part(w_up, w_down):
        pres, grads = [], []
        for b in range(count):
            cols = slice(b * ROWS, (b + 1) * ROWS)
            pres.append(mm(up_ref[...], w_up[:, cols]))
            grads.append(mm_nt(cot_ref[...], w_down[cols, :]))
        out, up_grad = None, None
        for b in range(count):
            cols = slice(b * ROWS, (b + 1) * ROWS)
            pre = pres[b]
            hidden_grad = grads[b].astype(BF16).astype(F32)
            phi = 0.5 * (1.0 + lax.erf(pre * ROOT_HALF))
            hidden = (pre * phi).astype(BF16)
            slope = phi + pre * jnp.exp(-0.5 * pre * pre) * INVERSE_ROOT_TAU
            pre_grad = (hidden_grad * slope).astype(BF16)
            hidden_ref[:, cols] = hidden
            pre_grad_ref[:, cols] = pre_grad
            out_part, up_part = mm(hidden, w_down[cols, :]), mm_nt(pre_grad, w_up[:, cols])
            out = out_part if out is None else out + out_part
            up_grad = up_part if up_grad is None else up_grad + up_part
        out_scr[...] += out
        up_scr[...] += up_grad

    @pl.when(step < half)
    def _():
        part(wu_ref[...], wd_ref[...])

    @pl.when(step >= half)
    def _():
        part(far_u_ref[...].reshape(width, -1), far_d_ref[...].reshape(-1, width))

    @pl.when(step == steps - 1)
    def _():
        out_ref[...] = out_scr[...].astype(out_ref.dtype)
        up_grad_ref[...] = up_scr[...].astype(up_grad_ref.dtype)


def feed(up_in, cot, w_up, w_down, far, dtype, *deps):
    rows, width = up_in.shape
    hidden = w_up.shape[1]
    size = 2 * ROWS
    half = hidden // size
    pieces, _, depth, _ = far.shape
    count = size // depth
    own = lambda i: jnp.minimum(i, half - 1)
    other = lambda i: jnp.maximum(i - half, 0)
    return pl.pallas_call(
        functools.partial(feed_kernel, half),
        grid=(2 * half,),
        in_specs=[
            whole(rows, width),
            whole(rows, width),
            pl.BlockSpec((width, size), lambda i: (0, own(i))),
            pl.BlockSpec((size, width), lambda i: (own(i), 0)),
            pl.BlockSpec((pieces, 1, depth, size), lambda i: (0, 0, 0, other(i))),
            pl.BlockSpec((count, 1, depth, width), lambda i: (other(i), 1, 0, 0)),
        ]
        + [pl.BlockSpec(memory_space=pl.ANY)] * len(deps),
        out_specs=[
            pl.BlockSpec((rows, size), lambda i: (0, i)),
            pl.BlockSpec((rows, size), lambda i: (0, i)),
            whole(rows, width),
            whole(rows, width),
        ],
        out_shape=[
            struct((rows, 2 * hidden), BF16),
            struct((rows, 2 * hidden), BF16),
            struct((rows, width), dtype),
            struct((rows, width), dtype),
        ],
        scratch_shapes=[pltpu.VMEM((rows, width), F32), pltpu.VMEM((rows, width), F32)],
        compiler_params=params(),
        cost_estimate=cost(10),
        name="feed",
    )(up_in, cot, w_up, w_down, far, far, *deps)


def feed_weights_kernel(count, half, *refs):
    lefts, refs = refs[: 2 * count], refs[2 * count :]
    rights, out_ref = refs[: 2 * count], refs[2 * count]
    step = pl.program_id(0)

    for which in range(2):

        @pl.when((step // half) % 2 == which)
        def _():
            total = None
            for m in range(which * count, (which + 1) * count):
                part = mm_tn(lefts[m][...], rights[m][...])
                total = part if total is None else total + part
            out_ref[...] = total.astype(BF16)


def feed_weights(ups, cots, pre_grads, hiddens):
    count = len(ups)
    rows, width = ups[0].shape
    hidden = hiddens[0].shape[1] // 2
    size = 512
    half = hidden // size

    def columns(which):
        def at(i):
            shard, inner = i // (2 * half), i % (2 * half)
            return (0, shard * half + jnp.clip(inner - which * half, 0, half - 1))

        return pl.BlockSpec((rows, size), at)

    return pl.pallas_call(
        functools.partial(feed_weights_kernel, count, half),
        grid=(4 * half,),
        in_specs=[whole(rows, width)] * (2 * count)
        + [columns(0)] * count
        + [columns(1)] * count,
        out_specs=pl.BlockSpec((width, size), lambda i: (0, i)),
        out_shape=struct((width, 4 * hidden), BF16),
        compiler_params=params(),
        cost_estimate=cost(11),
        name="feed_weights",
    )(*ups, *cots, *pre_grads, *hiddens)


def out_weights_kernel(experts, head_dim, heads, where_ref, *refs):
    own_refs, near_ref = refs[:heads], refs[heads]
    grad_ref, near_grad_ref, keep_ref, send_ref, mixed_scr, scr = refs[heads + 1 :]
    real = lane_of(ROWS) < head_dim

    def fill(begin, pack):
        pack = pack.astype(F32)
        out = jnp.where(real, pack, 0.0)
        for e in range(experts):
            gate = pack[:, head_dim + e : head_dim + e + 1]
            mixed_scr[begin : begin + ROWS, e * LANES : (e + 1) * LANES] = (gate * out).astype(
                BF16
            )

    for m in range(heads):

        @pl.when(pl.program_id(0) == m)
        def _():
            fill(0, own_refs[m][...])
            fill(ROWS, near_ref[m])

    scr[...] = mm_tn(mixed_scr[:ROWS], grad_ref[...]) + mm_tn(
        mixed_scr[ROWS:], near_grad_ref[...]
    )
    for k in range(GROUP):
        target = send_ref if k % 2 else keep_ref
        lanes = pl.ds(pl.multiple_of((where_ref[0] ^ k) * LANES, LANES), LANES)
        for e in range(experts):
            target[k // 2, e * head_dim : (e + 1) * head_dim, :] = scr[
                e * LANES : e * LANES + head_dim, lanes
            ].astype(BF16)


def out_weights(where, own_packs, near_packs, grad, near_grad, experts, head_dim):
    heads = len(own_packs)
    rows, width = grad.shape
    depth = experts * head_dim
    shape = (GROUP // 2, heads * depth, width // GROUP)
    spec = pl.BlockSpec((GROUP // 2, depth, width // GROUP), lambda m, w: (0, m, 0))
    return pl.pallas_call(
        functools.partial(out_weights_kernel, experts, head_dim, heads),
        grid_spec=pltpu.PrefetchScalarGridSpec(
            num_scalar_prefetch=1,
            grid=(heads,),
            in_specs=[whole(rows, LANES)] * heads
            + [whole(*near_packs.shape)]
            + [whole(rows, width)] * 2,
            out_specs=[spec] * 2,
            scratch_shapes=[
                pltpu.VMEM((2 * rows, experts * LANES), BF16),
                pltpu.VMEM((experts * LANES, width), F32),
            ],
        ),
        out_shape=[struct(shape, BF16)] * 2,
        compiler_params=params(),
        cost_estimate=cost(5),
        name="out_weights",
    )(where, *own_packs, near_packs, grad, near_grad)


def weights_kernel(
    experts,
    head_dim,
    counts,
    where_ref,
    normed_ref,
    key_ref,
    value_ref,
    gate_ref,
    query_ref,
    table_ref,
    rel_ref,
    w_ref,
    gain_ref,
    bias_ref,
    sums_ref,
    biases_ref,
    keep_ref,
    send_ref,
    small_ref,
    grads_scr,
    sum_scr,
    main_scr,
    rel_scr,
):
    step = pl.program_id(0)
    mem_steps, key_steps, rel_steps = counts
    query = (1 + experts) * LANES

    @pl.when(step == 0)
    def _():
        main_scr[...] = jnp.zeros_like(main_scr)
        sum_scr[...] = jnp.zeros_like(sum_scr)
        rel_scr[...] = jnp.zeros_like(rel_scr)

    def add(columns):
        grads = grads_scr[:, :columns]
        main_scr[:columns, :] += mm_tn(grads, normed_ref[...])
        sum_scr[:columns, :] += mm_tn(grads, jnp.ones((grads.shape[0], LANES), BF16))

    @pl.when(step < key_steps)
    def _():
        value_grad = value_ref[...]
        grads_scr[:, :LANES] = key_ref[...]
        for e in range(experts):
            gate = gate_ref[:, head_dim + e : head_dim + e + 1]
            grads_scr[:, LANES * (1 + e) : LANES * (2 + e)] = (gate * value_grad).astype(BF16)

    @pl.when(step < mem_steps)
    def _():
        add(query)

    @pl.when((step >= mem_steps) & (step < key_steps))
    def _():
        grads_scr[:, query:] = query_ref[...]
        add(query + LANES)

    @pl.when(step >= key_steps)
    def _():
        rel_scr[...] += mm_tn(rel_ref[...], table_ref[...])

    @pl.when(step == key_steps + rel_steps - 1)
    def _():
        weights = w_ref[...].astype(F32)
        bias_one = jnp.sum(weights * sum_scr[:, 0:1], axis=0, keepdims=True)
        inner = jnp.sum(weights * main_scr[...], axis=0, keepdims=True)
        small_ref[...] = jnp.zeros_like(small_ref)
        small_ref[0:1, :] = (inner - bias_ref[...] * bias_one) / gain_ref[...]
        small_ref[1:2, :] = bias_one
        small_ref[2:4, :] = sums_ref[...]
        small_ref[4:6, pl.ds(pl.multiple_of(where_ref[1] * LANES, LANES), LANES)] = biases_ref[...]
        for k in range(GROUP):
            target = send_ref if k % 2 else keep_ref
            at = k // 2
            lanes = pl.ds(pl.multiple_of((where_ref[0] ^ k) * LANES, LANES), LANES)
            row = 0

            def put(source, begin, size):
                target[at, row : row + size, :] = source[begin : begin + size, lanes].astype(BF16)
                return row + size

            for section in range(2 + experts):
                row = put(main_scr, section * LANES, head_dim)
            row = put(rel_scr, 0, head_dim)
            target[at, row:, :] = jnp.concatenate(
                [
                    main_scr[head_dim : head_dim + 8, lanes],
                    main_scr[query + head_dim : query + head_dim + 8, lanes],
                ],
                axis=0,
            ).astype(BF16)


def weight_grads(
    where,
    normed,
    key_grad,
    value_grad,
    gates,
    query_grad,
    table,
    rel_grad,
    w_all,
    gain,
    bias,
    sums_two,
    bias_sums,
    mem,
    head_dim,
    experts,
):
    keys, width = normed.shape
    cols = (2 + experts) * LANES
    big = 2 * ROWS
    mem_steps, key_steps = mem // big, keys // big
    rel_steps = table.shape[0] // big
    counts = (mem_steps, key_steps, rel_steps)
    rows = (3 + experts) * head_dim + 16
    key_row = lambda i, w: (jnp.minimum(i, key_steps - 1), 0)
    tok_row = lambda i, w: (jnp.clip(i - mem_steps, 0, key_steps - mem_steps - 1), 0)
    rel_row = lambda i, w: (jnp.clip(i - key_steps, 0, rel_steps - 1), 0)
    half = GROUP // 2
    return pl.pallas_call(
        functools.partial(weights_kernel, experts, head_dim, counts),
        grid_spec=pltpu.PrefetchScalarGridSpec(
            num_scalar_prefetch=1,
            grid=(key_steps + rel_steps,),
            in_specs=[
                pl.BlockSpec((big, width), key_row),
                pl.BlockSpec((big, LANES), key_row),
                pl.BlockSpec((big, LANES), key_row),
                pl.BlockSpec((big, LANES), key_row),
                pl.BlockSpec((big, LANES), tok_row),
                pl.BlockSpec((big, width), rel_row),
                pl.BlockSpec((big, LANES), rel_row),
                whole(cols, width),
                whole(1, width),
                whole(1, width),
                whole(2, width),
                whole(2, LANES),
            ],
            out_specs=[
                whole(half, rows, LANES),
                whole(half, rows, LANES),
                whole(8, width),
            ],
            scratch_shapes=[
                pltpu.VMEM((big, cols), BF16),
                pltpu.VMEM((cols, LANES), F32),
                pltpu.VMEM((cols, width), F32),
                pltpu.VMEM((LANES, width), F32),
            ],
        ),
        out_shape=[
            struct((half, rows, LANES), BF16),
            struct((half, rows, LANES), BF16),
            struct((8, width), F32),
        ],
        compiler_params=params(),
        cost_estimate=cost(15),
        name="weight_grads",
    )(
        where,
        normed,
        key_grad,
        value_grad,
        gates,
        query_grad,
        table,
        rel_grad,
        w_all,
        gain,
        bias,
        sums_two,
        bias_sums,
    )


def token_kernel(experts, head_dim, heads, z_ref, *refs):
    pack_refs, refs = refs[:heads], refs[heads:]
    own_ref, far_ref, tok_ref, mid_ref, gain_ref, out_ref, grads_scr, total_scr = refs
    step = pl.program_id(0)
    steps = pl.num_programs(0)
    query = (1 + experts) * LANES
    cols = query + LANES

    for m, pack_ref in enumerate(pack_refs):

        @pl.when(step == m)
        def _():
            value_pack = pack_ref[1].astype(F32)
            value_grad = jnp.where(lane_of(ROWS) < head_dim, value_pack, 0.0)
            grads_scr[:, :LANES] = pack_ref[0]
            for e in range(experts):
                gate = value_pack[:, head_dim + e : head_dim + e + 1]
                grads_scr[:, LANES * (1 + e) : LANES * (2 + e)] = (gate * value_grad).astype(BF16)
            grads_scr[:, query:] = pack_ref[2]

    @pl.when(step == 0)
    def _():
        total_scr[...] = mm(grads_scr[...], own_ref[:cols, :])

    @pl.when(step > 0)
    def _():
        weights = far_ref[...].reshape(-1, far_ref.shape[3])
        total_scr[...] += mm(grads_scr[...], weights[:cols, :])

    @pl.when(step == steps - 1)
    def _():
        normal, inv_std = norm_parts(tok_ref[...].astype(F32))
        out_ref[...] = mid_ref[...] + norm_back(total_scr[...], normal, inv_std, gain_ref[...])


def token_grads(rank, packs, own_w, far_w, tokens, middle_grad, gain, head_dim, experts):
    rows, width = middle_grad.shape
    heads = len(packs)
    pieces, _, piece, _ = far_w.shape
    shape = packs[0].shape
    cols = (2 + experts) * LANES
    return pl.pallas_call(
        functools.partial(token_kernel, experts, head_dim, heads),
        grid_spec=pltpu.PrefetchScalarGridSpec(
            num_scalar_prefetch=1,
            grid=(heads,),
            in_specs=[whole(*shape)] * heads
            + [
                whole(*own_w.shape),
                pl.BlockSpec(
                    (pieces, 1, piece, width), lambda m, z: (0, jnp.maximum(m - 1, 0), 0, 0)
                ),
                pl.BlockSpec((rows, width), lambda m, z: (z[0], 0)),
                whole(rows, width),
                whole(1, width),
            ],
            out_specs=whole(rows, width),
            scratch_shapes=[pltpu.VMEM((rows, cols), BF16), pltpu.VMEM((rows, width), F32)],
        ),
        out_shape=struct((rows, width), F32),
        compiler_params=params(),
        cost_estimate=cost(9),
        name="token_grads",
    )(rank, *packs, own_w, far_w, tokens, middle_grad, gain)


def swap(array, axis, mask):
    size = lax.axis_size(axis)
    return lax.ppermute(array, axis, [(i, i ^ mask) for i in range(size)])


def plus(left, right):
    return (left.astype(F32) + right.astype(F32)).astype(BF16)


def scatter_first(keep, far):
    return [plus(keep[m], far[m]) for m in range(keep.shape[0])]


def scatter_sends(blocks, unit):
    return [swap(blocks[m], "dp", 2 * m * unit) for m in range(1, len(blocks))]


def scatter_done(own, fars, unit, axis):
    out = own.astype(F32)
    for far in fars:
        out = out + far.astype(F32)
    mask = unit // 2
    while mask:
        size = out.shape[axis] // 2
        bit = (lax.axis_index("dp") // mask) % 2
        mine = lax.dynamic_slice_in_dim(out, bit * size, size, axis)
        theirs = lax.dynamic_slice_in_dim(out, (1 - bit) * size, size, axis)
        out = mine + swap(theirs.astype(BF16), "dp", mask).astype(F32)
        mask //= 2
    return out


def spread(far, *gates):
    pieces = [swap(far, "dp", 2 * m) for m in range(1, GROUP // 2)]
    even = after(jnp.stack([far] + pieces), *gates)
    odd = swap(even, "dp", 1)
    return even, odd


def on_device(
    tokens,
    memory,
    segments,
    value_routes,
    output_routes,
    first_gain,
    first_bias,
    second_gain,
    second_bias,
    query_head_weight,
    key_weight,
    position_weight,
    value_weight,
    value_select,
    output_expert_selector,
    output_expert_weight,
    content_bias,
    position_bias,
    up_projection_weight,
    down_projection_weight,
    cotangent,
):
    mem_len = memory.shape[1]
    toks, width = tokens.shape
    head_dim = query_head_weight.shape[2]
    experts = value_select.shape[2]
    hidden = up_projection_weight.shape[1]
    parts = lax.axis_size("tensor")
    rank = lax.axis_index("tensor")
    dp = lax.axis_size("dp")
    at = lax.axis_index("dp")
    others = range(1, parts)
    near, far_shard = 1, 2
    rank_ref = rank.reshape(1).astype(jnp.int32)
    row = lambda v: v.reshape(1, -1)
    lanes = lambda v: jnp.pad(v, ((0, 0), (0, LANES - head_dim)))

    own_out = output_expert_weight[0]
    size = width // GROUP
    own_block = lax.dynamic_slice_in_dim(own_out, (at % GROUP) * size, size, 1)
    far_out = jnp.concatenate([swap(own_block, "tensor", m) for m in others])
    cots = [cotangent, swap(cotangent, "tensor", near)]
    span = mem_len
    fine = 32
    rates = jnp.exp(jnp.arange(width // 2).astype(F32) * (-2.0 * math.log(10000.0) / width))
    coarse_at = (span - 1 - fine * jnp.arange(span // fine)).astype(F32)[:, None] * rates[None, :]
    fine_at = jnp.arange(fine).astype(F32)[:, None] * rates[None, :]
    sin_a, cos_a = jnp.sin(coarse_at)[:, None, :], jnp.cos(coarse_at)[:, None, :]
    sin_b, cos_b = jnp.sin(fine_at)[None, :, :], jnp.cos(fine_at)[None, :, :]
    sin_table = jnp.concatenate(
        [sin_a * cos_b - cos_a * sin_b, cos_a * cos_b + sin_a * sin_b], axis=2
    )
    sin_table = lax.optimization_barrier(sin_table.reshape(span, width).astype(BF16))
    rel_weight = jnp.concatenate(
        [position_weight[0].T, jnp.zeros((LANES - head_dim, width), BF16)]
    )
    rel_reverse = mm_nt(sin_table, rel_weight).astype(BF16)

    w_all, normed, key_vecs, value_vecs, every, vgate, qc, qp, ogate = project(
        memory[0],
        tokens,
        row(first_gain),
        row(first_bias),
        (
            key_weight[0].T,
            value_select[0].T,
            value_weight[0].T,
            query_head_weight[0].T,
            output_expert_selector[0].T,
        ),
        value_routes[0, :, 0].T,
        output_routes[:, 0].T,
        lanes(content_bias),
        lanes(position_bias),
        experts,
        head_dim,
    )
    steps = toks // ROWS
    seg = segments[0]
    seg_keys = jnp.stack([seg[i * ROWS : i * ROWS + span + ROWS] for i in range(steps)])[:, None]
    heads, probs, *packs = attend(
        rank_ref,
        after(qc, far_out),
        qp,
        key_vecs,
        value_vecs,
        rel_reverse,
        seg_keys,
        seg[mem_len:, None],
        ogate,
        head_dim,
    )

    piece = w_all.shape[0] // dp
    own_piece = lax.dynamic_slice_in_dim(w_all, at * piece, piece, 0)
    far_w = jnp.stack([swap(own_piece, "tensor", m) for m in others])
    even, odd = spread(far_out, packs[0], cots[1], far_w)
    blocks = (GROUP // 2, parts - 1) + own_block.shape
    even, odd = even.reshape(blocks), odd.reshape(blocks)
    depth = width // dp
    feed_piece = jnp.stack(
        [
            lax.dynamic_slice_in_dim(up_projection_weight, at * depth, depth, 0),
            lax.dynamic_slice_in_dim(down_projection_weight, at * (hidden // dp), hidden // dp, 0),
        ]
    )
    far_feed_near = swap(feed_piece, "tensor", far_shard)
    far_feed = lax.all_gather(after(far_feed_near, packs[0]), "dp", axis=0)
    packs = [packs[0]] + [swap(packs[m], "tensor", m) for m in others]
    group_at = at % GROUP
    where = jnp.stack([group_at // 2, group_at % 2, rank]).astype(jnp.int32)
    near_packs = swap(jnp.stack([packs[near], packs[near ^ far_shard]]), "tensor", near)
    full, middle, up_in = mix(
        where,
        packs,
        own_out,
        even,
        odd,
        tokens,
        row(second_gain),
        row(second_bias),
        experts,
        head_dim,
    )

    ups = [up_in, swap(up_in, "tensor", near)]
    unit = dp // GROUP
    where_grads = jnp.stack([at // unit, rank]).astype(jnp.int32)
    far_w = lax.all_gather(after(far_w, up_in), "dp", axis=0)
    shards = (up_projection_weight, down_projection_weight, far_feed)
    own_hidden, own_pre, own_result, own_up = feed(ups[0], cots[0], *shards, F32)
    near_hidden, near_pre, near_result, near_up = feed(ups[1], cots[1], *shards, BF16, own_pre)
    back_up = swap(near_up, "tensor", near)
    feed_sums = feed_weights(ups, cots, (own_pre, near_pre), (own_hidden, near_hidden))
    feed_sums = after(feed_sums, far_w, back_up)
    back_out = swap(near_result, "tensor", near)
    result = (middle + own_result + back_out.astype(F32)).astype(BF16)
    own_up = after(own_up, feed_sums)
    feed_sums = lax.psum_scatter(feed_sums, "dp", scatter_dimension=0, tiled=True)

    middle_grad, attn_grad, sums_two, *backs = mix_back(
        own_up, back_up, cotangent, middle, row(second_gain), full, packs, experts, head_dim
    )
    backs = [backs[0]] + [swap(backs[m], "tensor", m) for m in others]
    near_grad = swap(attn_grad, "tensor", near)

    key_grad, value_grad, query_grad, rel_grad, bias_sums, *grad_packs = attend_back(
        rank_ref,
        qc,
        qp,
        key_vecs,
        value_vecs,
        rel_reverse,
        probs,
        heads,
        ogate,
        every,
        vgate,
        backs,
        head_dim,
    )
    out_keep, out_send = out_weights(
        where_grads,
        [packs[0], packs[far_shard]],
        near_packs,
        attn_grad,
        after(near_grad, query_grad),
        experts,
        head_dim,
    )
    out_part = scatter_first(out_keep, swap(out_send, "dp", unit))
    rel_grad = after(rel_grad, *out_part)
    out_fars = scatter_sends(out_part, unit)
    grad_packs = [grad_packs[0]] + [swap(grad_packs[m], "tensor", m) for m in others]
    keep, send, small = weight_grads(
        where_grads,
        normed,
        key_grad,
        value_grad,
        vgate,
        query_grad,
        sin_table,
        rel_grad,
        w_all,
        row(first_gain),
        row(first_bias),
        sums_two,
        bias_sums,
        mem_len,
        head_dim,
        experts,
    )
    feed_own, feed_far = feed_sums[:, : 2 * hidden], feed_sums[:, 2 * hidden :]
    kept_far = swap(send, "dp", unit)
    small_far = swap(small, "dp", 1)
    feed_far = swap(after(feed_far, keep), "tensor", far_shard)
    tokens_grad = token_grads(
        rank_ref,
        grad_packs,
        w_all,
        after(far_w, keep, feed_own),
        tokens,
        middle_grad,
        row(first_gain),
        head_dim,
        experts,
    )
    kept_far, small_far, tokens_grad, *out_fars = together(
        kept_far, small_far, tokens_grad, *out_fars
    )
    kept = scatter_first(keep, kept_far)
    kept_fars = scatter_sends(kept, unit)
    small = small + small_far
    small_fars = [swap(small, "dp", m) for m in range(2, GROUP, 2)]
    out_sums = scatter_done(out_part[0], out_fars, unit, 1).reshape(2, experts * head_dim, -1)
    out_far = swap(out_sums[1].astype(BF16), "tensor", far_shard)
    feed_far, *fars = together(feed_far, *kept_fars, *small_fars)
    kept_fars, small_fars = fars[: len(fars) // 2], fars[len(fars) // 2 :]
    for far in small_fars:
        small = small + far
    mask = GROUP
    while mask < dp:
        small = small + swap(small, "dp", mask)
        mask *= 2
    small_fars = [swap(small, "tensor", m) for m in others]
    kept = scatter_done(kept[0], kept_fars, unit, 1)
    for far in small_fars:
        small = small + far
    out_w = out_sums[0] + out_far.astype(F32)
    feed_grads = feed_own.astype(F32) + feed_far.astype(F32)
    up_total = feed_grads[:, :hidden]
    down_total = feed_grads[:, hidden:].T
    biases = small[4:6, : parts * LANES].reshape(2, parts, LANES)[:, :, :head_dim]
    marks = [0, 1, 1 + experts, 2 + experts, 3 + experts]
    key_w, value_w, query_w, rel_w = (
        kept[a * head_dim : b * head_dim] for a, b in zip(marks, marks[1:])
    )
    select = marks[-1] * head_dim
    turn = lambda part: part.T[None]
    return (
        result,
        tokens_grad,
        small[0],
        small[1],
        small[2],
        small[3],
        turn(query_w),
        turn(key_w),
        turn(rel_w),
        turn(value_w),
        turn(kept[select : select + experts]),
        turn(kept[select + 8 : select + 8 + experts]),
        out_w[None],
        biases[0],
        biases[1],
        up_total,
        down_total,
    )


def solution(mesh):
    placed = (
        P("dp", None),
        P("dp", None, None),
        P("dp", None),
        P("dp", None, "tensor", None),
        P("dp", "tensor", None),
        P(),
        P(),
        P(),
        P(),
        P("tensor", None, None),
        P("tensor", None, None),
        P("tensor", None, None),
        P("tensor", None, None),
        P("tensor", None, None),
        P("tensor", None, None),
        P("tensor", None, None),
        P("tensor", None),
        P("tensor", None),
        P(None, "tensor"),
        P("tensor", None),
        P(("dp", "tensor"), None),
    )
    return jax.shard_map(
        on_device,
        mesh=mesh,
        in_specs=placed,
        out_specs=(
            P(("dp", "tensor"), None),
            P(("dp", "tensor"), None),
            P(),
            P(),
            P(),
            P(),
            P("tensor", "dp", None),
            P("tensor", "dp", None),
            P("tensor", "dp", None),
            P("tensor", "dp", None),
            P("tensor", "dp", None),
            P("tensor", "dp", None),
            P("tensor", None, "dp"),
            P(),
            P(),
            P("dp", "tensor"),
            P("tensor", "dp"),
        ),
        check_vma=False,
    )
```

```python
import functools
import math

import jax
import jax.numpy as jnp
from jax import lax
from jax.experimental import pallas as pl
from jax.experimental.pallas import tpu as pltpu
from jax.sharding import PartitionSpec as P

EPSILON = 1e-05
ROOT_HALF = 0.7071067811865476
INVERSE_ROOT_TAU = 0.3989422804014327
ROWS = 256
GROUP = 8
MIB = 1024 * 1024
BF16 = jnp.bfloat16
F32 = jnp.float32


def mm(left, right):
    return jnp.dot(left, right, preferred_element_type=F32)


def mm_nt(left, right):
    return lax.dot_general(left, right, (((1,), (1,)), ((), ())), preferred_element_type=F32)


def mm_tn(left, right):
    return lax.dot_general(left, right, (((0,), (0,)), ((), ())), preferred_element_type=F32)


def norm_parts(values):
    center = values - jnp.mean(values, axis=-1, keepdims=True)
    inv_std = lax.rsqrt(jnp.mean(center * center, axis=-1, keepdims=True) + EPSILON)
    return center * inv_std, inv_std


def norm_back(upstream, normal, inv_std, gain):
    scaled = upstream * gain
    return inv_std * (
        scaled
        - jnp.mean(scaled, axis=-1, keepdims=True)
        - normal * jnp.mean(scaled * normal, axis=-1, keepdims=True)
    )


def params():
    return pltpu.CompilerParams(vmem_limit_bytes=63 * MIB)


def cost(microseconds):
    return pl.CostEstimate(
        flops=int(microseconds * 1.15e9), bytes_accessed=MIB, transcendentals=0
    )


def struct(shape, dtype):
    return jax.ShapeDtypeStruct(shape, dtype)


def whole(*shape):
    return pl.BlockSpec(shape, lambda *_: (0,) * len(shape))

LANES = 128


def lane_of(rows):
    return lax.broadcasted_iota(jnp.int32, (rows, LANES), 1)


def picked(routes, head_dim):
    rows = routes.shape[1]
    routes = jnp.concatenate([routes, jnp.zeros((6, rows), jnp.int32)], axis=0).astype(F32).T
    lane = (lane_of(rows) - head_dim).astype(F32)
    return (lane == routes[:, 0:1]) | (lane == routes[:, 1:2])


def after(array, *deps):
    def body(*refs):
        del refs

    spec = pl.BlockSpec(memory_space=pl.ANY)
    return pl.pallas_call(
        body,
        in_specs=[spec] * (1 + len(deps)),
        out_specs=spec,
        out_shape=struct(array.shape, array.dtype),
        input_output_aliases={0: 0},
        name="after",
    )(array, *deps)


def together(*arrays):
    def body(*refs):
        del refs

    spec = pl.BlockSpec(memory_space=pl.ANY)
    return pl.pallas_call(
        body,
        in_specs=[spec] * len(arrays),
        out_specs=[spec] * len(arrays),
        out_shape=[struct(a.shape, a.dtype) for a in arrays],
        input_output_aliases={i: i for i in range(len(arrays))},
        name="together",
    )(*arrays)


def pile(*arrays):
    def body(*refs):
        for i, ref in enumerate(refs[:-1]):
            refs[-1][i] = ref[...]

    shape = arrays[0].shape
    return pl.pallas_call(
        body,
        in_specs=[whole(*shape)] * len(arrays),
        out_specs=whole(len(arrays), *shape),
        out_shape=struct((len(arrays),) + shape, arrays[0].dtype),
        grid=(1,),
        compiler_params=params(),
        cost_estimate=cost(2),
        name="pile",
    )(*arrays)


def project_kernel(
    experts,
    head_dim,
    mem_steps,
    scale,
    mem_ref,
    tok_ref,
    gain_ref,
    bias_ref,
    key_w_ref,
    vsel_ref,
    value_w_ref,
    query_w_ref,
    osel_ref,
    vroute_ref,
    oroute_ref,
    cb_ref,
    pb_ref,
    w_out_ref,
    normed_ref,
    key_ref,
    val_ref,
    every_ref,
    vgate_ref,
    qc_ref,
    qp_ref,
    ogate_ref,
    w_ref,
):
    step = pl.program_id(0)
    query = (1 + experts) * LANES

    @pl.when(step == 0)
    def _():
        w_ref[...] = jnp.zeros_like(w_ref)
        w_ref[:head_dim, :] = key_w_ref[...]
        w_ref[head_dim : head_dim + experts, :] = vsel_ref[...]
        for e in range(experts):
            w_ref[(1 + e) * LANES : (1 + e) * LANES + head_dim, :] = value_w_ref[
                e * head_dim : (e + 1) * head_dim, :
            ]
        w_ref[query : query + head_dim, :] = query_w_ref[...]
        w_ref[query + head_dim : query + head_dim + experts, :] = osel_ref[...]

    size = w_out_ref.shape[0]
    w_out_ref[...] = w_ref[pl.ds(pl.multiple_of(step * size, size), size), :]

    def rows_part(rows_ref, columns, last):
        blocks = [slice(i * ROWS, (i + 1) * ROWS) for i in range(rows_ref.shape[0] // ROWS)]
        normed, outs = [], []
        for rows in blocks:
            normal, _ = norm_parts(rows_ref[rows, :].astype(F32))
            normed.append((normal * gain_ref[...] + bias_ref[...]).astype(BF16))
            outs.append(mm_nt(normed[-1], w_ref[:columns, :]))
        lane = lane_of(ROWS)
        real = lane < head_dim
        for rows, norm, out in zip(blocks, normed, outs):
            normed_ref[rows, :] = norm
            first = out[:, :LANES]
            key_ref[rows, :] = jnp.where(real, first, 0.0).astype(BF16)
            every_ref[rows, :] = out[:, LANES:query].astype(BF16)
            gate = jnp.where(picked(vroute_ref[:, rows], head_dim), jax.nn.sigmoid(first), 0.0)
            vgate_ref[rows, :] = gate
            value = jnp.zeros((ROWS, LANES), F32)
            for e in range(experts):
                value = value + gate[:, head_dim + e : head_dim + e + 1] * (
                    out[:, (1 + e) * LANES : (2 + e) * LANES]
                )
            val_ref[rows, :] = value.astype(BF16)
            if last:
                q = out[:, query:]
                qc_ref[rows, :] = jnp.where(real, (q + cb_ref[...]) * scale, 0.0).astype(BF16)
                qp_ref[rows, :] = jnp.where(real, (q + pb_ref[...]) * scale, 0.0).astype(BF16)
                ogate_ref[rows, :] = jnp.where(
                    picked(oroute_ref[:, rows], head_dim), jax.nn.sigmoid(q), 0.0
                )

    @pl.when(step < mem_steps)
    def _():
        rows_part(mem_ref, query, False)

    @pl.when(step >= mem_steps)
    def _():
        rows_part(tok_ref, query + LANES, True)


def project(memory, tokens, gain, bias, weights, vroutes, oroutes, cb, pb, experts, head_dim):
    mem, width = memory.shape
    toks = tokens.shape[0]
    big = 2 * ROWS
    mem_steps, tok_steps = mem // big, toks // big
    steps = mem_steps + tok_steps
    keys = mem + toks
    cols = width
    mem_row = lambda i: (jnp.minimum(i, mem_steps - 1), 0)
    tok_row = lambda i: (jnp.maximum(i - mem_steps, 0), 0)
    row = lambda i: (i, 0)
    return pl.pallas_call(
        functools.partial(project_kernel, experts, head_dim, mem_steps, head_dim ** (-0.5)),
        grid=(steps,),
        in_specs=[
            pl.BlockSpec((big, width), mem_row),
            pl.BlockSpec((big, width), tok_row),
            whole(1, width),
            whole(1, width),
        ]
        + [whole(*w.shape) for w in weights]
        + [
            pl.BlockSpec((vroutes.shape[0], big), lambda i: (0, i)),
            pl.BlockSpec((oroutes.shape[0], big), lambda i: (0, jnp.maximum(i - mem_steps, 0))),
            whole(1, LANES),
            whole(1, LANES),
        ],
        out_specs=[
            pl.BlockSpec((cols // steps, width), row),
            pl.BlockSpec((big, width), row),
            pl.BlockSpec((big, LANES), row),
            pl.BlockSpec((big, LANES), row),
            pl.BlockSpec((big, experts * LANES), row),
            pl.BlockSpec((big, LANES), row),
            pl.BlockSpec((big, LANES), tok_row),
            pl.BlockSpec((big, LANES), tok_row),
            pl.BlockSpec((big, LANES), tok_row),
        ],
        out_shape=[
            struct((cols, width), BF16),
            struct((keys, width), BF16),
            struct((keys, LANES), BF16),
            struct((keys, LANES), BF16),
            struct((keys, experts * LANES), BF16),
            struct((keys, LANES), F32),
            struct((toks, LANES), BF16),
            struct((toks, LANES), BF16),
            struct((toks, LANES), F32),
        ],
        scratch_shapes=[pltpu.VMEM((cols, width), BF16)],
        compiler_params=params(),
        cost_estimate=cost(12),
        name="project",
    )(memory, tokens, gain, bias, *weights, vroutes, oroutes, cb, pb)


def attend_kernel(
    span,
    head_dim,
    count,
    z_ref,
    qc_ref,
    qp_ref,
    key_ref,
    val_ref,
    rel_ref,
    segk_ref,
    segq_ref,
    ogate_ref,
    heads_ref,
    probs_ref,
    *pack_refs,
):
    step = pl.program_id(0)
    wide = span + ROWS
    column = lax.broadcasted_iota(jnp.int32, (ROWS, ROWS), 1)
    causal = column <= lax.broadcasted_iota(jnp.int32, (ROWS, ROWS), 0)
    for b in range(count):
        rows = slice(b * ROWS, (b + 1) * ROWS)
        window = pl.ds((step * count + b) * ROWS, wide)
        content = mm_nt(qc_ref[rows, :], key_ref[window, :])
        reverse = mm_nt(qp_ref[rows, :], rel_ref[...])
        reverse = jnp.concatenate([reverse, jnp.zeros((ROWS, ROWS), F32)], axis=1)
        scores = content + pltpu.roll(reverse, 1, 1, stride=1, stride_axis=0)
        same = segk_ref[b] == segq_ref[rows, :]
        allowed = jnp.concatenate([same[:, :span], same[:, span:] & causal], axis=1)
        scores = jnp.where(allowed, scores, -1e30)
        expo = jnp.exp(scores - jnp.max(scores, axis=1, keepdims=True))
        probs = (expo * (1.0 / jnp.sum(expo, axis=1, keepdims=True))).astype(BF16)
        probs_ref[rows, :] = probs
        heads = mm(probs, val_ref[window, :])
        heads_ref[rows, :] = heads
        packed = jnp.where(lane_of(ROWS) < head_dim, heads, ogate_ref[rows, :]).astype(BF16)
        slot = (step * count + b) ^ z_ref[0]
        for m, pack_ref in enumerate(pack_refs):

            @pl.when(slot == m)
            def _():
                pack_ref[...] = packed


def attend(rank, qc, qp, key_vecs, value_vecs, rel_reverse, seg_keys, seg_query, ogate, head_dim):
    toks = qc.shape[0]
    keys = key_vecs.shape[0]
    span = rel_reverse.shape[0]
    steps = toks // ROWS
    count = 2
    big = count * ROWS
    wide = span + ROWS
    row = lambda i, z: (i, 0)
    return pl.pallas_call(
        functools.partial(attend_kernel, span, head_dim, count),
        grid_spec=pltpu.PrefetchScalarGridSpec(
            num_scalar_prefetch=1,
            grid=(steps // count,),
            in_specs=[
                pl.BlockSpec((big, LANES), row),
                pl.BlockSpec((big, LANES), row),
                whole(keys, LANES),
                whole(keys, LANES),
                whole(span, LANES),
                pl.BlockSpec((count, 1, wide), lambda i, z: (i, 0, 0)),
                pl.BlockSpec((big, 1), row),
                pl.BlockSpec((big, LANES), row),
            ],
            out_specs=[
                pl.BlockSpec((big, LANES), row),
                pl.BlockSpec((big, wide), row),
            ]
            + [whole(ROWS, LANES)] * steps,
        ),
        out_shape=[struct((toks, LANES), F32), struct((toks, wide), BF16)]
        + [struct((ROWS, LANES), BF16)] * steps,
        compiler_params=params(),
        cost_estimate=cost(8),
        name="attend",
    )(rank, qc, qp, key_vecs, value_vecs, rel_reverse, seg_keys, seg_query, ogate)


def attend_back_kernel(
    span,
    experts,
    head_dim,
    parts,
    z_ref,
    qc_ref,
    qp_ref,
    key_ref,
    val_ref,
    rel_ref,
    probs_ref,
    heads_ref,
    ogate_ref,
    every_ref,
    vgate_ref,
    *refs,
):
    back_refs, refs = refs[:parts], refs[parts:]
    key_grad_ref, value_grad_ref, query_grad_ref, rel_grad_ref, bias_ref = refs[:5]
    pack_refs, refs = refs[5 : 5 + parts // 2], refs[5 + parts // 2 :]
    keys_scr, values_scr, rel_scr, query_scr, back_scr = refs
    step = pl.program_id(0)
    steps = pl.num_programs(0)
    wide = span + ROWS
    mem = keys_scr.shape[0] - steps * ROWS
    scale = head_dim ** (-0.5)
    real = lane_of(ROWS) < head_dim

    @pl.when(step == 0)
    def _():
        keys_scr[...] = jnp.zeros_like(keys_scr)
        values_scr[...] = jnp.zeros_like(values_scr)
        rel_scr[...] = jnp.zeros_like(rel_scr)
        bias_ref[...] = jnp.zeros_like(bias_ref)

    slot = step ^ z_ref[0]
    for m, back_ref in enumerate(back_refs):

        @pl.when(slot == m)
        def _():
            back_scr[...] = back_ref[...]

    window = pl.ds(step * ROWS, wide)
    keys = key_ref[window, :]
    vals = val_ref[window, :]
    back = back_scr[...].astype(F32)
    out_grad = jnp.where(real, back, 0.0)
    delta = jnp.sum(out_grad * heads_ref[...], axis=1, keepdims=True)
    out_grad = out_grad.astype(BF16)
    probs = probs_ref[...]
    probs_grad = mm_nt(out_grad, vals)
    score_grad = (probs.astype(F32) * (probs_grad - delta)).astype(BF16)
    content_grad = mm(score_grad, keys).astype(BF16).astype(F32) * scale
    keys_scr[window, :] += mm_tn(score_grad, qc_ref[...])
    values_scr[window, :] += mm_tn(probs, out_grad)
    flip = (
        lax.broadcasted_iota(jnp.int32, (ROWS, ROWS), 0)
        + lax.broadcasted_iota(jnp.int32, (ROWS, ROWS), 1)
        == ROWS - 1
    ).astype(BF16)
    turned = mm(flip, score_grad)
    turned = pltpu.roll(turned, span, 1, stride=1, stride_axis=0)[:, :span].astype(BF16)
    place_grad = mm(turned, rel_ref[...]).astype(BF16)
    position_grad = mm(flip, place_grad) * scale
    rel_scr[...] += mm_tn(turned, mm(flip, qp_ref[...]).astype(BF16))
    bias_ref[0:1, :] += jnp.sum(content_grad, axis=0, keepdims=True)
    bias_ref[1:2, :] += jnp.sum(position_grad, axis=0, keepdims=True)
    gate = ogate_ref[...]
    query_grad = jnp.where(real, content_grad + position_grad, back * gate * (1.0 - gate))
    query_grad = query_grad.astype(BF16)
    query_grad_ref[...] = query_grad
    query_scr[pl.ds(step * ROWS, ROWS), :] = query_grad

    @pl.when(step == steps - 1)
    def _():
        rel_grad_ref[...] = rel_scr[...].astype(BF16)

        @pl.loop(0, (mem + steps * ROWS) // ROWS)
        def _(block):
            rows = pl.ds(block * ROWS, ROWS)
            value_grad = values_scr[rows, :]
            gates = vgate_ref[rows, :]
            value_grad_ref[rows, :] = value_grad
            logit = keys_scr[rows, :]
            lane = lane_of(ROWS)
            for e in range(experts):
                part = every_ref[rows, e * LANES : (e + 1) * LANES].astype(F32)
                total = jnp.sum(value_grad * part, axis=1, keepdims=True)
                logit = jnp.where(lane == head_dim + e, total, logit)
            key_grad = jnp.where(real, logit, logit * gates * (1.0 - gates)).astype(BF16)
            key_grad_ref[rows, :] = key_grad

            @pl.when(block * ROWS >= mem)
            def _():
                place = block - mem // ROWS
                slot = place ^ z_ref[0]
                value_pack = jnp.where(real, value_grad, gates).astype(BF16)
                for side, pack_ref in enumerate(pack_refs):

                    @pl.when(slot // 2 == side)
                    def _():
                        pack_ref[slot % 2, 0] = key_grad
                        pack_ref[slot % 2, 1] = value_pack
                        pack_ref[slot % 2, 2] = query_scr[pl.ds(place * ROWS, ROWS), :]


def attend_back(
    rank,
    qc,
    qp,
    key_vecs,
    value_vecs,
    rel_reverse,
    probs,
    heads,
    ogate,
    every,
    vgate,
    backs,
    head_dim,
):
    toks = qc.shape[0]
    keys = key_vecs.shape[0]
    span = rel_reverse.shape[0]
    steps = toks // ROWS
    wide = span + ROWS
    experts = every.shape[1] // LANES
    row = lambda i, z: (i, 0)
    return pl.pallas_call(
        functools.partial(attend_back_kernel, span, experts, head_dim, steps),
        grid_spec=pltpu.PrefetchScalarGridSpec(
            num_scalar_prefetch=1,
            grid=(steps,),
            in_specs=[
                pl.BlockSpec((ROWS, LANES), row),
                pl.BlockSpec((ROWS, LANES), row),
                whole(keys, LANES),
                whole(keys, LANES),
                whole(span, LANES),
                pl.BlockSpec((ROWS, wide), row),
                pl.BlockSpec((ROWS, LANES), row),
                pl.BlockSpec((ROWS, LANES), row),
                whole(keys, experts * LANES),
                whole(keys, LANES),
            ]
            + [whole(ROWS, LANES)] * steps,
            out_specs=[
                whole(keys, LANES),
                whole(keys, LANES),
                pl.BlockSpec((ROWS, LANES), row),
                whole(span, LANES),
                whole(2, LANES),
            ]
            + [whole(2, 3, ROWS, LANES)] * (steps // 2),
            scratch_shapes=[
                pltpu.VMEM((keys, LANES), F32),
                pltpu.VMEM((keys, LANES), F32),
                pltpu.VMEM((span, LANES), F32),
                pltpu.VMEM((toks, LANES), BF16),
                pltpu.VMEM((ROWS, LANES), BF16),
            ],
        ),
        out_shape=[
            struct((keys, LANES), BF16),
            struct((keys, LANES), F32),
            struct((toks, LANES), BF16),
            struct((span, LANES), BF16),
            struct((2, LANES), F32),
        ]
        + [struct((2, 3, ROWS, LANES), BF16)] * (steps // 2),
        compiler_params=params(),
        cost_estimate=cost(15),
        name="attend_back",
    )(rank, qc, qp, key_vecs, value_vecs, rel_reverse, probs, heads, ogate, every, vgate, *backs)


def mix_kernel(experts, head_dim, heads, where_ref, *refs):
    pack_refs, refs = refs[:heads], refs[heads:]
    own_ref, even_ref, odd_ref, tok_ref, gain_ref, bias_ref = refs[:6]
    full_ref, middle_ref, up_ref, mixed_scr, attn_scr = refs[6:]
    step = pl.program_id(0)
    steps = pl.num_programs(0)

    @pl.when(step == 0)
    def _():
        real = lane_of(ROWS) < head_dim
        for m in range(heads):
            pack = pack_refs[m][...].astype(F32)
            out = jnp.where(real, pack, 0.0)
            for e in range(experts):
                gate = pack[:, head_dim + e : head_dim + e + 1]
                mixed_scr[m, :, e * LANES : (e + 1) * LANES] = (gate * out).astype(BF16)

    turned = where_ref[1] == 1
    total = None
    for m in range(heads):
        if m == 0:
            weight = own_ref[...]
        else:
            even, odd = even_ref[0, m - 1], odd_ref[0, m - 1]
            weight = jnp.concatenate(
                [jnp.where(turned, odd, even), jnp.where(turned, even, odd)], axis=1
            )
        for e in range(experts):
            full_ref[m, e * LANES : e * LANES + head_dim, :] = weight[
                e * head_dim : (e + 1) * head_dim
            ]
            full_ref[m, e * LANES + head_dim : (e + 1) * LANES, :] = jnp.zeros(
                (LANES - head_dim, weight.shape[1]), BF16
            )
        part = mm(mixed_scr[m], full_ref[m])
        total = part if total is None else total + part
    block = where_ref[0] ^ step
    size = total.shape[1]
    attn_scr[:, pl.ds(pl.multiple_of(block * size, size), size)] = total

    @pl.when(step == steps - 1)
    def _():
        middle = tok_ref[...].astype(F32) + attn_scr[...]
        middle_ref[...] = middle
        normal, _ = norm_parts(middle)
        up_ref[...] = (normal * gain_ref[...] + bias_ref[...]).astype(BF16)


def mix(where, packs, own_weight, even, odd, tokens, gain, bias, experts, head_dim):
    heads = len(packs)
    rows = packs[0].shape[0]
    depth, width = own_weight.shape
    steps = even.shape[0]
    size = width // steps
    return pl.pallas_call(
        functools.partial(mix_kernel, experts, head_dim, heads),
        grid_spec=pltpu.PrefetchScalarGridSpec(
            num_scalar_prefetch=1,
            grid=(steps,),
            in_specs=[whole(rows, LANES)] * heads
            + [
                pl.BlockSpec((depth, size), lambda s, w: (0, w[0] ^ s)),
                pl.BlockSpec((1,) + even.shape[1:], lambda s, w: (s, 0, 0, 0)),
                pl.BlockSpec((1,) + odd.shape[1:], lambda s, w: (s, 0, 0, 0)),
                pl.BlockSpec((rows, width), lambda s, w: (w[2], 0)),
                whole(1, width),
                whole(1, width),
            ],
            out_specs=[
                pl.BlockSpec((heads, experts * LANES, size), lambda s, w: (0, 0, w[0] ^ s)),
                whole(rows, width),
                whole(rows, width),
            ],
            scratch_shapes=[
                pltpu.VMEM((heads, rows, experts * LANES), BF16),
                pltpu.VMEM((rows, width), F32),
            ],
        ),
        out_shape=[
            struct((heads, experts * LANES, width), BF16),
            struct((rows, width), F32),
            struct((rows, width), BF16),
        ],
        compiler_params=params(),
        cost_estimate=cost(9),
        name="mix",
    )(where, *packs, own_weight, even, odd, tokens, gain, bias)


def mix_back_kernel(experts, head_dim, heads, *refs):
    grad0_ref, grad1_ref, cot_ref, middle_ref, gain_ref, full_ref = refs[:6]
    pack_refs, refs = refs[6 : 6 + heads], refs[6 + heads :]
    middle_grad_ref, attn_grad_ref, sums_ref = refs[:3]
    back_refs = refs[3 : 3 + heads]
    step = pl.program_id(0)

    @pl.when(step == 0)
    def _():
        upstream = grad0_ref[...].astype(F32) + grad1_ref[...].astype(F32)
        normal, inv_std = norm_parts(middle_ref[...])
        sums_ref[0:1, :] = jnp.sum(upstream * normal, axis=0, keepdims=True)
        sums_ref[1:2, :] = jnp.sum(upstream, axis=0, keepdims=True)
        grad = cot_ref[...].astype(F32) + norm_back(upstream, normal, inv_std, gain_ref[...])
        middle_grad_ref[...] = grad
        attn_grad_ref[...] = grad.astype(BF16)

    mixed_grad = mm_nt(attn_grad_ref[...], full_ref[0]).astype(BF16).astype(F32)
    lane = lane_of(ROWS)
    real = lane < head_dim
    for m in range(heads):

        @pl.when(step == m)
        def _():
            pack = pack_refs[m][...].astype(F32)
            total = jnp.zeros((ROWS, LANES), F32)
            gates = jnp.zeros((ROWS, LANES), F32)
            for e in range(experts):
                part = mixed_grad[:, e * LANES : (e + 1) * LANES]
                total = total + pack[:, head_dim + e : head_dim + e + 1] * part
                inner = jnp.sum(part * pack, axis=1, keepdims=True)
                gates = jnp.where(lane == head_dim + e, inner, gates)
            back_refs[m][...] = jnp.where(real, total, gates).astype(BF16)


def mix_back(own_grad, far_grad, cot, middle, gain, full, packs, experts, head_dim):
    heads, depth, width = full.shape
    rows = middle.shape[0]
    return pl.pallas_call(
        functools.partial(mix_back_kernel, experts, head_dim, heads),
        grid=(heads,),
        in_specs=[whole(rows, width)] * 4
        + [whole(1, width), pl.BlockSpec((1, depth, width), lambda m: (m, 0, 0))]
        + [whole(rows, LANES)] * heads,
        out_specs=[whole(rows, width), whole(rows, width), whole(2, width)]
        + [whole(rows, LANES)] * heads,
        out_shape=[
            struct((rows, width), F32),
            struct((rows, width), BF16),
            struct((2, width), F32),
        ]
        + [struct((rows, LANES), BF16)] * heads,
        compiler_params=params(),
        cost_estimate=cost(10),
        name="mix_back",
    )(own_grad, far_grad, cot, middle, gain, full, *packs)


def feed_kernel(half, up_ref, cot_ref, wu_ref, wd_ref, far_u_ref, far_d_ref, *refs):
    refs = refs[-6:]
    hidden_ref, pre_grad_ref, out_ref, up_grad_ref, out_scr, up_scr = refs
    step = pl.program_id(0)
    steps = pl.num_programs(0)
    width = up_ref.shape[1]
    count = wu_ref.shape[1] // ROWS

    @pl.when(step == 0)
    def _():
        out_scr[...] = jnp.zeros_like(out_scr)
        up_scr[...] = jnp.zeros_like(up_scr)

    def part(w_up, w_down):
        pres, grads = [], []
        for b in range(count):
            cols = slice(b * ROWS, (b + 1) * ROWS)
            pres.append(mm(up_ref[...], w_up[:, cols]))
            grads.append(mm_nt(cot_ref[...], w_down[cols, :]))
        out, up_grad = None, None
        for b in range(count):
            cols = slice(b * ROWS, (b + 1) * ROWS)
            pre = pres[b]
            hidden_grad = grads[b].astype(BF16).astype(F32)
            phi = 0.5 * (1.0 + lax.erf(pre * ROOT_HALF))
            hidden = (pre * phi).astype(BF16)
            slope = phi + pre * jnp.exp(-0.5 * pre * pre) * INVERSE_ROOT_TAU
            pre_grad = (hidden_grad * slope).astype(BF16)
            hidden_ref[:, cols] = hidden
            pre_grad_ref[:, cols] = pre_grad
            out_part, up_part = mm(hidden, w_down[cols, :]), mm_nt(pre_grad, w_up[:, cols])
            out = out_part if out is None else out + out_part
            up_grad = up_part if up_grad is None else up_grad + up_part
        out_scr[...] += out
        up_scr[...] += up_grad

    @pl.when(step < half)
    def _():
        part(wu_ref[...], wd_ref[...])

    @pl.when(step >= half)
    def _():
        part(far_u_ref[...].reshape(width, -1), far_d_ref[...].reshape(-1, width))

    @pl.when(step == steps - 1)
    def _():
        out_ref[...] = out_scr[...].astype(out_ref.dtype)
        up_grad_ref[...] = up_scr[...].astype(up_grad_ref.dtype)


def feed(up_in, cot, w_up, w_down, far, dtype, *deps):
    rows, width = up_in.shape
    hidden = w_up.shape[1]
    size = 2 * ROWS
    half = hidden // size
    pieces, _, depth, _ = far.shape
    count = size // depth
    own = lambda i: jnp.minimum(i, half - 1)
    other = lambda i: jnp.maximum(i - half, 0)
    return pl.pallas_call(
        functools.partial(feed_kernel, half),
        grid=(2 * half,),
        in_specs=[
            whole(rows, width),
            whole(rows, width),
            pl.BlockSpec((width, size), lambda i: (0, own(i))),
            pl.BlockSpec((size, width), lambda i: (own(i), 0)),
            pl.BlockSpec((pieces, 1, depth, size), lambda i: (0, 0, 0, other(i))),
            pl.BlockSpec((count, 1, depth, width), lambda i: (other(i), 1, 0, 0)),
        ]
        + [pl.BlockSpec(memory_space=pl.ANY)] * len(deps),
        out_specs=[
            pl.BlockSpec((rows, size), lambda i: (0, i)),
            pl.BlockSpec((rows, size), lambda i: (0, i)),
            whole(rows, width),
            whole(rows, width),
        ],
        out_shape=[
            struct((rows, 2 * hidden), BF16),
            struct((rows, 2 * hidden), BF16),
            struct((rows, width), dtype),
            struct((rows, width), dtype),
        ],
        scratch_shapes=[pltpu.VMEM((rows, width), F32), pltpu.VMEM((rows, width), F32)],
        compiler_params=params(),
        cost_estimate=cost(10),
        name="feed",
    )(up_in, cot, w_up, w_down, far, far, *deps)


def feed_weights_kernel(count, half, *refs):
    lefts, refs = refs[: 2 * count], refs[2 * count :]
    rights, out_ref = refs[: 2 * count], refs[2 * count]
    step = pl.program_id(0)

    for which in range(2):

        @pl.when((step // half) % 2 == which)
        def _():
            total = None
            for m in range(which * count, (which + 1) * count):
                part = mm_tn(lefts[m][...], rights[m][...])
                total = part if total is None else total + part
            out_ref[...] = total.astype(BF16)


def feed_weights(ups, cots, pre_grads, hiddens):
    count = len(ups)
    rows, width = ups[0].shape
    hidden = hiddens[0].shape[1] // 2
    size = 512
    half = hidden // size

    def columns(which):
        def at(i):
            shard, inner = i // (2 * half), i % (2 * half)
            return (0, shard * half + jnp.clip(inner - which * half, 0, half - 1))

        return pl.BlockSpec((rows, size), at)

    return pl.pallas_call(
        functools.partial(feed_weights_kernel, count, half),
        grid=(4 * half,),
        in_specs=[whole(rows, width)] * (2 * count)
        + [columns(0)] * count
        + [columns(1)] * count,
        out_specs=pl.BlockSpec((width, size), lambda i: (0, i)),
        out_shape=struct((width, 4 * hidden), BF16),
        compiler_params=params(),
        cost_estimate=cost(11),
        name="feed_weights",
    )(*ups, *cots, *pre_grads, *hiddens)


def out_weights_kernel(experts, head_dim, heads, where_ref, *refs):
    own_refs, near_ref = refs[:heads], refs[heads]
    grad_ref, near_grad_ref, keep_ref, send_ref, mixed_scr, scr = refs[heads + 1 :]
    real = lane_of(ROWS) < head_dim

    def fill(begin, pack):
        pack = pack.astype(F32)
        out = jnp.where(real, pack, 0.0)
        for e in range(experts):
            gate = pack[:, head_dim + e : head_dim + e + 1]
            mixed_scr[begin : begin + ROWS, e * LANES : (e + 1) * LANES] = (gate * out).astype(
                BF16
            )

    for m in range(heads):

        @pl.when(pl.program_id(0) == m)
        def _():
            fill(0, own_refs[m][...])
            fill(ROWS, near_ref[m])

    scr[...] = mm_tn(mixed_scr[:ROWS], grad_ref[...]) + mm_tn(
        mixed_scr[ROWS:], near_grad_ref[...]
    )
    for k in range(GROUP):
        target = send_ref if k % 2 else keep_ref
        lanes = pl.ds(pl.multiple_of((where_ref[0] ^ k) * LANES, LANES), LANES)
        for e in range(experts):
            target[k // 2, e * head_dim : (e + 1) * head_dim, :] = scr[
                e * LANES : e * LANES + head_dim, lanes
            ].astype(BF16)


def out_weights(where, own_packs, near_packs, grad, near_grad, experts, head_dim):
    heads = len(own_packs)
    rows, width = grad.shape
    depth = experts * head_dim
    shape = (GROUP // 2, heads * depth, width // GROUP)
    spec = pl.BlockSpec((GROUP // 2, depth, width // GROUP), lambda m, w: (0, m, 0))
    return pl.pallas_call(
        functools.partial(out_weights_kernel, experts, head_dim, heads),
        grid_spec=pltpu.PrefetchScalarGridSpec(
            num_scalar_prefetch=1,
            grid=(heads,),
            in_specs=[whole(rows, LANES)] * heads
            + [whole(*near_packs.shape)]
            + [whole(rows, width)] * 2,
            out_specs=[spec] * 2,
            scratch_shapes=[
                pltpu.VMEM((2 * rows, experts * LANES), BF16),
                pltpu.VMEM((experts * LANES, width), F32),
            ],
        ),
        out_shape=[struct(shape, BF16)] * 2,
        compiler_params=params(),
        cost_estimate=cost(5),
        name="out_weights",
    )(where, *own_packs, near_packs, grad, near_grad)


def weights_kernel(
    experts,
    head_dim,
    counts,
    where_ref,
    normed_ref,
    key_ref,
    value_ref,
    gate_ref,
    query_ref,
    table_ref,
    rel_ref,
    w_ref,
    gain_ref,
    bias_ref,
    sums_ref,
    biases_ref,
    keep_ref,
    send_ref,
    small_ref,
    grads_scr,
    sum_scr,
    main_scr,
    rel_scr,
):
    step = pl.program_id(0)
    mem_steps, key_steps, rel_steps = counts
    query = (1 + experts) * LANES

    @pl.when(step == 0)
    def _():
        main_scr[...] = jnp.zeros_like(main_scr)
        sum_scr[...] = jnp.zeros_like(sum_scr)
        rel_scr[...] = jnp.zeros_like(rel_scr)

    def add(columns):
        grads = grads_scr[:, :columns]
        main_scr[:columns, :] += mm_tn(grads, normed_ref[...])
        sum_scr[:columns, :] += mm_tn(grads, jnp.ones((grads.shape[0], LANES), BF16))

    @pl.when(step < key_steps)
    def _():
        value_grad = value_ref[...]
        grads_scr[:, :LANES] = key_ref[...]
        for e in range(experts):
            gate = gate_ref[:, head_dim + e : head_dim + e + 1]
            grads_scr[:, LANES * (1 + e) : LANES * (2 + e)] = (gate * value_grad).astype(BF16)

    @pl.when(step < mem_steps)
    def _():
        add(query)

    @pl.when((step >= mem_steps) & (step < key_steps))
    def _():
        grads_scr[:, query:] = query_ref[...]
        add(query + LANES)

    @pl.when(step >= key_steps)
    def _():
        rel_scr[...] += mm_tn(rel_ref[...], table_ref[...])

    @pl.when(step == key_steps + rel_steps - 1)
    def _():
        weights = w_ref[...].astype(F32)
        bias_one = jnp.sum(weights * sum_scr[:, 0:1], axis=0, keepdims=True)
        inner = jnp.sum(weights * main_scr[...], axis=0, keepdims=True)
        small_ref[...] = jnp.zeros_like(small_ref)
        small_ref[0:1, :] = (inner - bias_ref[...] * bias_one) / gain_ref[...]
        small_ref[1:2, :] = bias_one
        small_ref[2:4, :] = sums_ref[...]
        small_ref[4:6, pl.ds(pl.multiple_of(where_ref[1] * LANES, LANES), LANES)] = biases_ref[...]
        for k in range(GROUP):
            target = send_ref if k % 2 else keep_ref
            at = k // 2
            lanes = pl.ds(pl.multiple_of((where_ref[0] ^ k) * LANES, LANES), LANES)
            row = 0

            def put(source, begin, size):
                target[at, row : row + size, :] = source[begin : begin + size, lanes].astype(BF16)
                return row + size

            for section in range(2 + experts):
                row = put(main_scr, section * LANES, head_dim)
            row = put(rel_scr, 0, head_dim)
            target[at, row:, :] = jnp.concatenate(
                [
                    main_scr[head_dim : head_dim + 8, lanes],
                    main_scr[query + head_dim : query + head_dim + 8, lanes],
                ],
                axis=0,
            ).astype(BF16)


def weight_grads(
    where,
    normed,
    key_grad,
    value_grad,
    gates,
    query_grad,
    table,
    rel_grad,
    w_all,
    gain,
    bias,
    sums_two,
    bias_sums,
    mem,
    head_dim,
    experts,
):
    keys, width = normed.shape
    cols = (2 + experts) * LANES
    big = 2 * ROWS
    mem_steps, key_steps = mem // big, keys // big
    rel_steps = table.shape[0] // big
    counts = (mem_steps, key_steps, rel_steps)
    rows = (3 + experts) * head_dim + 16
    key_row = lambda i, w: (jnp.minimum(i, key_steps - 1), 0)
    tok_row = lambda i, w: (jnp.clip(i - mem_steps, 0, key_steps - mem_steps - 1), 0)
    rel_row = lambda i, w: (jnp.clip(i - key_steps, 0, rel_steps - 1), 0)
    half = GROUP // 2
    return pl.pallas_call(
        functools.partial(weights_kernel, experts, head_dim, counts),
        grid_spec=pltpu.PrefetchScalarGridSpec(
            num_scalar_prefetch=1,
            grid=(key_steps + rel_steps,),
            in_specs=[
                pl.BlockSpec((big, width), key_row),
                pl.BlockSpec((big, LANES), key_row),
                pl.BlockSpec((big, LANES), key_row),
                pl.BlockSpec((big, LANES), key_row),
                pl.BlockSpec((big, LANES), tok_row),
                pl.BlockSpec((big, width), rel_row),
                pl.BlockSpec((big, LANES), rel_row),
                whole(cols, width),
                whole(1, width),
                whole(1, width),
                whole(2, width),
                whole(2, LANES),
            ],
            out_specs=[
                whole(half, rows, LANES),
                whole(half, rows, LANES),
                whole(8, width),
            ],
            scratch_shapes=[
                pltpu.VMEM((big, cols), BF16),
                pltpu.VMEM((cols, LANES), F32),
                pltpu.VMEM((cols, width), F32),
                pltpu.VMEM((LANES, width), F32),
            ],
        ),
        out_shape=[
            struct((half, rows, LANES), BF16),
            struct((half, rows, LANES), BF16),
            struct((8, width), F32),
        ],
        compiler_params=params(),
        cost_estimate=cost(15),
        name="weight_grads",
    )(
        where,
        normed,
        key_grad,
        value_grad,
        gates,
        query_grad,
        table,
        rel_grad,
        w_all,
        gain,
        bias,
        sums_two,
        bias_sums,
    )


def token_kernel(experts, head_dim, own_ref, far_ref, w_own_ref, w_far_ref, *refs):
    out_refs, grads_scr, total_scr = refs[:2], refs[2], refs[3]
    step = pl.program_id(0)
    query = (1 + experts) * LANES
    cols = query + LANES
    real = lane_of(ROWS) < head_dim

    def part(pack_ref, weights):
        for block in range(2):
            rows = slice(block * ROWS, (block + 1) * ROWS)
            value_pack = pack_ref[block, 1].astype(F32)
            value_grad = jnp.where(real, value_pack, 0.0)
            grads_scr[rows, :LANES] = pack_ref[block, 0]
            for e in range(experts):
                gate = value_pack[:, head_dim + e : head_dim + e + 1]
                grads_scr[rows, LANES * (1 + e) : LANES * (2 + e)] = (gate * value_grad).astype(
                    BF16
                )
            grads_scr[rows, query:] = pack_ref[block, 2]
        return mm(grads_scr[...], weights)

    @pl.when(step == 0)
    def _():
        total_scr[...] = part(own_ref, w_own_ref[:cols, :])

    @pl.when(step == 1)
    def _():
        weights = w_far_ref[...].reshape(-1, w_far_ref.shape[2])
        total = total_scr[...] + part(far_ref, weights[:cols, :])
        out_refs[0][...] = total[:ROWS]
        out_refs[1][...] = total[ROWS:].astype(BF16)


def token_parts(own_pack, far_pack, own_w, far_w, head_dim, experts):
    width = own_w.shape[1]
    rows = 2 * ROWS
    cols = (2 + experts) * LANES
    return pl.pallas_call(
        functools.partial(token_kernel, experts, head_dim),
        grid=(2,),
        in_specs=[
            whole(*own_pack.shape),
            whole(*far_pack.shape),
            whole(*own_w.shape),
            whole(*far_w.shape),
        ],
        out_specs=[whole(ROWS, width)] * 2,
        out_shape=[struct((ROWS, width), F32), struct((ROWS, width), BF16)],
        scratch_shapes=[pltpu.VMEM((rows, cols), BF16), pltpu.VMEM((rows, width), F32)],
        compiler_params=params(),
        cost_estimate=cost(6),
        name="token_parts",
    )(own_pack, far_pack, own_w, far_w)


def token_sum_kernel(z_ref, tok_ref, mid_ref, gain_ref, own_ref, near_ref, out_ref):
    total = own_ref[...] + near_ref[...].astype(F32)
    normal, inv_std = norm_parts(tok_ref[...].astype(F32))
    out_ref[...] = mid_ref[...] + norm_back(total, normal, inv_std, gain_ref[...])


def token_sum(rank, tokens, middle_grad, gain, own, near):
    rows, width = middle_grad.shape
    return pl.pallas_call(
        token_sum_kernel,
        grid_spec=pltpu.PrefetchScalarGridSpec(
            num_scalar_prefetch=1,
            grid=(1,),
            in_specs=[
                pl.BlockSpec((rows, width), lambda i, z: (z[0], 0)),
                whole(rows, width),
                whole(1, width),
                whole(rows, width),
                whole(rows, width),
            ],
            out_specs=whole(rows, width),
        ),
        out_shape=struct((rows, width), F32),
        compiler_params=params(),
        cost_estimate=cost(4),
        name="token_sum",
    )(rank, tokens, middle_grad, gain, own, near)


def swap(array, axis, mask):
    size = lax.axis_size(axis)
    return lax.ppermute(array, axis, [(i, i ^ mask) for i in range(size)])


def plus(left, right):
    return (left.astype(F32) + right.astype(F32)).astype(BF16)


def scatter_first(keep, far):
    return [plus(keep[m], far[m]) for m in range(keep.shape[0])]


def scatter_sends(blocks, unit):
    return [swap(blocks[m], "dp", 2 * m * unit) for m in range(1, len(blocks))]


def scatter_done(own, fars, unit, axis):
    out = own.astype(F32)
    for far in fars:
        out = out + far.astype(F32)
    mask = unit // 2
    while mask:
        size = out.shape[axis] // 2
        bit = (lax.axis_index("dp") // mask) % 2
        mine = lax.dynamic_slice_in_dim(out, bit * size, size, axis)
        theirs = lax.dynamic_slice_in_dim(out, (1 - bit) * size, size, axis)
        out = mine + swap(theirs.astype(BF16), "dp", mask).astype(F32)
        mask //= 2
    return out


def spread(far, *gates):
    pieces = [swap(far, "dp", 2 * m) for m in range(1, GROUP // 2)]
    even = after(pile(far, *pieces), *gates)
    odd = swap(even, "dp", 1)
    return even, odd


def on_device(
    tokens,
    memory,
    segments,
    value_routes,
    output_routes,
    first_gain,
    first_bias,
    second_gain,
    second_bias,
    query_head_weight,
    key_weight,
    position_weight,
    value_weight,
    value_select,
    output_expert_selector,
    output_expert_weight,
    content_bias,
    position_bias,
    up_projection_weight,
    down_projection_weight,
    cotangent,
):
    mem_len = memory.shape[1]
    toks, width = tokens.shape
    head_dim = query_head_weight.shape[2]
    experts = value_select.shape[2]
    hidden = up_projection_weight.shape[1]
    parts = lax.axis_size("tensor")
    rank = lax.axis_index("tensor")
    dp = lax.axis_size("dp")
    at = lax.axis_index("dp")
    others = range(1, parts)
    near, far_shard = 1, 2
    rank_ref = rank.reshape(1).astype(jnp.int32)
    row = lambda v: v.reshape(1, -1)
    lanes = lambda v: jnp.pad(v, ((0, 0), (0, LANES - head_dim)))

    own_out = output_expert_weight[0]
    size = width // GROUP
    own_block = lax.dynamic_slice_in_dim(own_out, (at % GROUP) * size, size, 1)
    far_out = pile(*[swap(own_block, "tensor", m) for m in others]).reshape(-1, size)
    cots = [cotangent, swap(cotangent, "tensor", near)]
    span = mem_len
    fine = 32
    rates = jnp.exp(jnp.arange(width // 2).astype(F32) * (-2.0 * math.log(10000.0) / width))
    coarse_at = (span - 1 - fine * jnp.arange(span // fine)).astype(F32)[:, None] * rates[None, :]
    fine_at = jnp.arange(fine).astype(F32)[:, None] * rates[None, :]
    sin_a, cos_a = jnp.sin(coarse_at)[:, None, :], jnp.cos(coarse_at)[:, None, :]
    sin_b, cos_b = jnp.sin(fine_at)[None, :, :], jnp.cos(fine_at)[None, :, :]
    sin_table = jnp.concatenate(
        [sin_a * cos_b - cos_a * sin_b, cos_a * cos_b + sin_a * sin_b], axis=2
    )
    sin_table = lax.optimization_barrier(sin_table.reshape(span, width).astype(BF16))
    rel_weight = jnp.concatenate(
        [position_weight[0].T, jnp.zeros((LANES - head_dim, width), BF16)]
    )
    rel_reverse = mm_nt(sin_table, rel_weight).astype(BF16)

    w_all, normed, key_vecs, value_vecs, every, vgate, qc, qp, ogate = project(
        memory[0],
        tokens,
        row(first_gain),
        row(first_bias),
        (
            key_weight[0].T,
            value_select[0].T,
            value_weight[0].T,
            query_head_weight[0].T,
            output_expert_selector[0].T,
        ),
        value_routes[0, :, 0].T,
        output_routes[:, 0].T,
        lanes(content_bias),
        lanes(position_bias),
        experts,
        head_dim,
    )
    steps = toks // ROWS
    seg = segments[0]
    seg_keys = jnp.stack([seg[i * ROWS : i * ROWS + span + ROWS] for i in range(steps)])[:, None]
    heads, probs, *packs = attend(
        rank_ref,
        qc,
        qp,
        key_vecs,
        value_vecs,
        rel_reverse,
        seg_keys,
        seg[mem_len:, None],
        ogate,
        head_dim,
    )

    piece = w_all.shape[0] // dp
    own_piece = lax.dynamic_slice_in_dim(w_all, at * piece, piece, 0)
    far_w = swap(own_piece, "tensor", far_shard)
    even, odd = spread(after(far_out, qc), packs[0], cots[1], far_w)
    blocks = (GROUP // 2, parts - 1) + own_block.shape
    even, odd = even.reshape(blocks), odd.reshape(blocks)
    depth = width // dp
    feed_piece = jnp.stack(
        [
            lax.dynamic_slice_in_dim(up_projection_weight, at * depth, depth, 0),
            lax.dynamic_slice_in_dim(down_projection_weight, at * (hidden // dp), hidden // dp, 0),
        ]
    )
    far_feed_near = swap(feed_piece, "tensor", far_shard)
    far_feed = lax.all_gather(after(far_feed_near, qc, far_out, rel_reverse), "dp", axis=0)
    packs = [packs[0]] + [swap(packs[m], "tensor", m) for m in others]
    group_at = at % GROUP
    where = jnp.stack([group_at // 2, group_at % 2, rank]).astype(jnp.int32)
    near_packs = swap(jnp.stack([packs[near], packs[near ^ far_shard]]), "tensor", near)
    full, middle, up_in = mix(
        where,
        packs,
        own_out,
        even,
        odd,
        tokens,
        row(second_gain),
        row(second_bias),
        experts,
        head_dim,
    )

    ups = [up_in, swap(up_in, "tensor", near)]
    unit = dp // GROUP
    where_grads = jnp.stack([at // unit, rank]).astype(jnp.int32)
    far_w = lax.all_gather(after(far_w, up_in), "dp", axis=0)
    shards = (up_projection_weight, down_projection_weight, far_feed)
    own_hidden, own_pre, own_result, own_up = feed(ups[0], cots[0], *shards, F32)
    near_hidden, near_pre, near_result, near_up = feed(ups[1], cots[1], *shards, BF16, own_pre)
    back_up = swap(near_up, "tensor", near)
    feed_sums = feed_weights(ups, cots, (own_pre, near_pre), (own_hidden, near_hidden))
    feed_sums = after(feed_sums, far_w, back_up)
    back_out = swap(near_result, "tensor", near)
    own_up = after(own_up, feed_sums)
    feed_sums = lax.psum_scatter(feed_sums, "dp", scatter_dimension=0, tiled=True)

    middle_grad, attn_grad, sums_two, *backs = mix_back(
        own_up, back_up, cotangent, middle, row(second_gain), full, packs, experts, head_dim
    )
    backs = [backs[0]] + [swap(backs[m], "tensor", m) for m in others]
    near_grad = swap(attn_grad, "tensor", near)

    key_grad, value_grad, query_grad, rel_grad, bias_sums, *grad_packs = attend_back(
        rank_ref,
        qc,
        qp,
        key_vecs,
        value_vecs,
        rel_reverse,
        probs,
        heads,
        ogate,
        every,
        vgate,
        backs,
        head_dim,
    )
    out_keep, out_send = out_weights(
        where_grads,
        [packs[0], packs[far_shard]],
        near_packs,
        attn_grad,
        after(near_grad, query_grad),
        experts,
        head_dim,
    )
    out_part = scatter_first(out_keep, swap(out_send, "dp", unit))
    rel_grad = after(rel_grad, *out_part)
    out_fars = scatter_sends(out_part, unit)
    far_pack = swap(grad_packs[1], "tensor", far_shard)
    keep, send, small = weight_grads(
        where_grads,
        normed,
        key_grad,
        value_grad,
        vgate,
        query_grad,
        sin_table,
        rel_grad,
        w_all,
        row(first_gain),
        row(first_bias),
        sums_two,
        bias_sums,
        mem_len,
        head_dim,
        experts,
    )
    kept_far = swap(send, "dp", unit)
    small_far = swap(small, "dp", 1)
    token_own, token_near = token_parts(
        grad_packs[0], far_pack, w_all, after(far_w, keep), head_dim, experts
    )
    feed_own, feed_far = feed_sums[:, : 2 * hidden], feed_sums[:, 2 * hidden :]
    kept_far, small_far, token_near, feed_far, *out_fars = together(
        kept_far, small_far, token_near, feed_far, *out_fars
    )
    feed_far = swap(feed_far, "tensor", far_shard)
    token_near = swap(token_near, "tensor", near)
    kept = scatter_first(keep, kept_far)
    kept_fars = scatter_sends(kept, unit)
    small = small + small_far
    small_fars = [swap(small, "dp", m) for m in range(2, GROUP, 2)]
    out_sums = scatter_done(out_part[0], out_fars, unit, 1).reshape(2, experts * head_dim, -1)
    out_far = swap(out_sums[1].astype(BF16), "tensor", far_shard)
    token_near, *fars = together(token_near, *kept_fars, *small_fars)
    kept_fars, small_fars = fars[: len(fars) // 2], fars[len(fars) // 2 :]
    for far in small_fars:
        small = small + far
    mask = GROUP
    while mask < dp:
        small = small + swap(small, "dp", mask)
        mask *= 2
    small_fars = [swap(small, "tensor", m) for m in others]
    feed_far, *small_fars = together(feed_far, *small_fars)
    kept = scatter_done(kept[0], kept_fars, unit, 1)
    for far in small_fars:
        small = small + far
    tokens_grad = token_sum(
        rank_ref, tokens, middle_grad, row(first_gain), token_own, token_near
    )
    result = (middle + own_result + after(back_out, keep).astype(F32)).astype(BF16)
    out_w = out_sums[0] + after(out_far, token_near).astype(F32)
    feed_grads = feed_own.astype(F32) + feed_far.astype(F32)
    up_total = feed_grads[:, :hidden]
    down_total = feed_grads[:, hidden:].T
    biases = small[4:6, : parts * LANES].reshape(2, parts, LANES)[:, :, :head_dim]
    marks = [0, 1, 1 + experts, 2 + experts, 3 + experts]
    key_w, value_w, query_w, rel_w = (
        kept[a * head_dim : b * head_dim] for a, b in zip(marks, marks[1:])
    )
    select = marks[-1] * head_dim
    turn = lambda part: part.T[None]
    return (
        result,
        tokens_grad,
        small[0],
        small[1],
        small[2],
        small[3],
        turn(query_w),
        turn(key_w),
        turn(rel_w),
        turn(value_w),
        turn(kept[select : select + experts]),
        turn(kept[select + 8 : select + 8 + experts]),
        out_w[None],
        biases[0],
        biases[1],
        up_total,
        down_total,
    )


def solution(mesh):
    placed = (
        P("dp", None),
        P("dp", None, None),
        P("dp", None),
        P("dp", None, "tensor", None),
        P("dp", "tensor", None),
        P(),
        P(),
        P(),
        P(),
        P("tensor", None, None),
        P("tensor", None, None),
        P("tensor", None, None),
        P("tensor", None, None),
        P("tensor", None, None),
        P("tensor", None, None),
        P("tensor", None, None),
        P("tensor", None),
        P("tensor", None),
        P(None, "tensor"),
        P("tensor", None),
        P(("dp", "tensor"), None),
    )
    return jax.shard_map(
        on_device,
        mesh=mesh,
        in_specs=placed,
        out_specs=(
            P(("dp", "tensor"), None),
            P(("dp", "tensor"), None),
            P(),
            P(),
            P(),
            P(),
            P("tensor", "dp", None),
            P("tensor", "dp", None),
            P("tensor", "dp", None),
            P("tensor", "dp", None),
            P("tensor", "dp", None),
            P("tensor", "dp", None),
            P("tensor", None, "dp"),
            P(),
            P(),
            P("dp", "tensor"),
            P("tensor", "dp"),
        ),
        check_vma=False,
    )
```

```python
import functools
import math

import jax
import jax.numpy as jnp
from jax import lax
from jax.experimental import pallas as pl
from jax.experimental.pallas import tpu as pltpu
from jax.sharding import PartitionSpec as P

EPSILON = 1e-05
ROOT_HALF = 0.7071067811865476
INVERSE_ROOT_TAU = 0.3989422804014327
ROWS = 256
GROUP = 8
MIB = 1024 * 1024
BF16 = jnp.bfloat16
F32 = jnp.float32


def mm(left, right):
    return jnp.dot(left, right, preferred_element_type=F32)


def mm_nt(left, right):
    return lax.dot_general(left, right, (((1,), (1,)), ((), ())), preferred_element_type=F32)


def mm_tn(left, right):
    return lax.dot_general(left, right, (((0,), (0,)), ((), ())), preferred_element_type=F32)


def norm_parts(values):
    center = values - jnp.mean(values, axis=-1, keepdims=True)
    inv_std = lax.rsqrt(jnp.mean(center * center, axis=-1, keepdims=True) + EPSILON)
    return center * inv_std, inv_std


def norm_back(upstream, normal, inv_std, gain):
    scaled = upstream * gain
    return inv_std * (
        scaled
        - jnp.mean(scaled, axis=-1, keepdims=True)
        - normal * jnp.mean(scaled * normal, axis=-1, keepdims=True)
    )


def params():
    return pltpu.CompilerParams(vmem_limit_bytes=63 * MIB)


def cost(microseconds):
    return pl.CostEstimate(
        flops=int(microseconds * 1.15e9), bytes_accessed=MIB, transcendentals=0
    )


def struct(shape, dtype):
    return jax.ShapeDtypeStruct(shape, dtype)


def whole(*shape):
    return pl.BlockSpec(shape, lambda *_: (0,) * len(shape))

LANES = 128


def lane_of(rows):
    return lax.broadcasted_iota(jnp.int32, (rows, LANES), 1)


def picked(routes, head_dim):
    rows = routes.shape[1]
    routes = jnp.concatenate([routes, jnp.zeros((6, rows), jnp.int32)], axis=0).astype(F32).T
    lane = (lane_of(rows) - head_dim).astype(F32)
    return (lane == routes[:, 0:1]) | (lane == routes[:, 1:2])


def after(array, *deps):
    def body(*refs):
        del refs

    spec = pl.BlockSpec(memory_space=pl.ANY)
    return pl.pallas_call(
        body,
        in_specs=[spec] * (1 + len(deps)),
        out_specs=spec,
        out_shape=struct(array.shape, array.dtype),
        input_output_aliases={0: 0},
        name="after",
    )(array, *deps)


def together(*arrays):
    def body(*refs):
        del refs

    spec = pl.BlockSpec(memory_space=pl.ANY)
    return pl.pallas_call(
        body,
        in_specs=[spec] * len(arrays),
        out_specs=[spec] * len(arrays),
        out_shape=[struct(a.shape, a.dtype) for a in arrays],
        input_output_aliases={i: i for i in range(len(arrays))},
        name="together",
    )(*arrays)


def pile(*arrays):
    def body(*refs):
        for i, ref in enumerate(refs[:-1]):
            refs[-1][i] = ref[...]

    shape = arrays[0].shape
    return pl.pallas_call(
        body,
        in_specs=[whole(*shape)] * len(arrays),
        out_specs=whole(len(arrays), *shape),
        out_shape=struct((len(arrays),) + shape, arrays[0].dtype),
        grid=(1,),
        compiler_params=params(),
        cost_estimate=cost(2),
        name="pile",
    )(*arrays)


def project_kernel(
    experts,
    head_dim,
    mem_steps,
    scale,
    mem_ref,
    tok_ref,
    gain_ref,
    bias_ref,
    key_w_ref,
    vsel_ref,
    value_w_ref,
    query_w_ref,
    osel_ref,
    vroute_ref,
    oroute_ref,
    cb_ref,
    pb_ref,
    w_out_ref,
    normed_ref,
    key_ref,
    val_ref,
    every_ref,
    vgate_ref,
    qc_ref,
    qp_ref,
    ogate_ref,
    w_ref,
):
    step = pl.program_id(0)
    query = (1 + experts) * LANES

    @pl.when(step == 0)
    def _():
        w_ref[...] = jnp.zeros_like(w_ref)
        w_ref[:head_dim, :] = key_w_ref[...]
        w_ref[head_dim : head_dim + experts, :] = vsel_ref[...]
        for e in range(experts):
            w_ref[(1 + e) * LANES : (1 + e) * LANES + head_dim, :] = value_w_ref[
                e * head_dim : (e + 1) * head_dim, :
            ]
        w_ref[query : query + head_dim, :] = query_w_ref[...]
        w_ref[query + head_dim : query + head_dim + experts, :] = osel_ref[...]

    size = w_out_ref.shape[0]
    w_out_ref[...] = w_ref[pl.ds(pl.multiple_of(step * size, size), size), :]

    def rows_part(rows_ref, columns, last):
        blocks = [slice(i * ROWS, (i + 1) * ROWS) for i in range(rows_ref.shape[0] // ROWS)]
        normed, outs = [], []
        for rows in blocks:
            normal, _ = norm_parts(rows_ref[rows, :].astype(F32))
            normed.append((normal * gain_ref[...] + bias_ref[...]).astype(BF16))
            outs.append(mm_nt(normed[-1], w_ref[:columns, :]))
        lane = lane_of(ROWS)
        real = lane < head_dim
        for rows, norm, out in zip(blocks, normed, outs):
            normed_ref[rows, :] = norm
            first = out[:, :LANES]
            key_ref[rows, :] = jnp.where(real, first, 0.0).astype(BF16)
            every_ref[rows, :] = out[:, LANES:query].astype(BF16)
            gate = jnp.where(picked(vroute_ref[:, rows], head_dim), jax.nn.sigmoid(first), 0.0)
            vgate_ref[rows, :] = gate
            value = jnp.zeros((ROWS, LANES), F32)
            for e in range(experts):
                value = value + gate[:, head_dim + e : head_dim + e + 1] * (
                    out[:, (1 + e) * LANES : (2 + e) * LANES]
                )
            val_ref[rows, :] = value.astype(BF16)
            if last:
                q = out[:, query:]
                qc_ref[rows, :] = jnp.where(real, (q + cb_ref[...]) * scale, 0.0).astype(BF16)
                qp_ref[rows, :] = jnp.where(real, (q + pb_ref[...]) * scale, 0.0).astype(BF16)
                ogate_ref[rows, :] = jnp.where(
                    picked(oroute_ref[:, rows], head_dim), jax.nn.sigmoid(q), 0.0
                )

    @pl.when(step < mem_steps)
    def _():
        rows_part(mem_ref, query, False)

    @pl.when(step >= mem_steps)
    def _():
        rows_part(tok_ref, query + LANES, True)


def project(memory, tokens, gain, bias, weights, vroutes, oroutes, cb, pb, experts, head_dim):
    mem, width = memory.shape
    toks = tokens.shape[0]
    big = 2 * ROWS
    mem_steps, tok_steps = mem // big, toks // big
    steps = mem_steps + tok_steps
    keys = mem + toks
    cols = width
    mem_row = lambda i: (jnp.minimum(i, mem_steps - 1), 0)
    tok_row = lambda i: (jnp.maximum(i - mem_steps, 0), 0)
    row = lambda i: (i, 0)
    return pl.pallas_call(
        functools.partial(project_kernel, experts, head_dim, mem_steps, head_dim ** (-0.5)),
        grid=(steps,),
        in_specs=[
            pl.BlockSpec((big, width), mem_row),
            pl.BlockSpec((big, width), tok_row),
            whole(1, width),
            whole(1, width),
        ]
        + [whole(*w.shape) for w in weights]
        + [
            pl.BlockSpec((vroutes.shape[0], big), lambda i: (0, i)),
            pl.BlockSpec((oroutes.shape[0], big), lambda i: (0, jnp.maximum(i - mem_steps, 0))),
            whole(1, LANES),
            whole(1, LANES),
        ],
        out_specs=[
            pl.BlockSpec((cols // steps, width), row),
            pl.BlockSpec((big, width), row),
            pl.BlockSpec((big, LANES), row),
            pl.BlockSpec((big, LANES), row),
            pl.BlockSpec((big, experts * LANES), row),
            pl.BlockSpec((big, LANES), row),
            pl.BlockSpec((big, LANES), tok_row),
            pl.BlockSpec((big, LANES), tok_row),
            pl.BlockSpec((big, LANES), tok_row),
        ],
        out_shape=[
            struct((cols, width), BF16),
            struct((keys, width), BF16),
            struct((keys, LANES), BF16),
            struct((keys, LANES), BF16),
            struct((keys, experts * LANES), BF16),
            struct((keys, LANES), F32),
            struct((toks, LANES), BF16),
            struct((toks, LANES), BF16),
            struct((toks, LANES), F32),
        ],
        scratch_shapes=[pltpu.VMEM((cols, width), BF16)],
        compiler_params=params(),
        cost_estimate=cost(12),
        name="project",
    )(memory, tokens, gain, bias, *weights, vroutes, oroutes, cb, pb)


def attend_kernel(
    span,
    head_dim,
    count,
    z_ref,
    qc_ref,
    qp_ref,
    key_ref,
    val_ref,
    rel_ref,
    segk_ref,
    segq_ref,
    ogate_ref,
    heads_ref,
    probs_ref,
    *pack_refs,
):
    step = pl.program_id(0)
    wide = span + ROWS
    column = lax.broadcasted_iota(jnp.int32, (ROWS, ROWS), 1)
    causal = column <= lax.broadcasted_iota(jnp.int32, (ROWS, ROWS), 0)
    for b in range(count):
        rows = slice(b * ROWS, (b + 1) * ROWS)
        window = pl.ds((step * count + b) * ROWS, wide)
        content = mm_nt(qc_ref[rows, :], key_ref[window, :])
        reverse = mm_nt(qp_ref[rows, :], rel_ref[...])
        reverse = jnp.concatenate([reverse, jnp.zeros((ROWS, ROWS), F32)], axis=1)
        scores = content + pltpu.roll(reverse, 1, 1, stride=1, stride_axis=0)
        same = segk_ref[b] == segq_ref[rows, :]
        allowed = jnp.concatenate([same[:, :span], same[:, span:] & causal], axis=1)
        scores = jnp.where(allowed, scores, -1e30)
        expo = jnp.exp(scores - jnp.max(scores, axis=1, keepdims=True))
        probs = (expo * (1.0 / jnp.sum(expo, axis=1, keepdims=True))).astype(BF16)
        probs_ref[rows, :] = probs
        heads = mm(probs, val_ref[window, :])
        heads_ref[rows, :] = heads
        packed = jnp.where(lane_of(ROWS) < head_dim, heads, ogate_ref[rows, :]).astype(BF16)
        slot = (step * count + b) ^ z_ref[0]
        for side, pack_ref in enumerate(pack_refs):

            @pl.when(slot // 2 == side)
            def _():
                pack_ref[slot % 2] = packed


def attend(rank, qc, qp, key_vecs, value_vecs, rel_reverse, seg_keys, seg_query, ogate, head_dim):
    toks = qc.shape[0]
    keys = key_vecs.shape[0]
    span = rel_reverse.shape[0]
    steps = toks // ROWS
    count = 2
    big = count * ROWS
    wide = span + ROWS
    row = lambda i, z: (i, 0)
    return pl.pallas_call(
        functools.partial(attend_kernel, span, head_dim, count),
        grid_spec=pltpu.PrefetchScalarGridSpec(
            num_scalar_prefetch=1,
            grid=(steps // count,),
            in_specs=[
                pl.BlockSpec((big, LANES), row),
                pl.BlockSpec((big, LANES), row),
                whole(keys, LANES),
                whole(keys, LANES),
                whole(span, LANES),
                pl.BlockSpec((count, 1, wide), lambda i, z: (i, 0, 0)),
                pl.BlockSpec((big, 1), row),
                pl.BlockSpec((big, LANES), row),
            ],
            out_specs=[
                pl.BlockSpec((big, LANES), row),
                pl.BlockSpec((big, wide), row),
            ]
            + [whole(2, ROWS, LANES)] * (steps // 2),
        ),
        out_shape=[struct((toks, LANES), F32), struct((toks, wide), BF16)]
        + [struct((2, ROWS, LANES), BF16)] * (steps // 2),
        compiler_params=params(),
        cost_estimate=cost(8),
        name="attend",
    )(rank, qc, qp, key_vecs, value_vecs, rel_reverse, seg_keys, seg_query, ogate)


def attend_back_kernel(
    span,
    experts,
    head_dim,
    parts,
    z_ref,
    qc_ref,
    qp_ref,
    key_ref,
    val_ref,
    rel_ref,
    probs_ref,
    heads_ref,
    ogate_ref,
    every_ref,
    vgate_ref,
    *refs,
):
    back_refs, refs = refs[: parts // 2], refs[parts // 2 :]
    key_grad_ref, value_grad_ref, query_grad_ref, rel_grad_ref, bias_ref = refs[:5]
    pack_refs, refs = refs[5 : 5 + parts // 2], refs[5 + parts // 2 :]
    keys_scr, values_scr, rel_scr, query_scr, back_scr = refs
    step = pl.program_id(0)
    steps = pl.num_programs(0)
    wide = span + ROWS
    mem = keys_scr.shape[0] - steps * ROWS
    scale = head_dim ** (-0.5)
    real = lane_of(ROWS) < head_dim

    @pl.when(step == 0)
    def _():
        keys_scr[...] = jnp.zeros_like(keys_scr)
        values_scr[...] = jnp.zeros_like(values_scr)
        rel_scr[...] = jnp.zeros_like(rel_scr)
        bias_ref[...] = jnp.zeros_like(bias_ref)

    slot = step ^ z_ref[0]
    for side, back_ref in enumerate(back_refs):

        @pl.when(slot // 2 == side)
        def _():
            back_scr[...] = back_ref[slot % 2]

    window = pl.ds(step * ROWS, wide)
    keys = key_ref[window, :]
    vals = val_ref[window, :]
    back = back_scr[...].astype(F32)
    out_grad = jnp.where(real, back, 0.0)
    delta = jnp.sum(out_grad * heads_ref[...], axis=1, keepdims=True)
    out_grad = out_grad.astype(BF16)
    probs = probs_ref[...]
    probs_grad = mm_nt(out_grad, vals)
    score_grad = (probs.astype(F32) * (probs_grad - delta)).astype(BF16)
    content_grad = mm(score_grad, keys).astype(BF16).astype(F32) * scale
    keys_scr[window, :] += mm_tn(score_grad, qc_ref[...])
    values_scr[window, :] += mm_tn(probs, out_grad)
    flip = (
        lax.broadcasted_iota(jnp.int32, (ROWS, ROWS), 0)
        + lax.broadcasted_iota(jnp.int32, (ROWS, ROWS), 1)
        == ROWS - 1
    ).astype(BF16)
    turned = mm(flip, score_grad)
    turned = pltpu.roll(turned, span, 1, stride=1, stride_axis=0)[:, :span].astype(BF16)
    place_grad = mm(turned, rel_ref[...]).astype(BF16)
    position_grad = mm(flip, place_grad) * scale
    rel_scr[...] += mm_tn(turned, mm(flip, qp_ref[...]).astype(BF16))
    bias_ref[0:1, :] += jnp.sum(content_grad, axis=0, keepdims=True)
    bias_ref[1:2, :] += jnp.sum(position_grad, axis=0, keepdims=True)
    gate = ogate_ref[...]
    query_grad = jnp.where(real, content_grad + position_grad, back * gate * (1.0 - gate))
    query_grad = query_grad.astype(BF16)
    query_grad_ref[...] = query_grad
    query_scr[pl.ds(step * ROWS, ROWS), :] = query_grad

    @pl.when(step == steps - 1)
    def _():
        rel_grad_ref[...] = rel_scr[...].astype(BF16)

        @pl.loop(0, (mem + steps * ROWS) // ROWS)
        def _(block):
            rows = pl.ds(block * ROWS, ROWS)
            value_grad = values_scr[rows, :]
            gates = vgate_ref[rows, :]
            value_grad_ref[rows, :] = value_grad
            logit = keys_scr[rows, :]
            lane = lane_of(ROWS)
            for e in range(experts):
                part = every_ref[rows, e * LANES : (e + 1) * LANES].astype(F32)
                total = jnp.sum(value_grad * part, axis=1, keepdims=True)
                logit = jnp.where(lane == head_dim + e, total, logit)
            key_grad = jnp.where(real, logit, logit * gates * (1.0 - gates)).astype(BF16)
            key_grad_ref[rows, :] = key_grad

            @pl.when(block * ROWS >= mem)
            def _():
                place = block - mem // ROWS
                slot = place ^ z_ref[0]
                value_pack = jnp.where(real, value_grad, gates).astype(BF16)
                for side, pack_ref in enumerate(pack_refs):

                    @pl.when(slot // 2 == side)
                    def _():
                        pack_ref[slot % 2, 0] = key_grad
                        pack_ref[slot % 2, 1] = value_pack
                        pack_ref[slot % 2, 2] = query_scr[pl.ds(place * ROWS, ROWS), :]


def attend_back(
    rank,
    qc,
    qp,
    key_vecs,
    value_vecs,
    rel_reverse,
    probs,
    heads,
    ogate,
    every,
    vgate,
    backs,
    head_dim,
):
    toks = qc.shape[0]
    keys = key_vecs.shape[0]
    span = rel_reverse.shape[0]
    steps = toks // ROWS
    wide = span + ROWS
    experts = every.shape[1] // LANES
    row = lambda i, z: (i, 0)
    return pl.pallas_call(
        functools.partial(attend_back_kernel, span, experts, head_dim, steps),
        grid_spec=pltpu.PrefetchScalarGridSpec(
            num_scalar_prefetch=1,
            grid=(steps,),
            in_specs=[
                pl.BlockSpec((ROWS, LANES), row),
                pl.BlockSpec((ROWS, LANES), row),
                whole(keys, LANES),
                whole(keys, LANES),
                whole(span, LANES),
                pl.BlockSpec((ROWS, wide), row),
                pl.BlockSpec((ROWS, LANES), row),
                pl.BlockSpec((ROWS, LANES), row),
                whole(keys, experts * LANES),
                whole(keys, LANES),
            ]
            + [whole(2, ROWS, LANES)] * (steps // 2),
            out_specs=[
                whole(keys, LANES),
                whole(keys, LANES),
                pl.BlockSpec((ROWS, LANES), row),
                whole(span, LANES),
                whole(2, LANES),
            ]
            + [whole(2, 3, ROWS, LANES)] * (steps // 2),
            scratch_shapes=[
                pltpu.VMEM((keys, LANES), F32),
                pltpu.VMEM((keys, LANES), F32),
                pltpu.VMEM((span, LANES), F32),
                pltpu.VMEM((toks, LANES), BF16),
                pltpu.VMEM((ROWS, LANES), BF16),
            ],
        ),
        out_shape=[
            struct((keys, LANES), BF16),
            struct((keys, LANES), F32),
            struct((toks, LANES), BF16),
            struct((span, LANES), BF16),
            struct((2, LANES), F32),
        ]
        + [struct((2, 3, ROWS, LANES), BF16)] * (steps // 2),
        compiler_params=params(),
        cost_estimate=cost(15),
        name="attend_back",
    )(rank, qc, qp, key_vecs, value_vecs, rel_reverse, probs, heads, ogate, every, vgate, *backs)


def mix_kernel(experts, head_dim, where_ref, *refs):
    pack_refs, refs = refs[:2], refs[2:]
    own_ref, even_ref, odd_ref, full_ref, own_part_ref, near_part_ref, mixed_scr = refs
    step = pl.program_id(0)

    @pl.when(step == 0)
    def _():
        real = lane_of(ROWS) < head_dim
        for h in range(2):
            for block in range(2):
                pack = pack_refs[h][block].astype(F32)
                out = jnp.where(real, pack, 0.0)
                rows = slice(block * ROWS, (block + 1) * ROWS)
                for e in range(experts):
                    gate = pack[:, head_dim + e : head_dim + e + 1]
                    mixed_scr[h, rows, e * LANES : (e + 1) * LANES] = (gate * out).astype(BF16)

    turned = where_ref[1] == 1
    even, odd = even_ref[0], odd_ref[0]
    far = jnp.concatenate([jnp.where(turned, odd, even), jnp.where(turned, even, odd)], axis=1)
    total = None
    for h, weight in enumerate((own_ref[...], far)):
        for e in range(experts):
            full_ref[h, e * LANES : e * LANES + head_dim, :] = weight[
                e * head_dim : (e + 1) * head_dim
            ]
            full_ref[h, e * LANES + head_dim : (e + 1) * LANES, :] = jnp.zeros(
                (LANES - head_dim, weight.shape[1]), BF16
            )
        part = mm(mixed_scr[h], full_ref[h])
        total = part if total is None else total + part
    own_part_ref[...] = total[:ROWS]
    near_part_ref[...] = total[ROWS:].astype(BF16)


def mix(where, packs, own_weight, even, odd, experts, head_dim):
    depth, width = own_weight.shape
    steps = even.shape[0]
    size = width // steps
    column = lambda s, w: (0, w[0] ^ s)
    return pl.pallas_call(
        functools.partial(mix_kernel, experts, head_dim),
        grid_spec=pltpu.PrefetchScalarGridSpec(
            num_scalar_prefetch=1,
            grid=(steps,),
            in_specs=[whole(2, ROWS, LANES)] * 2
            + [
                pl.BlockSpec((depth, size), column),
                pl.BlockSpec((1,) + even.shape[1:], lambda s, w: (s, 0, 0)),
                pl.BlockSpec((1,) + odd.shape[1:], lambda s, w: (s, 0, 0)),
            ],
            out_specs=[
                pl.BlockSpec((2, experts * LANES, size), lambda s, w: (0, 0, w[0] ^ s)),
                pl.BlockSpec((ROWS, size), column),
                pl.BlockSpec((ROWS, size), column),
            ],
            scratch_shapes=[pltpu.VMEM((2, 2 * ROWS, experts * LANES), BF16)],
        ),
        out_shape=[
            struct((2, experts * LANES, width), BF16),
            struct((ROWS, width), F32),
            struct((ROWS, width), BF16),
        ],
        compiler_params=params(),
        cost_estimate=cost(7),
        name="mix",
    )(where, *packs, own_weight, even, odd)


def middle_kernel(z_ref, tok_ref, own_ref, near_ref, gain_ref, bias_ref, middle_ref, up_ref):
    middle = tok_ref[...].astype(F32) + (own_ref[...] + near_ref[...].astype(F32))
    middle_ref[...] = middle
    normal, _ = norm_parts(middle)
    up_ref[...] = (normal * gain_ref[...] + bias_ref[...]).astype(BF16)


def middle_rows(rank, tokens, own, near, gain, bias):
    rows, width = own.shape
    steps = 2
    block = pl.BlockSpec((rows // steps, width), lambda i, z: (i, 0))
    return pl.pallas_call(
        middle_kernel,
        grid_spec=pltpu.PrefetchScalarGridSpec(
            num_scalar_prefetch=1,
            grid=(steps,),
            in_specs=[
                pl.BlockSpec((rows // steps, width), lambda i, z: (z[0] * steps + i, 0)),
                block,
                block,
                whole(1, width),
                whole(1, width),
            ],
            out_specs=[block, block],
        ),
        out_shape=[struct((rows, width), F32), struct((rows, width), BF16)],
        compiler_params=params(),
        cost_estimate=cost(3),
        name="middle",
    )(rank, tokens, own, near, gain, bias)


def middle_back_kernel(
    own_ref, near_ref, cot_ref, middle_ref, gain_ref, grad_ref, low_ref, sums_ref
):
    upstream = own_ref[...].astype(F32) + near_ref[...].astype(F32)
    normal, inv_std = norm_parts(middle_ref[...])

    @pl.when(pl.program_id(0) == 0)
    def _():
        sums_ref[...] = jnp.zeros_like(sums_ref)

    sums_ref[0:1, :] += jnp.sum(upstream * normal, axis=0, keepdims=True)
    sums_ref[1:2, :] += jnp.sum(upstream, axis=0, keepdims=True)
    grad = cot_ref[...].astype(F32) + norm_back(upstream, normal, inv_std, gain_ref[...])
    grad_ref[...] = grad
    low_ref[...] = grad.astype(BF16)


def middle_back(own, near, cot, middle, gain):
    rows, width = middle.shape
    steps = 2
    block = pl.BlockSpec((rows // steps, width), lambda i: (i, 0))
    return pl.pallas_call(
        middle_back_kernel,
        grid=(steps,),
        in_specs=[block] * 4 + [whole(1, width)],
        out_specs=[block, block, whole(2, width)],
        out_shape=[
            struct((rows, width), F32),
            struct((rows, width), BF16),
            struct((2, width), F32),
        ],
        compiler_params=params(),
        cost_estimate=cost(4),
        name="middle_back",
    )(own, near, cot, middle, gain)


def heads_back_kernel(experts, head_dim, own_ref, near_ref, full_ref, *refs):
    pack_refs, out_refs = refs[:2], refs[2:]
    lane = lane_of(ROWS)
    real = lane < head_dim
    grads = [mm_nt(ref[...], full_ref[0]) for ref in (own_ref, near_ref)]
    for h in range(2):

        @pl.when(pl.program_id(0) == h)
        def _():
            for block, grad in enumerate(grads):
                grad = grad.astype(BF16).astype(F32)
                pack = pack_refs[h][block].astype(F32)
                total = jnp.zeros((ROWS, LANES), F32)
                gates = jnp.zeros((ROWS, LANES), F32)
                for e in range(experts):
                    part = grad[:, e * LANES : (e + 1) * LANES]
                    total = total + pack[:, head_dim + e : head_dim + e + 1] * part
                    inner = jnp.sum(part * pack, axis=1, keepdims=True)
                    gates = jnp.where(lane == head_dim + e, inner, gates)
                out_refs[h][block] = jnp.where(real, total, gates).astype(BF16)


def heads_back(own, near, full, packs, experts, head_dim):
    heads, depth, width = full.shape
    rows = own.shape[0]
    return pl.pallas_call(
        functools.partial(heads_back_kernel, experts, head_dim),
        grid=(heads,),
        in_specs=[whole(rows, width)] * 2
        + [pl.BlockSpec((1, depth, width), lambda m: (m, 0, 0))]
        + [whole(2, ROWS, LANES)] * 2,
        out_specs=[whole(2, ROWS, LANES)] * 2,
        out_shape=[struct((2, ROWS, LANES), BF16)] * 2,
        compiler_params=params(),
        cost_estimate=cost(6),
        name="heads_back",
    )(own, near, full, *packs)


def feed_kernel(half, up_ref, cot_ref, wu_ref, wd_ref, far_u_ref, far_d_ref, *refs):
    refs = refs[-6:]
    hidden_ref, pre_grad_ref, out_ref, up_grad_ref, out_scr, up_scr = refs
    step = pl.program_id(0)
    steps = pl.num_programs(0)
    width = up_ref.shape[1]
    count = wu_ref.shape[1] // ROWS

    @pl.when(step == 0)
    def _():
        out_scr[...] = jnp.zeros_like(out_scr)
        up_scr[...] = jnp.zeros_like(up_scr)

    def part(w_up, w_down):
        pres, grads = [], []
        for b in range(count):
            cols = slice(b * ROWS, (b + 1) * ROWS)
            pres.append(mm(up_ref[...], w_up[:, cols]))
            grads.append(mm_nt(cot_ref[...], w_down[cols, :]))
        out, up_grad = None, None
        for b in range(count):
            cols = slice(b * ROWS, (b + 1) * ROWS)
            pre = pres[b]
            hidden_grad = grads[b].astype(BF16).astype(F32)
            phi = 0.5 * (1.0 + lax.erf(pre * ROOT_HALF))
            hidden = (pre * phi).astype(BF16)
            slope = phi + pre * jnp.exp(-0.5 * pre * pre) * INVERSE_ROOT_TAU
            pre_grad = (hidden_grad * slope).astype(BF16)
            hidden_ref[:, cols] = hidden
            pre_grad_ref[:, cols] = pre_grad
            out_part, up_part = mm(hidden, w_down[cols, :]), mm_nt(pre_grad, w_up[:, cols])
            out = out_part if out is None else out + out_part
            up_grad = up_part if up_grad is None else up_grad + up_part
        out_scr[...] += out
        up_scr[...] += up_grad

    @pl.when(step < half)
    def _():
        part(wu_ref[...], wd_ref[...])

    @pl.when(step >= half)
    def _():
        part(far_u_ref[...].reshape(width, -1), far_d_ref[...].reshape(-1, width))

    @pl.when(step == steps - 1)
    def _():
        out_ref[...] = out_scr[...].astype(out_ref.dtype)
        up_grad_ref[...] = up_scr[...].astype(up_grad_ref.dtype)


def feed(up_in, cot, w_up, w_down, far, dtype, *deps):
    rows, width = up_in.shape
    hidden = w_up.shape[1]
    size = 2 * ROWS
    half = hidden // size
    pieces, _, depth, _ = far.shape
    count = size // depth
    own = lambda i: jnp.minimum(i, half - 1)
    other = lambda i: jnp.maximum(i - half, 0)
    return pl.pallas_call(
        functools.partial(feed_kernel, half),
        grid=(2 * half,),
        in_specs=[
            whole(rows, width),
            whole(rows, width),
            pl.BlockSpec((width, size), lambda i: (0, own(i))),
            pl.BlockSpec((size, width), lambda i: (own(i), 0)),
            pl.BlockSpec((pieces, 1, depth, size), lambda i: (0, 0, 0, other(i))),
            pl.BlockSpec((count, 1, depth, width), lambda i: (other(i), 1, 0, 0)),
        ]
        + [pl.BlockSpec(memory_space=pl.ANY)] * len(deps),
        out_specs=[
            pl.BlockSpec((rows, size), lambda i: (0, i)),
            pl.BlockSpec((rows, size), lambda i: (0, i)),
            whole(rows, width),
            whole(rows, width),
        ],
        out_shape=[
            struct((rows, 2 * hidden), BF16),
            struct((rows, 2 * hidden), BF16),
            struct((rows, width), dtype),
            struct((rows, width), dtype),
        ],
        scratch_shapes=[pltpu.VMEM((rows, width), F32), pltpu.VMEM((rows, width), F32)],
        compiler_params=params(),
        cost_estimate=cost(10),
        name="feed",
    )(up_in, cot, w_up, w_down, far, far, *deps)


def feed_weights_kernel(count, half, *refs):
    lefts, refs = refs[: 2 * count], refs[2 * count :]
    rights, out_ref = refs[: 2 * count], refs[2 * count]
    step = pl.program_id(0)

    for which in range(2):

        @pl.when((step // half) % 2 == which)
        def _():
            total = None
            for m in range(which * count, (which + 1) * count):
                part = mm_tn(lefts[m][...], rights[m][...])
                total = part if total is None else total + part
            out_ref[...] = total.astype(BF16)


def feed_weights(ups, cots, pre_grads, hiddens):
    count = len(ups)
    rows, width = ups[0].shape
    hidden = hiddens[0].shape[1] // 2
    size = 512
    half = hidden // size

    def columns(which):
        def at(i):
            shard, inner = i // (2 * half), i % (2 * half)
            return (0, shard * half + jnp.clip(inner - which * half, 0, half - 1))

        return pl.BlockSpec((rows, size), at)

    return pl.pallas_call(
        functools.partial(feed_weights_kernel, count, half),
        grid=(4 * half,),
        in_specs=[whole(rows, width)] * (2 * count)
        + [columns(0)] * count
        + [columns(1)] * count,
        out_specs=pl.BlockSpec((width, size), lambda i: (0, i)),
        out_shape=struct((width, 4 * hidden), BF16),
        compiler_params=params(),
        cost_estimate=cost(11),
        name="feed_weights",
    )(*ups, *cots, *pre_grads, *hiddens)


def out_weights_kernel(experts, head_dim, heads, where_ref, *refs):
    pack_refs, refs = refs[:heads], refs[heads:]
    grad_ref, near_grad_ref, keep_ref, send_ref, mixed_scr, scr = refs
    real = lane_of(ROWS) < head_dim

    def fill(begin, pack):
        pack = pack.astype(F32)
        out = jnp.where(real, pack, 0.0)
        for e in range(experts):
            gate = pack[:, head_dim + e : head_dim + e + 1]
            mixed_scr[begin : begin + ROWS, e * LANES : (e + 1) * LANES] = (gate * out).astype(
                BF16
            )

    for m in range(heads):

        @pl.when(pl.program_id(0) == m)
        def _():
            fill(0, pack_refs[m][0])
            fill(ROWS, pack_refs[m][1])

    scr[...] = mm_tn(mixed_scr[:ROWS], grad_ref[...]) + mm_tn(
        mixed_scr[ROWS:], near_grad_ref[...]
    )
    for k in range(GROUP):
        target = send_ref if k % 2 else keep_ref
        lanes = pl.ds(pl.multiple_of((where_ref[0] ^ k) * LANES, LANES), LANES)
        for e in range(experts):
            target[k // 2, e * head_dim : (e + 1) * head_dim, :] = scr[
                e * LANES : e * LANES + head_dim, lanes
            ].astype(BF16)


def out_weights(where, packs, grad, near_grad, experts, head_dim):
    heads = len(packs)
    rows, width = grad.shape
    depth = experts * head_dim
    shape = (GROUP // 2, heads * depth, width // GROUP)
    spec = pl.BlockSpec((GROUP // 2, depth, width // GROUP), lambda m, w: (0, m, 0))
    return pl.pallas_call(
        functools.partial(out_weights_kernel, experts, head_dim, heads),
        grid_spec=pltpu.PrefetchScalarGridSpec(
            num_scalar_prefetch=1,
            grid=(heads,),
            in_specs=[whole(2, rows, LANES)] * heads + [whole(rows, width)] * 2,
            out_specs=[spec] * 2,
            scratch_shapes=[
                pltpu.VMEM((2 * rows, experts * LANES), BF16),
                pltpu.VMEM((experts * LANES, width), F32),
            ],
        ),
        out_shape=[struct(shape, BF16)] * 2,
        compiler_params=params(),
        cost_estimate=cost(5),
        name="out_weights",
    )(where, *packs, grad, near_grad)


def weights_kernel(
    experts,
    head_dim,
    counts,
    where_ref,
    normed_ref,
    key_ref,
    value_ref,
    gate_ref,
    query_ref,
    table_ref,
    rel_ref,
    w_ref,
    gain_ref,
    bias_ref,
    sums_ref,
    biases_ref,
    keep_ref,
    send_ref,
    small_ref,
    grads_scr,
    sum_scr,
    main_scr,
    rel_scr,
):
    step = pl.program_id(0)
    mem_steps, key_steps, rel_steps = counts
    query = (1 + experts) * LANES

    @pl.when(step == 0)
    def _():
        main_scr[...] = jnp.zeros_like(main_scr)
        sum_scr[...] = jnp.zeros_like(sum_scr)
        rel_scr[...] = jnp.zeros_like(rel_scr)

    def add(columns):
        grads = grads_scr[:, :columns]
        main_scr[:columns, :] += mm_tn(grads, normed_ref[...])
        sum_scr[:columns, :] += mm_tn(grads, jnp.ones((grads.shape[0], LANES), BF16))

    @pl.when(step < key_steps)
    def _():
        value_grad = value_ref[...]
        grads_scr[:, :LANES] = key_ref[...]
        for e in range(experts):
            gate = gate_ref[:, head_dim + e : head_dim + e + 1]
            grads_scr[:, LANES * (1 + e) : LANES * (2 + e)] = (gate * value_grad).astype(BF16)

    @pl.when(step < mem_steps)
    def _():
        add(query)

    @pl.when((step >= mem_steps) & (step < key_steps))
    def _():
        grads_scr[:, query:] = query_ref[...]
        add(query + LANES)

    @pl.when(step >= key_steps)
    def _():
        rel_scr[...] += mm_tn(rel_ref[...], table_ref[...])

    @pl.when(step == key_steps + rel_steps - 1)
    def _():
        weights = w_ref[...].astype(F32)
        bias_one = jnp.sum(weights * sum_scr[:, 0:1], axis=0, keepdims=True)
        inner = jnp.sum(weights * main_scr[...], axis=0, keepdims=True)
        small_ref[...] = jnp.zeros_like(small_ref)
        small_ref[0:1, :] = (inner - bias_ref[...] * bias_one) / gain_ref[...]
        small_ref[1:2, :] = bias_one
        small_ref[2:4, :] = sums_ref[...]
        small_ref[4:6, pl.ds(pl.multiple_of(where_ref[1] * LANES, LANES), LANES)] = biases_ref[...]
        for k in range(GROUP):
            target = send_ref if k % 2 else keep_ref
            at = k // 2
            lanes = pl.ds(pl.multiple_of((where_ref[0] ^ k) * LANES, LANES), LANES)
            row = 0

            def put(source, begin, size):
                target[at, row : row + size, :] = source[begin : begin + size, lanes].astype(BF16)
                return row + size

            for section in range(2 + experts):
                row = put(main_scr, section * LANES, head_dim)
            row = put(rel_scr, 0, head_dim)
            target[at, row:, :] = jnp.concatenate(
                [
                    main_scr[head_dim : head_dim + 8, lanes],
                    main_scr[query + head_dim : query + head_dim + 8, lanes],
                ],
                axis=0,
            ).astype(BF16)


def weight_grads(
    where,
    normed,
    key_grad,
    value_grad,
    gates,
    query_grad,
    table,
    rel_grad,
    w_all,
    gain,
    bias,
    sums_two,
    bias_sums,
    mem,
    head_dim,
    experts,
):
    keys, width = normed.shape
    cols = (2 + experts) * LANES
    big = 2 * ROWS
    mem_steps, key_steps = mem // big, keys // big
    rel_steps = table.shape[0] // big
    counts = (mem_steps, key_steps, rel_steps)
    rows = (3 + experts) * head_dim + 16
    key_row = lambda i, w: (jnp.minimum(i, key_steps - 1), 0)
    tok_row = lambda i, w: (jnp.clip(i - mem_steps, 0, key_steps - mem_steps - 1), 0)
    rel_row = lambda i, w: (jnp.clip(i - key_steps, 0, rel_steps - 1), 0)
    half = GROUP // 2
    return pl.pallas_call(
        functools.partial(weights_kernel, experts, head_dim, counts),
        grid_spec=pltpu.PrefetchScalarGridSpec(
            num_scalar_prefetch=1,
            grid=(key_steps + rel_steps,),
            in_specs=[
                pl.BlockSpec((big, width), key_row),
                pl.BlockSpec((big, LANES), key_row),
                pl.BlockSpec((big, LANES), key_row),
                pl.BlockSpec((big, LANES), key_row),
                pl.BlockSpec((big, LANES), tok_row),
                pl.BlockSpec((big, width), rel_row),
                pl.BlockSpec((big, LANES), rel_row),
                whole(cols, width),
                whole(1, width),
                whole(1, width),
                whole(2, width),
                whole(2, LANES),
            ],
            out_specs=[
                whole(half, rows, LANES),
                whole(half, rows, LANES),
                whole(8, width),
            ],
            scratch_shapes=[
                pltpu.VMEM((big, cols), BF16),
                pltpu.VMEM((cols, LANES), F32),
                pltpu.VMEM((cols, width), F32),
                pltpu.VMEM((LANES, width), F32),
            ],
        ),
        out_shape=[
            struct((half, rows, LANES), BF16),
            struct((half, rows, LANES), BF16),
            struct((8, width), F32),
        ],
        compiler_params=params(),
        cost_estimate=cost(15),
        name="weight_grads",
    )(
        where,
        normed,
        key_grad,
        value_grad,
        gates,
        query_grad,
        table,
        rel_grad,
        w_all,
        gain,
        bias,
        sums_two,
        bias_sums,
    )


def token_kernel(experts, head_dim, own_ref, far_ref, w_own_ref, w_far_ref, *refs):
    out_refs, grads_scr, total_scr = refs[:2], refs[2], refs[3]
    step = pl.program_id(0)
    query = (1 + experts) * LANES
    cols = query + LANES
    real = lane_of(ROWS) < head_dim

    def part(pack_ref, weights):
        for block in range(2):
            rows = slice(block * ROWS, (block + 1) * ROWS)
            value_pack = pack_ref[block, 1].astype(F32)
            value_grad = jnp.where(real, value_pack, 0.0)
            grads_scr[rows, :LANES] = pack_ref[block, 0]
            for e in range(experts):
                gate = value_pack[:, head_dim + e : head_dim + e + 1]
                grads_scr[rows, LANES * (1 + e) : LANES * (2 + e)] = (gate * value_grad).astype(
                    BF16
                )
            grads_scr[rows, query:] = pack_ref[block, 2]
        return mm(grads_scr[...], weights)

    @pl.when(step == 0)
    def _():
        total_scr[...] = part(own_ref, w_own_ref[:cols, :])

    @pl.when(step == 1)
    def _():
        weights = w_far_ref[...].reshape(-1, w_far_ref.shape[2])
        total = total_scr[...] + part(far_ref, weights[:cols, :])
        out_refs[0][...] = total[:ROWS]
        out_refs[1][...] = total[ROWS:].astype(BF16)


def token_parts(own_pack, far_pack, own_w, far_w, head_dim, experts):
    width = own_w.shape[1]
    rows = 2 * ROWS
    cols = (2 + experts) * LANES
    return pl.pallas_call(
        functools.partial(token_kernel, experts, head_dim),
        grid=(2,),
        in_specs=[
            whole(*own_pack.shape),
            whole(*far_pack.shape),
            whole(*own_w.shape),
            whole(*far_w.shape),
        ],
        out_specs=[whole(ROWS, width)] * 2,
        out_shape=[struct((ROWS, width), F32), struct((ROWS, width), BF16)],
        scratch_shapes=[pltpu.VMEM((rows, cols), BF16), pltpu.VMEM((rows, width), F32)],
        compiler_params=params(),
        cost_estimate=cost(6),
        name="token_parts",
    )(own_pack, far_pack, own_w, far_w)


def token_sum_kernel(z_ref, tok_ref, mid_ref, gain_ref, own_ref, near_ref, out_ref):
    total = own_ref[...] + near_ref[...].astype(F32)
    normal, inv_std = norm_parts(tok_ref[...].astype(F32))
    out_ref[...] = mid_ref[...] + norm_back(total, normal, inv_std, gain_ref[...])


def token_sum(rank, tokens, middle_grad, gain, own, near):
    rows, width = middle_grad.shape
    return pl.pallas_call(
        token_sum_kernel,
        grid_spec=pltpu.PrefetchScalarGridSpec(
            num_scalar_prefetch=1,
            grid=(1,),
            in_specs=[
                pl.BlockSpec((rows, width), lambda i, z: (z[0], 0)),
                whole(rows, width),
                whole(1, width),
                whole(rows, width),
                whole(rows, width),
            ],
            out_specs=whole(rows, width),
        ),
        out_shape=struct((rows, width), F32),
        compiler_params=params(),
        cost_estimate=cost(4),
        name="token_sum",
    )(rank, tokens, middle_grad, gain, own, near)


def swap(array, axis, mask):
    size = lax.axis_size(axis)
    return lax.ppermute(array, axis, [(i, i ^ mask) for i in range(size)])


def plus(left, right):
    return (left.astype(F32) + right.astype(F32)).astype(BF16)


def scatter_first(keep, far):
    return [plus(keep[m], far[m]) for m in range(keep.shape[0])]


def scatter_sends(blocks, unit):
    return [swap(blocks[m], "dp", 2 * m * unit) for m in range(1, len(blocks))]


def scatter_done(own, fars, unit, axis):
    out = own.astype(F32)
    for far in fars:
        out = out + far.astype(F32)
    mask = unit // 2
    while mask:
        size = out.shape[axis] // 2
        bit = (lax.axis_index("dp") // mask) % 2
        mine = lax.dynamic_slice_in_dim(out, bit * size, size, axis)
        theirs = lax.dynamic_slice_in_dim(out, (1 - bit) * size, size, axis)
        out = mine + swap(theirs.astype(BF16), "dp", mask).astype(F32)
        mask //= 2
    return out


def spread(far, *gates):
    pieces = [swap(far, "dp", 2 * m) for m in range(1, GROUP // 2)]
    even = after(pile(far, *pieces), *gates)
    odd = swap(even, "dp", 1)
    return even, odd


def on_device(
    tokens,
    memory,
    segments,
    value_routes,
    output_routes,
    first_gain,
    first_bias,
    second_gain,
    second_bias,
    query_head_weight,
    key_weight,
    position_weight,
    value_weight,
    value_select,
    output_expert_selector,
    output_expert_weight,
    content_bias,
    position_bias,
    up_projection_weight,
    down_projection_weight,
    cotangent,
):
    mem_len = memory.shape[1]
    toks, width = tokens.shape
    head_dim = query_head_weight.shape[2]
    experts = value_select.shape[2]
    hidden = up_projection_weight.shape[1]
    parts = lax.axis_size("tensor")
    rank = lax.axis_index("tensor")
    dp = lax.axis_size("dp")
    at = lax.axis_index("dp")
    others = range(1, parts)
    near, far_shard = 1, 2
    rank_ref = rank.reshape(1).astype(jnp.int32)
    row = lambda v: v.reshape(1, -1)
    lanes = lambda v: jnp.pad(v, ((0, 0), (0, LANES - head_dim)))

    own_out = output_expert_weight[0]
    size = width // GROUP
    own_block = lax.dynamic_slice_in_dim(own_out, (at % GROUP) * size, size, 1)
    far_out = swap(own_block, "tensor", far_shard)
    span = mem_len
    fine = 32
    rates = jnp.exp(jnp.arange(width // 2).astype(F32) * (-2.0 * math.log(10000.0) / width))
    coarse_at = (span - 1 - fine * jnp.arange(span // fine)).astype(F32)[:, None] * rates[None, :]
    fine_at = jnp.arange(fine).astype(F32)[:, None] * rates[None, :]
    sin_a, cos_a = jnp.sin(coarse_at)[:, None, :], jnp.cos(coarse_at)[:, None, :]
    sin_b, cos_b = jnp.sin(fine_at)[None, :, :], jnp.cos(fine_at)[None, :, :]
    sin_table = jnp.concatenate(
        [sin_a * cos_b - cos_a * sin_b, cos_a * cos_b + sin_a * sin_b], axis=2
    )
    sin_table = lax.optimization_barrier(sin_table.reshape(span, width).astype(BF16))
    rel_weight = jnp.concatenate(
        [position_weight[0].T, jnp.zeros((LANES - head_dim, width), BF16)]
    )
    rel_reverse = mm_nt(sin_table, rel_weight).astype(BF16)

    w_all, normed, key_vecs, value_vecs, every, vgate, qc, qp, ogate = project(
        memory[0],
        tokens,
        row(first_gain),
        row(first_bias),
        (
            key_weight[0].T,
            value_select[0].T,
            value_weight[0].T,
            query_head_weight[0].T,
            output_expert_selector[0].T,
        ),
        value_routes[0, :, 0].T,
        output_routes[:, 0].T,
        lanes(content_bias),
        lanes(position_bias),
        experts,
        head_dim,
    )
    steps = toks // ROWS
    seg = segments[0]
    seg_keys = jnp.stack([seg[i * ROWS : i * ROWS + span + ROWS] for i in range(steps)])[:, None]
    seg_keys = after(seg_keys, far_out)
    heads, probs, *packs = attend(
        rank_ref,
        qc,
        qp,
        key_vecs,
        value_vecs,
        rel_reverse,
        seg_keys,
        seg[mem_len:, None],
        ogate,
        head_dim,
    )

    depth = width // dp
    feed_piece = jnp.stack(
        [
            lax.dynamic_slice_in_dim(up_projection_weight, at * depth, depth, 0),
            lax.dynamic_slice_in_dim(down_projection_weight, at * (hidden // dp), hidden // dp, 0),
        ]
    )
    far_feed = swap(feed_piece, "tensor", far_shard)
    far_feed = lax.all_gather(after(far_feed, packs[0]), "dp", axis=0)
    packs = [packs[0], swap(packs[1], "tensor", far_shard)]
    even, odd = spread(after(far_out, qc), packs[1])
    cots = [cotangent, swap(after(cotangent, packs[1]), "tensor", near)]
    piece = w_all.shape[0] // dp
    own_piece = lax.dynamic_slice_in_dim(w_all, at * piece, piece, 0)
    far_w = swap(after(own_piece, packs[1]), "tensor", far_shard)
    group_at = at % GROUP
    where = jnp.stack([group_at // 2, group_at % 2, rank]).astype(jnp.int32)
    full, own_part, near_part = mix(where, packs, own_out, even, odd, experts, head_dim)
    middle, up_in = middle_rows(
        rank_ref,
        tokens,
        after(own_part, far_w, cots[1]),
        swap(near_part, "tensor", near),
        row(second_gain),
        row(second_bias),
    )

    ups = [up_in, swap(up_in, "tensor", near)]
    unit = dp // GROUP
    where_grads = jnp.stack([at // unit, rank]).astype(jnp.int32)
    far_w = lax.all_gather(after(far_w, up_in), "dp", axis=0)
    shards = (up_projection_weight, down_projection_weight, far_feed)
    own_hidden, own_pre, own_result, own_up = feed(ups[0], cots[0], *shards, F32)
    near_hidden, near_pre, near_result, near_up = feed(ups[1], cots[1], *shards, BF16, own_pre)
    back_up = swap(near_up, "tensor", near)
    feed_sums = feed_weights(ups, cots, (own_pre, near_pre), (own_hidden, near_hidden))
    feed_sums = after(feed_sums, far_w, back_up)
    back_out = swap(near_result, "tensor", near)
    own_up = after(own_up, feed_sums)
    feed_sums = lax.psum_scatter(feed_sums, "dp", scatter_dimension=0, tiled=True)

    middle_grad, attn_grad, sums_two = middle_back(
        own_up, back_up, cotangent, middle, row(second_gain)
    )
    near_grad = swap(attn_grad, "tensor", near)
    backs = heads_back(attn_grad, near_grad, full, packs, experts, head_dim)
    out_keep, out_send = out_weights(where_grads, packs, attn_grad, near_grad, experts, head_dim)
    backs = [after(backs[0], out_keep), swap(backs[1], "tensor", far_shard)]

    key_grad, value_grad, query_grad, rel_grad, bias_sums, *grad_packs = attend_back(
        rank_ref,
        qc,
        qp,
        key_vecs,
        value_vecs,
        rel_reverse,
        probs,
        heads,
        ogate,
        every,
        vgate,
        backs,
        head_dim,
    )
    out_part = scatter_first(out_keep, swap(out_send, "dp", unit))
    rel_grad = after(rel_grad, *out_part)
    out_fars = scatter_sends(out_part, unit)
    far_pack = swap(grad_packs[1], "tensor", far_shard)
    keep, send, small = weight_grads(
        where_grads,
        normed,
        key_grad,
        value_grad,
        vgate,
        query_grad,
        sin_table,
        rel_grad,
        w_all,
        row(first_gain),
        row(first_bias),
        sums_two,
        bias_sums,
        mem_len,
        head_dim,
        experts,
    )
    kept_far = swap(send, "dp", unit)
    small_fars = [swap(small, "tensor", m) for m in others]
    out_fars = [after(far, keep) for far in out_fars]
    out_sums = scatter_done(out_part[0], out_fars, unit, 1).reshape(2, experts * head_dim, -1)
    out_low = out_sums[1].astype(BF16)
    out_far = swap(out_low, "tensor", far_shard)
    token_own, token_near = token_parts(
        grad_packs[0], far_pack, w_all, after(far_w, keep, out_low), head_dim, experts
    )
    feed_own, feed_far = feed_sums[:, : 2 * hidden], feed_sums[:, 2 * hidden :]
    kept_far, token_near, feed_far, out_far, *small_fars = together(
        kept_far, token_near, feed_far, out_far, *small_fars
    )
    feed_far = swap(feed_far, "tensor", far_shard)
    token_near = swap(token_near, "tensor", near)
    kept = scatter_first(keep, kept_far)
    kept_fars = scatter_sends(kept, unit)
    for far in small_fars:
        small = small + far
    small_fars = [swap(small, "dp", m) for m in range(2, GROUP, 2)]
    feed_far, *fars = together(feed_far, *kept_fars, *small_fars)
    kept_fars, small_fars = fars[: len(fars) // 2], fars[len(fars) // 2 :]
    for far in small_fars:
        small = small + far
    mask = GROUP
    while mask < dp:
        small = small + swap(small, "dp", mask)
        mask *= 2
    small = small + swap(small, "dp", 1)
    kept = scatter_done(kept[0], kept_fars, unit, 1)
    tokens_grad = token_sum(
        rank_ref, tokens, middle_grad, row(first_gain), token_own, token_near
    )
    result = (middle + own_result + after(back_out, keep).astype(F32)).astype(BF16)
    out_w = out_sums[0] + out_far.astype(F32)
    feed_grads = feed_own.astype(F32) + feed_far.astype(F32)
    up_total = feed_grads[:, :hidden]
    down_total = feed_grads[:, hidden:].T
    biases = small[4:6, : parts * LANES].reshape(2, parts, LANES)[:, :, :head_dim]
    marks = [0, 1, 1 + experts, 2 + experts, 3 + experts]
    key_w, value_w, query_w, rel_w = (
        kept[a * head_dim : b * head_dim] for a, b in zip(marks, marks[1:])
    )
    select = marks[-1] * head_dim
    turn = lambda part: part.T[None]
    return (
        result,
        tokens_grad,
        small[0],
        small[1],
        small[2],
        small[3],
        turn(query_w),
        turn(key_w),
        turn(rel_w),
        turn(value_w),
        turn(kept[select : select + experts]),
        turn(kept[select + 8 : select + 8 + experts]),
        out_w[None],
        biases[0],
        biases[1],
        up_total,
        down_total,
    )


def solution(mesh):
    placed = (
        P("dp", None),
        P("dp", None, None),
        P("dp", None),
        P("dp", None, "tensor", None),
        P("dp", "tensor", None),
        P(),
        P(),
        P(),
        P(),
        P("tensor", None, None),
        P("tensor", None, None),
        P("tensor", None, None),
        P("tensor", None, None),
        P("tensor", None, None),
        P("tensor", None, None),
        P("tensor", None, None),
        P("tensor", None),
        P("tensor", None),
        P(None, "tensor"),
        P("tensor", None),
        P(("dp", "tensor"), None),
    )
    return jax.shard_map(
        on_device,
        mesh=mesh,
        in_specs=placed,
        out_specs=(
            P(("dp", "tensor"), None),
            P(("dp", "tensor"), None),
            P(),
            P(),
            P(),
            P(),
            P("tensor", "dp", None),
            P("tensor", "dp", None),
            P("tensor", "dp", None),
            P("tensor", "dp", None),
            P("tensor", "dp", None),
            P("tensor", "dp", None),
            P("tensor", None, "dp"),
            P(),
            P(),
            P("dp", "tensor"),
            P("tensor", "dp"),
        ),
        check_vma=False,
    )
```

```python
import functools
import math

import jax
import jax.numpy as jnp
from jax import lax
from jax.experimental import pallas as pl
from jax.experimental.pallas import tpu as pltpu
from jax.sharding import PartitionSpec as P

EPSILON = 1e-05
ROOT_HALF = 0.7071067811865476
INVERSE_ROOT_TAU = 0.3989422804014327
ROWS = 256
GROUP = 8
MIB = 1024 * 1024
BF16 = jnp.bfloat16
F32 = jnp.float32


def mm(left, right):
    return jnp.dot(left, right, preferred_element_type=F32)


def mm_nt(left, right):
    return lax.dot_general(left, right, (((1,), (1,)), ((), ())), preferred_element_type=F32)


def mm_tn(left, right):
    return lax.dot_general(left, right, (((0,), (0,)), ((), ())), preferred_element_type=F32)


def norm_parts(values):
    center = values - jnp.mean(values, axis=-1, keepdims=True)
    inv_std = lax.rsqrt(jnp.mean(center * center, axis=-1, keepdims=True) + EPSILON)
    return center * inv_std, inv_std


def norm_back(upstream, normal, inv_std, gain):
    scaled = upstream * gain
    return inv_std * (
        scaled
        - jnp.mean(scaled, axis=-1, keepdims=True)
        - normal * jnp.mean(scaled * normal, axis=-1, keepdims=True)
    )


def params():
    return pltpu.CompilerParams(vmem_limit_bytes=63 * MIB)


def cost(microseconds):
    return pl.CostEstimate(
        flops=int(microseconds * 1.15e9), bytes_accessed=0, transcendentals=0
    )


def struct(shape, dtype):
    return jax.ShapeDtypeStruct(shape, dtype)


def whole(*shape):
    return pl.BlockSpec(shape, lambda *_: (0,) * len(shape))

LANES = 128


def lane_of(rows):
    return lax.broadcasted_iota(jnp.int32, (rows, LANES), 1)


def picked(routes, head_dim):
    rows = routes.shape[1]
    routes = jnp.concatenate([routes, jnp.zeros((6, rows), jnp.int32)], axis=0).astype(F32).T
    lane = (lane_of(rows) - head_dim).astype(F32)
    return (lane == routes[:, 0:1]) | (lane == routes[:, 1:2])


def after(array, *deps, span=0):
    def body(*refs):
        del refs

    spec = pl.BlockSpec(memory_space=pl.ANY)
    return pl.pallas_call(
        body,
        in_specs=[spec] * (1 + len(deps)),
        out_specs=spec,
        out_shape=struct(array.shape, array.dtype),
        input_output_aliases={0: 0},
        cost_estimate=cost(span),
        name="after",
    )(array, *deps)


def together(*arrays, span=0):
    def body(*refs):
        del refs

    spec = pl.BlockSpec(memory_space=pl.ANY)
    return pl.pallas_call(
        body,
        in_specs=[spec] * len(arrays),
        out_specs=[spec] * len(arrays),
        out_shape=[struct(a.shape, a.dtype) for a in arrays],
        input_output_aliases={i: i for i in range(len(arrays))},
        cost_estimate=cost(span),
        name="together",
    )(*arrays)


def pile(*arrays):
    def body(*refs):
        for i, ref in enumerate(refs[:-1]):
            refs[-1][i] = ref[...]

    shape = arrays[0].shape
    return pl.pallas_call(
        body,
        in_specs=[whole(*shape)] * len(arrays),
        out_specs=whole(len(arrays), *shape),
        out_shape=struct((len(arrays),) + shape, arrays[0].dtype),
        grid=(1,),
        compiler_params=params(),
        cost_estimate=cost(2),
        name="pile",
    )(*arrays)


def project_kernel(
    experts,
    head_dim,
    mem_steps,
    scale,
    mem_ref,
    tok_ref,
    gain_ref,
    bias_ref,
    key_w_ref,
    vsel_ref,
    value_w_ref,
    query_w_ref,
    osel_ref,
    vroute_ref,
    oroute_ref,
    cb_ref,
    pb_ref,
    w_out_ref,
    normed_ref,
    key_ref,
    val_ref,
    every_ref,
    vgate_ref,
    qc_ref,
    qp_ref,
    ogate_ref,
    w_ref,
):
    step = pl.program_id(0)
    query = (1 + experts) * LANES

    @pl.when(step == 0)
    def _():
        w_ref[...] = jnp.zeros_like(w_ref)
        w_ref[:head_dim, :] = key_w_ref[...]
        w_ref[head_dim : head_dim + experts, :] = vsel_ref[...]
        for e in range(experts):
            w_ref[(1 + e) * LANES : (1 + e) * LANES + head_dim, :] = value_w_ref[
                e * head_dim : (e + 1) * head_dim, :
            ]
        w_ref[query : query + head_dim, :] = query_w_ref[...]
        w_ref[query + head_dim : query + head_dim + experts, :] = osel_ref[...]

    size = w_out_ref.shape[0]
    w_out_ref[...] = w_ref[pl.ds(pl.multiple_of(step * size, size), size), :]

    def rows_part(rows_ref, columns, last):
        blocks = [slice(i * ROWS, (i + 1) * ROWS) for i in range(rows_ref.shape[0] // ROWS)]
        normed, outs = [], []
        for rows in blocks:
            normal, _ = norm_parts(rows_ref[rows, :].astype(F32))
            normed.append((normal * gain_ref[...] + bias_ref[...]).astype(BF16))
            outs.append(mm_nt(normed[-1], w_ref[:columns, :]))
        lane = lane_of(ROWS)
        real = lane < head_dim
        for rows, norm, out in zip(blocks, normed, outs):
            normed_ref[rows, :] = norm
            first = out[:, :LANES]
            key_ref[rows, :] = jnp.where(real, first, 0.0).astype(BF16)
            every_ref[rows, :] = out[:, LANES:query].astype(BF16)
            gate = jnp.where(picked(vroute_ref[:, rows], head_dim), jax.nn.sigmoid(first), 0.0)
            vgate_ref[rows, :] = gate
            value = jnp.zeros((ROWS, LANES), F32)
            for e in range(experts):
                value = value + gate[:, head_dim + e : head_dim + e + 1] * (
                    out[:, (1 + e) * LANES : (2 + e) * LANES]
                )
            val_ref[rows, :] = value.astype(BF16)
            if last:
                q = out[:, query:]
                qc_ref[rows, :] = jnp.where(real, (q + cb_ref[...]) * scale, 0.0).astype(BF16)
                qp_ref[rows, :] = jnp.where(real, (q + pb_ref[...]) * scale, 0.0).astype(BF16)
                ogate_ref[rows, :] = jnp.where(
                    picked(oroute_ref[:, rows], head_dim), jax.nn.sigmoid(q), 0.0
                )

    @pl.when(step < mem_steps)
    def _():
        rows_part(mem_ref, query, False)

    @pl.when(step >= mem_steps)
    def _():
        rows_part(tok_ref, query + LANES, True)


def project(memory, tokens, gain, bias, weights, vroutes, oroutes, cb, pb, experts, head_dim):
    mem, width = memory.shape
    toks = tokens.shape[0]
    big = 2 * ROWS
    mem_steps, tok_steps = mem // big, toks // big
    steps = mem_steps + tok_steps
    keys = mem + toks
    cols = width
    mem_row = lambda i: (jnp.minimum(i, mem_steps - 1), 0)
    tok_row = lambda i: (jnp.maximum(i - mem_steps, 0), 0)
    row = lambda i: (i, 0)
    return pl.pallas_call(
        functools.partial(project_kernel, experts, head_dim, mem_steps, head_dim ** (-0.5)),
        grid=(steps,),
        in_specs=[
            pl.BlockSpec((big, width), mem_row),
            pl.BlockSpec((big, width), tok_row),
            whole(1, width),
            whole(1, width),
        ]
        + [whole(*w.shape) for w in weights]
        + [
            pl.BlockSpec((vroutes.shape[0], big), lambda i: (0, i)),
            pl.BlockSpec((oroutes.shape[0], big), lambda i: (0, jnp.maximum(i - mem_steps, 0))),
            whole(1, LANES),
            whole(1, LANES),
        ],
        out_specs=[
            pl.BlockSpec((cols // steps, width), row),
            pl.BlockSpec((big, width), row),
            pl.BlockSpec((big, LANES), row),
            pl.BlockSpec((big, LANES), row),
            pl.BlockSpec((big, experts * LANES), row),
            pl.BlockSpec((big, LANES), row),
            pl.BlockSpec((big, LANES), tok_row),
            pl.BlockSpec((big, LANES), tok_row),
            pl.BlockSpec((big, LANES), tok_row),
        ],
        out_shape=[
            struct((cols, width), BF16),
            struct((keys, width), BF16),
            struct((keys, LANES), BF16),
            struct((keys, LANES), BF16),
            struct((keys, experts * LANES), BF16),
            struct((keys, LANES), F32),
            struct((toks, LANES), BF16),
            struct((toks, LANES), BF16),
            struct((toks, LANES), F32),
        ],
        scratch_shapes=[pltpu.VMEM((cols, width), BF16)],
        compiler_params=params(),
        cost_estimate=cost(12),
        name="project",
    )(memory, tokens, gain, bias, *weights, vroutes, oroutes, cb, pb)


def attend_kernel(
    span,
    head_dim,
    count,
    z_ref,
    qc_ref,
    qp_ref,
    key_ref,
    val_ref,
    rel_ref,
    segk_ref,
    segq_ref,
    ogate_ref,
    heads_ref,
    probs_ref,
    *pack_refs,
):
    step = pl.program_id(0)
    wide = span + ROWS
    column = lax.broadcasted_iota(jnp.int32, (ROWS, ROWS), 1)
    causal = column <= lax.broadcasted_iota(jnp.int32, (ROWS, ROWS), 0)
    for b in range(count):
        rows = slice(b * ROWS, (b + 1) * ROWS)
        window = pl.ds((step * count + b) * ROWS, wide)
        content = mm_nt(qc_ref[rows, :], key_ref[window, :])
        reverse = mm_nt(qp_ref[rows, :], rel_ref[...])
        reverse = jnp.concatenate([reverse, jnp.zeros((ROWS, ROWS), F32)], axis=1)
        scores = content + pltpu.roll(reverse, 1, 1, stride=1, stride_axis=0)
        same = segk_ref[b] == segq_ref[rows, :]
        allowed = jnp.concatenate([same[:, :span], same[:, span:] & causal], axis=1)
        scores = jnp.where(allowed, scores, -1e30)
        expo = jnp.exp(scores - jnp.max(scores, axis=1, keepdims=True))
        probs = (expo * (1.0 / jnp.sum(expo, axis=1, keepdims=True))).astype(BF16)
        probs_ref[rows, :] = probs
        heads = mm(probs, val_ref[window, :])
        heads_ref[rows, :] = heads
        packed = jnp.where(lane_of(ROWS) < head_dim, heads, ogate_ref[rows, :]).astype(BF16)
        slot = (step * count + b) ^ z_ref[0]
        for side, pack_ref in enumerate(pack_refs):

            @pl.when(slot // 2 == side)
            def _():
                pack_ref[slot % 2] = packed


def attend(rank, qc, qp, key_vecs, value_vecs, rel_reverse, seg_keys, seg_query, ogate, head_dim):
    toks = qc.shape[0]
    keys = key_vecs.shape[0]
    span = rel_reverse.shape[0]
    steps = toks // ROWS
    count = 2
    big = count * ROWS
    wide = span + ROWS
    row = lambda i, z: (i, 0)
    return pl.pallas_call(
        functools.partial(attend_kernel, span, head_dim, count),
        grid_spec=pltpu.PrefetchScalarGridSpec(
            num_scalar_prefetch=1,
            grid=(steps // count,),
            in_specs=[
                pl.BlockSpec((big, LANES), row),
                pl.BlockSpec((big, LANES), row),
                whole(keys, LANES),
                whole(keys, LANES),
                whole(span, LANES),
                pl.BlockSpec((count, 1, wide), lambda i, z: (i, 0, 0)),
                pl.BlockSpec((big, 1), row),
                pl.BlockSpec((big, LANES), row),
            ],
            out_specs=[
                pl.BlockSpec((big, LANES), row),
                pl.BlockSpec((big, wide), row),
            ]
            + [whole(2, ROWS, LANES)] * (steps // 2),
        ),
        out_shape=[struct((toks, LANES), F32), struct((toks, wide), BF16)]
        + [struct((2, ROWS, LANES), BF16)] * (steps // 2),
        compiler_params=params(),
        cost_estimate=cost(8),
        name="attend",
    )(rank, qc, qp, key_vecs, value_vecs, rel_reverse, seg_keys, seg_query, ogate)


def attend_back_kernel(
    span,
    experts,
    head_dim,
    parts,
    z_ref,
    qc_ref,
    qp_ref,
    key_ref,
    val_ref,
    rel_ref,
    probs_ref,
    heads_ref,
    ogate_ref,
    every_ref,
    vgate_ref,
    *refs,
):
    back_refs, refs = refs[: parts // 2], refs[parts // 2 :]
    key_grad_ref, value_grad_ref, query_grad_ref, rel_grad_ref, bias_ref = refs[:5]
    pack_refs, refs = refs[5 : 5 + parts // 2], refs[5 + parts // 2 :]
    keys_scr, values_scr, rel_scr, query_scr, back_scr = refs
    step = pl.program_id(0)
    steps = pl.num_programs(0)
    wide = span + ROWS
    mem = keys_scr.shape[0] - steps * ROWS
    scale = head_dim ** (-0.5)
    real = lane_of(ROWS) < head_dim

    @pl.when(step == 0)
    def _():
        keys_scr[...] = jnp.zeros_like(keys_scr)
        values_scr[...] = jnp.zeros_like(values_scr)
        rel_scr[...] = jnp.zeros_like(rel_scr)
        bias_ref[...] = jnp.zeros_like(bias_ref)

    slot = step ^ z_ref[0]
    for side, back_ref in enumerate(back_refs):

        @pl.when(slot // 2 == side)
        def _():
            back_scr[...] = back_ref[slot % 2]

    window = pl.ds(step * ROWS, wide)
    keys = key_ref[window, :]
    vals = val_ref[window, :]
    back = back_scr[...].astype(F32)
    out_grad = jnp.where(real, back, 0.0)
    delta = jnp.sum(out_grad * heads_ref[...], axis=1, keepdims=True)
    out_grad = out_grad.astype(BF16)
    probs = probs_ref[...]
    probs_grad = mm_nt(out_grad, vals)
    score_grad = (probs.astype(F32) * (probs_grad - delta)).astype(BF16)
    content_grad = mm(score_grad, keys).astype(BF16).astype(F32) * scale
    keys_scr[window, :] += mm_tn(score_grad, qc_ref[...])
    values_scr[window, :] += mm_tn(probs, out_grad)
    flip = (
        lax.broadcasted_iota(jnp.int32, (ROWS, ROWS), 0)
        + lax.broadcasted_iota(jnp.int32, (ROWS, ROWS), 1)
        == ROWS - 1
    ).astype(BF16)
    turned = mm(flip, score_grad)
    turned = pltpu.roll(turned, span, 1, stride=1, stride_axis=0)[:, :span].astype(BF16)
    place_grad = mm(turned, rel_ref[...]).astype(BF16)
    position_grad = mm(flip, place_grad) * scale
    rel_scr[...] += mm_tn(turned, mm(flip, qp_ref[...]).astype(BF16))
    bias_ref[0:1, :] += jnp.sum(content_grad, axis=0, keepdims=True)
    bias_ref[1:2, :] += jnp.sum(position_grad, axis=0, keepdims=True)
    gate = ogate_ref[...]
    query_grad = jnp.where(real, content_grad + position_grad, back * gate * (1.0 - gate))
    query_grad = query_grad.astype(BF16)
    query_grad_ref[...] = query_grad
    query_scr[pl.ds(step * ROWS, ROWS), :] = query_grad

    @pl.when(step == steps - 1)
    def _():
        rel_grad_ref[...] = rel_scr[...].astype(BF16)

        @pl.loop(0, (mem + steps * ROWS) // ROWS)
        def _(block):
            rows = pl.ds(block * ROWS, ROWS)
            value_grad = values_scr[rows, :]
            gates = vgate_ref[rows, :]
            value_grad_ref[rows, :] = value_grad
            logit = keys_scr[rows, :]
            lane = lane_of(ROWS)
            for e in range(experts):
                part = every_ref[rows, e * LANES : (e + 1) * LANES].astype(F32)
                total = jnp.sum(value_grad * part, axis=1, keepdims=True)
                logit = jnp.where(lane == head_dim + e, total, logit)
            key_grad = jnp.where(real, logit, logit * gates * (1.0 - gates)).astype(BF16)
            key_grad_ref[rows, :] = key_grad

            @pl.when(block * ROWS >= mem)
            def _():
                place = block - mem // ROWS
                slot = place ^ z_ref[0]
                value_pack = jnp.where(real, value_grad, gates).astype(BF16)
                for side, pack_ref in enumerate(pack_refs):

                    @pl.when(slot // 2 == side)
                    def _():
                        pack_ref[slot % 2, 0] = key_grad
                        pack_ref[slot % 2, 1] = value_pack
                        pack_ref[slot % 2, 2] = query_scr[pl.ds(place * ROWS, ROWS), :]


def attend_back(
    rank,
    qc,
    qp,
    key_vecs,
    value_vecs,
    rel_reverse,
    probs,
    heads,
    ogate,
    every,
    vgate,
    backs,
    head_dim,
):
    toks = qc.shape[0]
    keys = key_vecs.shape[0]
    span = rel_reverse.shape[0]
    steps = toks // ROWS
    wide = span + ROWS
    experts = every.shape[1] // LANES
    row = lambda i, z: (i, 0)
    return pl.pallas_call(
        functools.partial(attend_back_kernel, span, experts, head_dim, steps),
        grid_spec=pltpu.PrefetchScalarGridSpec(
            num_scalar_prefetch=1,
            grid=(steps,),
            in_specs=[
                pl.BlockSpec((ROWS, LANES), row),
                pl.BlockSpec((ROWS, LANES), row),
                whole(keys, LANES),
                whole(keys, LANES),
                whole(span, LANES),
                pl.BlockSpec((ROWS, wide), row),
                pl.BlockSpec((ROWS, LANES), row),
                pl.BlockSpec((ROWS, LANES), row),
                whole(keys, experts * LANES),
                whole(keys, LANES),
            ]
            + [whole(2, ROWS, LANES)] * (steps // 2),
            out_specs=[
                whole(keys, LANES),
                whole(keys, LANES),
                pl.BlockSpec((ROWS, LANES), row),
                whole(span, LANES),
                whole(2, LANES),
            ]
            + [whole(2, 3, ROWS, LANES)] * (steps // 2),
            scratch_shapes=[
                pltpu.VMEM((keys, LANES), F32),
                pltpu.VMEM((keys, LANES), F32),
                pltpu.VMEM((span, LANES), F32),
                pltpu.VMEM((toks, LANES), BF16),
                pltpu.VMEM((ROWS, LANES), BF16),
            ],
        ),
        out_shape=[
            struct((keys, LANES), BF16),
            struct((keys, LANES), F32),
            struct((toks, LANES), BF16),
            struct((span, LANES), BF16),
            struct((2, LANES), F32),
        ]
        + [struct((2, 3, ROWS, LANES), BF16)] * (steps // 2),
        compiler_params=params(),
        cost_estimate=cost(15),
        name="attend_back",
    )(rank, qc, qp, key_vecs, value_vecs, rel_reverse, probs, heads, ogate, every, vgate, *backs)


def mix_kernel(experts, head_dim, where_ref, *refs):
    pack_refs, refs = refs[:2], refs[2:]
    own_ref, even_ref, odd_ref, full_ref, own_part_ref, near_part_ref, mixed_scr = refs
    step = pl.program_id(0)

    @pl.when(step == 0)
    def _():
        real = lane_of(ROWS) < head_dim
        for h in range(2):
            for block in range(2):
                pack = pack_refs[h][block].astype(F32)
                out = jnp.where(real, pack, 0.0)
                rows = slice(block * ROWS, (block + 1) * ROWS)
                for e in range(experts):
                    gate = pack[:, head_dim + e : head_dim + e + 1]
                    mixed_scr[h, rows, e * LANES : (e + 1) * LANES] = (gate * out).astype(BF16)

    turned = where_ref[1] == 1
    even, odd = even_ref[0], odd_ref[0]
    far = jnp.concatenate([jnp.where(turned, odd, even), jnp.where(turned, even, odd)], axis=1)
    total = None
    for h, weight in enumerate((own_ref[...], far)):
        for e in range(experts):
            full_ref[h, e * LANES : e * LANES + head_dim, :] = weight[
                e * head_dim : (e + 1) * head_dim
            ]
            full_ref[h, e * LANES + head_dim : (e + 1) * LANES, :] = jnp.zeros(
                (LANES - head_dim, weight.shape[1]), BF16
            )
        part = mm(mixed_scr[h], full_ref[h])
        total = part if total is None else total + part
    own_part_ref[...] = total[:ROWS]
    near_part_ref[...] = total[ROWS:].astype(BF16)


def mix(where, packs, own_weight, even, odd, experts, head_dim):
    depth, width = own_weight.shape
    steps = even.shape[0]
    size = width // steps
    column = lambda s, w: (0, w[0] ^ s)
    return pl.pallas_call(
        functools.partial(mix_kernel, experts, head_dim),
        grid_spec=pltpu.PrefetchScalarGridSpec(
            num_scalar_prefetch=1,
            grid=(steps,),
            in_specs=[whole(2, ROWS, LANES)] * 2
            + [
                pl.BlockSpec((depth, size), column),
                pl.BlockSpec((1,) + even.shape[1:], lambda s, w: (s, 0, 0)),
                pl.BlockSpec((1,) + odd.shape[1:], lambda s, w: (s, 0, 0)),
            ],
            out_specs=[
                pl.BlockSpec((2, experts * LANES, size), lambda s, w: (0, 0, w[0] ^ s)),
                pl.BlockSpec((ROWS, size), column),
                pl.BlockSpec((ROWS, size), column),
            ],
            scratch_shapes=[pltpu.VMEM((2, 2 * ROWS, experts * LANES), BF16)],
        ),
        out_shape=[
            struct((2, experts * LANES, width), BF16),
            struct((ROWS, width), F32),
            struct((ROWS, width), BF16),
        ],
        compiler_params=params(),
        cost_estimate=cost(7),
        name="mix",
    )(where, *packs, own_weight, even, odd)


def middle_kernel(z_ref, tok_ref, own_ref, near_ref, gain_ref, bias_ref, middle_ref, up_ref):
    middle = tok_ref[...].astype(F32) + (own_ref[...] + near_ref[...].astype(F32))
    middle_ref[...] = middle
    normal, _ = norm_parts(middle)
    up_ref[...] = (normal * gain_ref[...] + bias_ref[...]).astype(BF16)


def middle_rows(rank, tokens, own, near, gain, bias):
    rows, width = own.shape
    steps = 2
    block = pl.BlockSpec((rows // steps, width), lambda i, z: (i, 0))
    return pl.pallas_call(
        middle_kernel,
        grid_spec=pltpu.PrefetchScalarGridSpec(
            num_scalar_prefetch=1,
            grid=(steps,),
            in_specs=[
                pl.BlockSpec((rows // steps, width), lambda i, z: (z[0] * steps + i, 0)),
                block,
                block,
                whole(1, width),
                whole(1, width),
            ],
            out_specs=[block, block],
        ),
        out_shape=[struct((rows, width), F32), struct((rows, width), BF16)],
        compiler_params=params(),
        cost_estimate=cost(3),
        name="middle",
    )(rank, tokens, own, near, gain, bias)


def middle_back_kernel(
    own_ref, near_ref, cot_ref, middle_ref, gain_ref, grad_ref, low_ref, sums_ref
):
    upstream = own_ref[...].astype(F32) + near_ref[...].astype(F32)
    normal, inv_std = norm_parts(middle_ref[...])

    @pl.when(pl.program_id(0) == 0)
    def _():
        sums_ref[...] = jnp.zeros_like(sums_ref)

    sums_ref[0:1, :] += jnp.sum(upstream * normal, axis=0, keepdims=True)
    sums_ref[1:2, :] += jnp.sum(upstream, axis=0, keepdims=True)
    grad = cot_ref[...].astype(F32) + norm_back(upstream, normal, inv_std, gain_ref[...])
    grad_ref[...] = grad
    low_ref[...] = grad.astype(BF16)


def middle_back(own, near, cot, middle, gain):
    rows, width = middle.shape
    steps = 2
    block = pl.BlockSpec((rows // steps, width), lambda i: (i, 0))
    return pl.pallas_call(
        middle_back_kernel,
        grid=(steps,),
        in_specs=[block] * 4 + [whole(1, width)],
        out_specs=[block, block, whole(2, width)],
        out_shape=[
            struct((rows, width), F32),
            struct((rows, width), BF16),
            struct((2, width), F32),
        ],
        compiler_params=params(),
        cost_estimate=cost(4),
        name="middle_back",
    )(own, near, cot, middle, gain)


def heads_back_kernel(experts, head_dim, own_ref, near_ref, full_ref, *refs):
    pack_refs, out_refs = refs[:2], refs[2:]
    lane = lane_of(ROWS)
    real = lane < head_dim
    grads = [mm_nt(ref[...], full_ref[0]) for ref in (own_ref, near_ref)]
    for h in range(2):

        @pl.when(pl.program_id(0) == h)
        def _():
            for block, grad in enumerate(grads):
                grad = grad.astype(BF16).astype(F32)
                pack = pack_refs[h][block].astype(F32)
                total = jnp.zeros((ROWS, LANES), F32)
                gates = jnp.zeros((ROWS, LANES), F32)
                for e in range(experts):
                    part = grad[:, e * LANES : (e + 1) * LANES]
                    total = total + pack[:, head_dim + e : head_dim + e + 1] * part
                    inner = jnp.sum(part * pack, axis=1, keepdims=True)
                    gates = jnp.where(lane == head_dim + e, inner, gates)
                out_refs[h][block] = jnp.where(real, total, gates).astype(BF16)


def heads_back(own, near, full, packs, experts, head_dim):
    heads, depth, width = full.shape
    rows = own.shape[0]
    return pl.pallas_call(
        functools.partial(heads_back_kernel, experts, head_dim),
        grid=(heads,),
        in_specs=[whole(rows, width)] * 2
        + [pl.BlockSpec((1, depth, width), lambda m: (m, 0, 0))]
        + [whole(2, ROWS, LANES)] * 2,
        out_specs=[whole(2, ROWS, LANES)] * 2,
        out_shape=[struct((2, ROWS, LANES), BF16)] * 2,
        compiler_params=params(),
        cost_estimate=cost(6),
        name="heads_back",
    )(own, near, full, *packs)


def feed_kernel(half, up_ref, cot_ref, wu_ref, wd_ref, far_u_ref, far_d_ref, *refs):
    refs = refs[-6:]
    hidden_ref, pre_grad_ref, out_ref, up_grad_ref, out_scr, up_scr = refs
    step = pl.program_id(0)
    steps = pl.num_programs(0)
    width = up_ref.shape[1]
    count = wu_ref.shape[1] // ROWS

    @pl.when(step == 0)
    def _():
        out_scr[...] = jnp.zeros_like(out_scr)
        up_scr[...] = jnp.zeros_like(up_scr)

    def part(w_up, w_down):
        pres, grads = [], []
        for b in range(count):
            cols = slice(b * ROWS, (b + 1) * ROWS)
            pres.append(mm(up_ref[...], w_up[:, cols]))
            grads.append(mm_nt(cot_ref[...], w_down[cols, :]))
        out, up_grad = None, None
        for b in range(count):
            cols = slice(b * ROWS, (b + 1) * ROWS)
            pre = pres[b]
            hidden_grad = grads[b].astype(BF16).astype(F32)
            phi = 0.5 * (1.0 + lax.erf(pre * ROOT_HALF))
            hidden = (pre * phi).astype(BF16)
            slope = phi + pre * jnp.exp(-0.5 * pre * pre) * INVERSE_ROOT_TAU
            pre_grad = (hidden_grad * slope).astype(BF16)
            hidden_ref[:, cols] = hidden
            pre_grad_ref[:, cols] = pre_grad
            out_part, up_part = mm(hidden, w_down[cols, :]), mm_nt(pre_grad, w_up[:, cols])
            out = out_part if out is None else out + out_part
            up_grad = up_part if up_grad is None else up_grad + up_part
        out_scr[...] += out
        up_scr[...] += up_grad

    @pl.when(step < half)
    def _():
        part(wu_ref[...], wd_ref[...])

    @pl.when(step >= half)
    def _():
        part(far_u_ref[...].reshape(width, -1), far_d_ref[...].reshape(-1, width))

    @pl.when(step == steps - 1)
    def _():
        out_ref[...] = out_scr[...].astype(out_ref.dtype)
        up_grad_ref[...] = up_scr[...].astype(up_grad_ref.dtype)


def feed(up_in, cot, w_up, w_down, far, dtype, *deps):
    rows, width = up_in.shape
    hidden = w_up.shape[1]
    size = 2 * ROWS
    half = hidden // size
    pieces, _, depth, _ = far.shape
    count = size // depth
    own = lambda i: jnp.minimum(i, half - 1)
    other = lambda i: jnp.maximum(i - half, 0)
    return pl.pallas_call(
        functools.partial(feed_kernel, half),
        grid=(2 * half,),
        in_specs=[
            whole(rows, width),
            whole(rows, width),
            pl.BlockSpec((width, size), lambda i: (0, own(i))),
            pl.BlockSpec((size, width), lambda i: (own(i), 0)),
            pl.BlockSpec((pieces, 1, depth, size), lambda i: (0, 0, 0, other(i))),
            pl.BlockSpec((count, 1, depth, width), lambda i: (other(i), 1, 0, 0)),
        ]
        + [pl.BlockSpec(memory_space=pl.ANY)] * len(deps),
        out_specs=[
            pl.BlockSpec((rows, size), lambda i: (0, i)),
            pl.BlockSpec((rows, size), lambda i: (0, i)),
            whole(rows, width),
            whole(rows, width),
        ],
        out_shape=[
            struct((rows, 2 * hidden), BF16),
            struct((rows, 2 * hidden), BF16),
            struct((rows, width), dtype),
            struct((rows, width), dtype),
        ],
        scratch_shapes=[pltpu.VMEM((rows, width), F32), pltpu.VMEM((rows, width), F32)],
        compiler_params=params(),
        cost_estimate=cost(10),
        name="feed",
    )(up_in, cot, w_up, w_down, far, far, *deps)


def feed_weights_kernel(count, half, *refs):
    lefts, refs = refs[: 2 * count], refs[2 * count :]
    rights, out_ref = refs[: 2 * count], refs[2 * count]
    step = pl.program_id(0)

    for which in range(2):

        @pl.when((step // half) % 2 == which)
        def _():
            total = None
            for m in range(which * count, (which + 1) * count):
                part = mm_tn(lefts[m][...], rights[m][...])
                total = part if total is None else total + part
            out_ref[...] = total.astype(BF16)


def feed_weights(ups, cots, pre_grads, hiddens):
    count = len(ups)
    rows, width = ups[0].shape
    hidden = hiddens[0].shape[1] // 2
    size = 512
    half = hidden // size

    def columns(which):
        def at(i):
            shard, inner = i // (2 * half), i % (2 * half)
            return (0, shard * half + jnp.clip(inner - which * half, 0, half - 1))

        return pl.BlockSpec((rows, size), at)

    return pl.pallas_call(
        functools.partial(feed_weights_kernel, count, half),
        grid=(4 * half,),
        in_specs=[whole(rows, width)] * (2 * count)
        + [columns(0)] * count
        + [columns(1)] * count,
        out_specs=pl.BlockSpec((width, size), lambda i: (0, i)),
        out_shape=struct((width, 4 * hidden), BF16),
        compiler_params=params(),
        cost_estimate=cost(11),
        name="feed_weights",
    )(*ups, *cots, *pre_grads, *hiddens)


def out_weights_kernel(experts, head_dim, heads, where_ref, *refs):
    pack_refs, refs = refs[:heads], refs[heads:]
    grad_ref, near_grad_ref, keep_ref, send_ref, mixed_scr, scr = refs
    real = lane_of(ROWS) < head_dim

    def fill(begin, pack):
        pack = pack.astype(F32)
        out = jnp.where(real, pack, 0.0)
        for e in range(experts):
            gate = pack[:, head_dim + e : head_dim + e + 1]
            mixed_scr[begin : begin + ROWS, e * LANES : (e + 1) * LANES] = (gate * out).astype(
                BF16
            )

    for m in range(heads):

        @pl.when(pl.program_id(0) == m)
        def _():
            fill(0, pack_refs[m][0])
            fill(ROWS, pack_refs[m][1])

    scr[...] = mm_tn(mixed_scr[:ROWS], grad_ref[...]) + mm_tn(
        mixed_scr[ROWS:], near_grad_ref[...]
    )
    for k in range(GROUP):
        target = send_ref if k % 2 else keep_ref
        lanes = pl.ds(pl.multiple_of((where_ref[0] ^ k) * LANES, LANES), LANES)
        for e in range(experts):
            target[k // 2, e * head_dim : (e + 1) * head_dim, :] = scr[
                e * LANES : e * LANES + head_dim, lanes
            ].astype(BF16)


def out_weights(where, packs, grad, near_grad, experts, head_dim):
    heads = len(packs)
    rows, width = grad.shape
    depth = experts * head_dim
    shape = (GROUP // 2, heads * depth, width // GROUP)
    spec = pl.BlockSpec((GROUP // 2, depth, width // GROUP), lambda m, w: (0, m, 0))
    return pl.pallas_call(
        functools.partial(out_weights_kernel, experts, head_dim, heads),
        grid_spec=pltpu.PrefetchScalarGridSpec(
            num_scalar_prefetch=1,
            grid=(heads,),
            in_specs=[whole(2, rows, LANES)] * heads + [whole(rows, width)] * 2,
            out_specs=[spec] * 2,
            scratch_shapes=[
                pltpu.VMEM((2 * rows, experts * LANES), BF16),
                pltpu.VMEM((experts * LANES, width), F32),
            ],
        ),
        out_shape=[struct(shape, BF16)] * 2,
        compiler_params=params(),
        cost_estimate=cost(5),
        name="out_weights",
    )(where, *packs, grad, near_grad)


def weights_kernel(
    experts,
    head_dim,
    counts,
    where_ref,
    normed_ref,
    key_ref,
    value_ref,
    gate_ref,
    query_ref,
    table_ref,
    rel_ref,
    w_ref,
    gain_ref,
    bias_ref,
    sums_ref,
    biases_ref,
    keep_ref,
    send_ref,
    small_ref,
    grads_scr,
    sum_scr,
    main_scr,
    rel_scr,
):
    step = pl.program_id(0)
    mem_steps, key_steps, rel_steps = counts
    query = (1 + experts) * LANES

    @pl.when(step == 0)
    def _():
        main_scr[...] = jnp.zeros_like(main_scr)
        sum_scr[...] = jnp.zeros_like(sum_scr)
        rel_scr[...] = jnp.zeros_like(rel_scr)

    def add(columns):
        grads = grads_scr[:, :columns]
        main_scr[:columns, :] += mm_tn(grads, normed_ref[...])
        sum_scr[0:1, :columns] += jnp.sum(grads.astype(F32), axis=0, keepdims=True)

    @pl.when(step < key_steps)
    def _():
        value_grad = value_ref[...]
        grads_scr[:, :LANES] = key_ref[...]
        for e in range(experts):
            gate = gate_ref[:, head_dim + e : head_dim + e + 1]
            grads_scr[:, LANES * (1 + e) : LANES * (2 + e)] = (gate * value_grad).astype(BF16)

    @pl.when(step < mem_steps)
    def _():
        add(query)

    @pl.when((step >= mem_steps) & (step < key_steps))
    def _():
        grads_scr[:, query:] = query_ref[...]
        add(query + LANES)

    @pl.when(step >= key_steps)
    def _():
        rel_scr[...] += mm_tn(rel_ref[...], table_ref[...])

    @pl.when(step == key_steps + rel_steps - 1)
    def _():
        weights = w_ref[...].astype(F32)
        sums = sum_scr[...].T
        bias_one = jnp.sum(weights * sums[:, 0:1], axis=0, keepdims=True)
        inner = jnp.sum(weights * main_scr[...], axis=0, keepdims=True)
        small_ref[...] = jnp.zeros_like(small_ref)
        small_ref[0:1, :] = (inner - bias_ref[...] * bias_one) / gain_ref[...]
        small_ref[1:2, :] = bias_one
        small_ref[2:4, :] = sums_ref[...]
        small_ref[4:6, pl.ds(pl.multiple_of(where_ref[1] * LANES, LANES), LANES)] = biases_ref[...]
        for k in range(GROUP):
            target = send_ref if k % 2 else keep_ref
            at = k // 2
            lanes = pl.ds(pl.multiple_of((where_ref[0] ^ k) * LANES, LANES), LANES)
            row = 0

            def put(source, begin, size):
                target[at, row : row + size, :] = source[begin : begin + size, lanes].astype(BF16)
                return row + size

            for section in range(2 + experts):
                row = put(main_scr, section * LANES, head_dim)
            row = put(rel_scr, 0, head_dim)
            target[at, row:, :] = jnp.concatenate(
                [
                    main_scr[head_dim : head_dim + 8, lanes],
                    main_scr[query + head_dim : query + head_dim + 8, lanes],
                ],
                axis=0,
            ).astype(BF16)


def weight_grads(
    where,
    normed,
    key_grad,
    value_grad,
    gates,
    query_grad,
    table,
    rel_grad,
    w_all,
    gain,
    bias,
    sums_two,
    bias_sums,
    mem,
    head_dim,
    experts,
):
    keys, width = normed.shape
    cols = (2 + experts) * LANES
    big = 4 * ROWS
    mem_steps, key_steps = mem // big, keys // big
    rel_steps = table.shape[0] // big
    counts = (mem_steps, key_steps, rel_steps)
    rows = (3 + experts) * head_dim + 16
    key_row = lambda i, w: (jnp.minimum(i, key_steps - 1), 0)
    tok_row = lambda i, w: (jnp.clip(i - mem_steps, 0, key_steps - mem_steps - 1), 0)
    rel_row = lambda i, w: (jnp.clip(i - key_steps, 0, rel_steps - 1), 0)
    half = GROUP // 2
    return pl.pallas_call(
        functools.partial(weights_kernel, experts, head_dim, counts),
        grid_spec=pltpu.PrefetchScalarGridSpec(
            num_scalar_prefetch=1,
            grid=(key_steps + rel_steps,),
            in_specs=[
                pl.BlockSpec((big, width), key_row),
                pl.BlockSpec((big, LANES), key_row),
                pl.BlockSpec((big, LANES), key_row),
                pl.BlockSpec((big, LANES), key_row),
                pl.BlockSpec((big, LANES), tok_row),
                pl.BlockSpec((big, width), rel_row),
                pl.BlockSpec((big, LANES), rel_row),
                whole(cols, width),
                whole(1, width),
                whole(1, width),
                whole(2, width),
                whole(2, LANES),
            ],
            out_specs=[
                whole(half, rows, LANES),
                whole(half, rows, LANES),
                whole(8, width),
            ],
            scratch_shapes=[
                pltpu.VMEM((big, cols), BF16),
                pltpu.VMEM((8, cols), F32),
                pltpu.VMEM((cols, width), F32),
                pltpu.VMEM((LANES, width), F32),
            ],
        ),
        out_shape=[
            struct((half, rows, LANES), BF16),
            struct((half, rows, LANES), BF16),
            struct((8, width), F32),
        ],
        compiler_params=params(),
        cost_estimate=cost(15),
        name="weight_grads",
    )(
        where,
        normed,
        key_grad,
        value_grad,
        gates,
        query_grad,
        table,
        rel_grad,
        w_all,
        gain,
        bias,
        sums_two,
        bias_sums,
    )


def token_kernel(experts, head_dim, own_ref, far_ref, w_own_ref, w_far_ref, *refs):
    out_refs, grads_scr, total_scr = refs[:2], refs[2], refs[3]
    step = pl.program_id(0)
    query = (1 + experts) * LANES
    cols = query + LANES
    real = lane_of(ROWS) < head_dim

    def part(pack_ref, weights):
        for block in range(2):
            rows = slice(block * ROWS, (block + 1) * ROWS)
            value_pack = pack_ref[block, 1].astype(F32)
            value_grad = jnp.where(real, value_pack, 0.0)
            grads_scr[rows, :LANES] = pack_ref[block, 0]
            for e in range(experts):
                gate = value_pack[:, head_dim + e : head_dim + e + 1]
                grads_scr[rows, LANES * (1 + e) : LANES * (2 + e)] = (gate * value_grad).astype(
                    BF16
                )
            grads_scr[rows, query:] = pack_ref[block, 2]
        return mm(grads_scr[...], weights)

    @pl.when(step == 0)
    def _():
        total_scr[...] = part(own_ref, w_own_ref[:cols, :])

    @pl.when(step == 1)
    def _():
        weights = w_far_ref[...].reshape(-1, w_far_ref.shape[2])
        total = total_scr[...] + part(far_ref, weights[:cols, :])
        out_refs[0][...] = total[:ROWS]
        out_refs[1][...] = total[ROWS:].astype(BF16)


def token_parts(own_pack, far_pack, own_w, far_w, head_dim, experts):
    width = own_w.shape[1]
    rows = 2 * ROWS
    cols = (2 + experts) * LANES
    return pl.pallas_call(
        functools.partial(token_kernel, experts, head_dim),
        grid=(2,),
        in_specs=[
            whole(*own_pack.shape),
            whole(*far_pack.shape),
            whole(*own_w.shape),
            whole(*far_w.shape),
        ],
        out_specs=[whole(ROWS, width)] * 2,
        out_shape=[struct((ROWS, width), F32), struct((ROWS, width), BF16)],
        scratch_shapes=[pltpu.VMEM((rows, cols), BF16), pltpu.VMEM((rows, width), F32)],
        compiler_params=params(),
        cost_estimate=cost(6),
        name="token_parts",
    )(own_pack, far_pack, own_w, far_w)


def token_sum_kernel(z_ref, tok_ref, mid_ref, gain_ref, own_ref, near_ref, out_ref):
    total = own_ref[...] + near_ref[...].astype(F32)
    normal, inv_std = norm_parts(tok_ref[...].astype(F32))
    out_ref[...] = mid_ref[...] + norm_back(total, normal, inv_std, gain_ref[...])


def token_sum(rank, tokens, middle_grad, gain, own, near):
    rows, width = middle_grad.shape
    return pl.pallas_call(
        token_sum_kernel,
        grid_spec=pltpu.PrefetchScalarGridSpec(
            num_scalar_prefetch=1,
            grid=(1,),
            in_specs=[
                pl.BlockSpec((rows, width), lambda i, z: (z[0], 0)),
                whole(rows, width),
                whole(1, width),
                whole(rows, width),
                whole(rows, width),
            ],
            out_specs=whole(rows, width),
        ),
        out_shape=struct((rows, width), F32),
        compiler_params=params(),
        cost_estimate=cost(4),
        name="token_sum",
    )(rank, tokens, middle_grad, gain, own, near)


def swap(array, axis, mask):
    size = lax.axis_size(axis)
    return lax.ppermute(array, axis, [(i, i ^ mask) for i in range(size)])


def plus(left, right):
    return (left.astype(F32) + right.astype(F32)).astype(BF16)


def scatter_first(keep, far):
    return [plus(keep[m], far[m]) for m in range(keep.shape[0])]


def scatter_sends(blocks, unit):
    return [swap(blocks[m], "dp", 2 * m * unit) for m in range(1, len(blocks))]


def scatter_done(own, fars, unit, axis):
    out = own.astype(F32)
    for far in fars:
        out = out + far.astype(F32)
    mask = unit // 2
    while mask:
        size = out.shape[axis] // 2
        bit = (lax.axis_index("dp") // mask) % 2
        mine = lax.dynamic_slice_in_dim(out, bit * size, size, axis)
        theirs = lax.dynamic_slice_in_dim(out, (1 - bit) * size, size, axis)
        out = mine + swap(theirs.astype(BF16), "dp", mask).astype(F32)
        mask //= 2
    return out


def spread(far, *gates):
    pieces = [swap(far, "dp", 2 * m) for m in range(1, GROUP // 2)]
    even = after(pile(far, *pieces), *gates)
    odd = swap(even, "dp", 1)
    return even, odd


def on_device(
    tokens,
    memory,
    segments,
    value_routes,
    output_routes,
    first_gain,
    first_bias,
    second_gain,
    second_bias,
    query_head_weight,
    key_weight,
    position_weight,
    value_weight,
    value_select,
    output_expert_selector,
    output_expert_weight,
    content_bias,
    position_bias,
    up_projection_weight,
    down_projection_weight,
    cotangent,
):
    mem_len = memory.shape[1]
    toks, width = tokens.shape
    head_dim = query_head_weight.shape[2]
    experts = value_select.shape[2]
    hidden = up_projection_weight.shape[1]
    parts = lax.axis_size("tensor")
    rank = lax.axis_index("tensor")
    dp = lax.axis_size("dp")
    at = lax.axis_index("dp")
    others = range(1, parts)
    near, far_shard = 1, 2
    rank_ref = rank.reshape(1).astype(jnp.int32)
    row = lambda v: v.reshape(1, -1)
    lanes = lambda v: jnp.pad(v, ((0, 0), (0, LANES - head_dim)))

    own_out = output_expert_weight[0]
    size = width // GROUP
    own_block = lax.dynamic_slice_in_dim(own_out, (at % GROUP) * size, size, 1)
    far_out = swap(own_block, "tensor", far_shard)
    span = mem_len
    fine = 32
    rates = jnp.exp(jnp.arange(width // 2).astype(F32) * (-2.0 * math.log(10000.0) / width))
    coarse_at = (span - 1 - fine * jnp.arange(span // fine)).astype(F32)[:, None] * rates[None, :]
    fine_at = jnp.arange(fine).astype(F32)[:, None] * rates[None, :]
    sin_a, cos_a = jnp.sin(coarse_at)[:, None, :], jnp.cos(coarse_at)[:, None, :]
    sin_b, cos_b = jnp.sin(fine_at)[None, :, :], jnp.cos(fine_at)[None, :, :]
    sin_table = jnp.concatenate(
        [sin_a * cos_b - cos_a * sin_b, cos_a * cos_b + sin_a * sin_b], axis=2
    )
    sin_table = lax.optimization_barrier(sin_table.reshape(span, width).astype(BF16))
    rel_weight = jnp.concatenate(
        [position_weight[0].T, jnp.zeros((LANES - head_dim, width), BF16)]
    )
    rel_reverse = mm_nt(sin_table, rel_weight).astype(BF16)

    w_all, normed, key_vecs, value_vecs, every, vgate, qc, qp, ogate = project(
        memory[0],
        tokens,
        row(first_gain),
        row(first_bias),
        (
            key_weight[0].T,
            value_select[0].T,
            value_weight[0].T,
            query_head_weight[0].T,
            output_expert_selector[0].T,
        ),
        value_routes[0, :, 0].T,
        output_routes[:, 0].T,
        lanes(content_bias),
        lanes(position_bias),
        experts,
        head_dim,
    )
    steps = toks // ROWS
    seg = segments[0]
    seg_keys = jnp.stack([seg[i * ROWS : i * ROWS + span + ROWS] for i in range(steps)])[:, None]
    seg_keys = after(seg_keys, far_out)
    heads, probs, *packs = attend(
        rank_ref,
        qc,
        qp,
        key_vecs,
        value_vecs,
        rel_reverse,
        seg_keys,
        seg[mem_len:, None],
        ogate,
        head_dim,
    )

    depth = width // dp
    feed_piece = jnp.stack(
        [
            lax.dynamic_slice_in_dim(up_projection_weight, at * depth, depth, 0),
            lax.dynamic_slice_in_dim(down_projection_weight, at * (hidden // dp), hidden // dp, 0),
        ]
    )
    far_feed = swap(feed_piece, "tensor", far_shard)
    far_feed = lax.all_gather(after(far_feed, packs[0]), "dp", axis=0)
    packs = [packs[0], swap(packs[1], "tensor", far_shard)]
    even, odd = spread(after(far_out, qc), packs[1])
    cots = [cotangent, swap(after(cotangent, packs[1]), "tensor", near)]
    piece = w_all.shape[0] // dp
    own_piece = lax.dynamic_slice_in_dim(w_all, at * piece, piece, 0)
    far_w = swap(after(own_piece, packs[1]), "tensor", far_shard)
    group_at = at % GROUP
    where = jnp.stack([group_at // 2, group_at % 2, rank]).astype(jnp.int32)
    full, own_part, near_part = mix(where, packs, own_out, even, odd, experts, head_dim)
    middle, up_in = middle_rows(
        rank_ref,
        tokens,
        after(own_part, far_w, cots[1]),
        swap(near_part, "tensor", near),
        row(second_gain),
        row(second_bias),
    )

    ups = [up_in, swap(up_in, "tensor", near)]
    unit = dp // GROUP
    where_grads = jnp.stack([at // unit, rank]).astype(jnp.int32)
    far_w = lax.all_gather(after(far_w, up_in), "dp", axis=0)
    shards = (up_projection_weight, down_projection_weight, far_feed)
    own_hidden, own_pre, own_result, own_up = feed(ups[0], cots[0], *shards, F32)
    near_hidden, near_pre, near_result, near_up = feed(ups[1], cots[1], *shards, BF16, own_pre)
    back_up = swap(near_up, "tensor", near)
    feed_sums = feed_weights(ups, cots, (own_pre, near_pre), (own_hidden, near_hidden))
    feed_sums = after(feed_sums, far_w, back_up)
    own_up = after(own_up, feed_sums)
    feed_sums = lax.psum_scatter(feed_sums, "dp", scatter_dimension=0, tiled=True)

    middle_grad, attn_grad, sums_two = middle_back(
        own_up, back_up, cotangent, middle, row(second_gain)
    )
    near_grad = swap(attn_grad, "tensor", near)
    backs = heads_back(attn_grad, near_grad, full, packs, experts, head_dim)
    out_keep, out_send = out_weights(where_grads, packs, attn_grad, near_grad, experts, head_dim)
    backs = [after(backs[0], out_keep), swap(backs[1], "tensor", far_shard)]
    back_out = swap(after(near_result, backs[1]), "tensor", near)

    key_grad, value_grad, query_grad, rel_grad, bias_sums, *grad_packs = attend_back(
        rank_ref,
        qc,
        qp,
        key_vecs,
        value_vecs,
        rel_reverse,
        probs,
        heads,
        ogate,
        every,
        vgate,
        backs,
        head_dim,
    )
    out_part = scatter_first(out_keep, swap(out_send, "dp", unit))
    rel_grad = after(rel_grad, *out_part, back_out)
    out_fars = scatter_sends(out_part, unit)
    far_pack = swap(grad_packs[1], "tensor", far_shard)
    keep, send, small = weight_grads(
        where_grads,
        normed,
        key_grad,
        value_grad,
        vgate,
        query_grad,
        sin_table,
        rel_grad,
        w_all,
        row(first_gain),
        row(first_bias),
        sums_two,
        bias_sums,
        mem_len,
        head_dim,
        experts,
    )
    token_own, token_near = token_parts(
        grad_packs[0], far_pack, w_all, after(far_w, keep), head_dim, experts
    )
    send, small = (after(each, token_near, span=20) for each in (send, small))
    token_near = swap(token_near, "tensor", near)
    kept_far = swap(send, "dp", unit)
    small_fars = [swap(small, "tensor", m) for m in others]
    out_fars = [after(far, send) for far in out_fars]
    out_sums = scatter_done(out_part[0], out_fars, unit, 1).reshape(2, experts * head_dim, -1)
    out_low = out_sums[1].astype(BF16)
    feed_own, feed_far = feed_sums[:, : 2 * hidden], feed_sums[:, 2 * hidden :]
    kept_far, feed_far, *small_fars = together(kept_far, feed_far, *small_fars)
    feed_far = swap(feed_far, "tensor", far_shard)
    out_far = swap(out_low, "tensor", far_shard)
    kept = scatter_first(keep, kept_far)
    for far in small_fars:
        small = small + far
    kept_fars = scatter_sends(kept, unit)
    small_fars = [swap(small, "dp", m) for m in range(2, GROUP, 2)]
    feed_far, *fars = together(feed_far, *kept_fars, *small_fars)
    kept_fars, small_fars = fars[: len(fars) // 2], fars[len(fars) // 2 :]
    for far in small_fars:
        small = small + far
    mask = GROUP
    while mask < dp:
        small = small + swap(small, "dp", mask)
        mask *= 2
    small = small + swap(small, "dp", 1)
    kept = scatter_done(kept[0], kept_fars, unit, 1)
    tokens_grad = token_sum(
        rank_ref, tokens, middle_grad, row(first_gain), token_own, token_near
    )
    result = (middle + own_result + after(back_out, keep).astype(F32)).astype(BF16)
    out_w = out_sums[0] + after(out_far, *kept_fars).astype(F32)
    feed_grads = feed_own.astype(F32) + feed_far.astype(F32)
    up_total = feed_grads[:, :hidden]
    down_total = feed_grads[:, hidden:].T
    biases = small[4:6, : parts * LANES].reshape(2, parts, LANES)[:, :, :head_dim]
    marks = [0, 1, 1 + experts, 2 + experts, 3 + experts]
    key_w, value_w, query_w, rel_w = (
        kept[a * head_dim : b * head_dim] for a, b in zip(marks, marks[1:])
    )
    select = marks[-1] * head_dim
    turn = lambda part: part.T[None]
    return (
        result,
        tokens_grad,
        small[0],
        small[1],
        small[2],
        small[3],
        turn(query_w),
        turn(key_w),
        turn(rel_w),
        turn(value_w),
        turn(kept[select : select + experts]),
        turn(kept[select + 8 : select + 8 + experts]),
        out_w[None],
        biases[0],
        biases[1],
        up_total,
        down_total,
    )


def solution(mesh):
    placed = (
        P("dp", None),
        P("dp", None, None),
        P("dp", None),
        P("dp", None, "tensor", None),
        P("dp", "tensor", None),
        P(),
        P(),
        P(),
        P(),
        P("tensor", None, None),
        P("tensor", None, None),
        P("tensor", None, None),
        P("tensor", None, None),
        P("tensor", None, None),
        P("tensor", None, None),
        P("tensor", None, None),
        P("tensor", None),
        P("tensor", None),
        P(None, "tensor"),
        P("tensor", None),
        P(("dp", "tensor"), None),
    )
    return jax.shard_map(
        on_device,
        mesh=mesh,
        in_specs=placed,
        out_specs=(
            P(("dp", "tensor"), None),
            P(("dp", "tensor"), None),
            P(),
            P(),
            P(),
            P(),
            P("tensor", "dp", None),
            P("tensor", "dp", None),
            P("tensor", "dp", None),
            P("tensor", "dp", None),
            P("tensor", "dp", None),
            P("tensor", "dp", None),
            P("tensor", None, "dp"),
            P(),
            P(),
            P("dp", "tensor"),
            P("tensor", "dp"),
        ),
        check_vma=False,
    )
```

```python
import functools
import math

import jax
import jax.numpy as jnp
from jax import lax
from jax.experimental import pallas as pl
from jax.experimental.pallas import tpu as pltpu
from jax.sharding import PartitionSpec as P

EPSILON = 1e-05
ROOT_HALF = 0.7071067811865476
INVERSE_ROOT_TAU = 0.3989422804014327
ROWS = 256
GROUP = 8
MIB = 1024 * 1024
BF16 = jnp.bfloat16
F32 = jnp.float32


def mm(left, right):
    return jnp.dot(left, right, preferred_element_type=F32)


def mm_nt(left, right):
    return lax.dot_general(left, right, (((1,), (1,)), ((), ())), preferred_element_type=F32)


def mm_tn(left, right):
    return lax.dot_general(left, right, (((0,), (0,)), ((), ())), preferred_element_type=F32)


def norm_parts(values):
    center = values - jnp.mean(values, axis=-1, keepdims=True)
    inv_std = lax.rsqrt(jnp.mean(center * center, axis=-1, keepdims=True) + EPSILON)
    return center * inv_std, inv_std


def norm_back(upstream, normal, inv_std, gain):
    scaled = upstream * gain
    return inv_std * (
        scaled
        - jnp.mean(scaled, axis=-1, keepdims=True)
        - normal * jnp.mean(scaled * normal, axis=-1, keepdims=True)
    )


def params():
    return pltpu.CompilerParams(vmem_limit_bytes=63 * MIB)


def cost(microseconds):
    return pl.CostEstimate(
        flops=int(microseconds * 1.15e9), bytes_accessed=0, transcendentals=0
    )


def struct(shape, dtype):
    return jax.ShapeDtypeStruct(shape, dtype)


def whole(*shape):
    return pl.BlockSpec(shape, lambda *_: (0,) * len(shape))

LANES = 128


def lane_of(rows):
    return lax.broadcasted_iota(jnp.int32, (rows, LANES), 1)


def picked(routes, head_dim):
    rows = routes.shape[1]
    routes = jnp.concatenate([routes, jnp.zeros((6, rows), jnp.int32)], axis=0).astype(F32).T
    lane = (lane_of(rows) - head_dim).astype(F32)
    return (lane == routes[:, 0:1]) | (lane == routes[:, 1:2])


def after(array, *deps, span=0):
    def body(*refs):
        del refs

    spec = pl.BlockSpec(memory_space=pl.ANY)
    return pl.pallas_call(
        body,
        in_specs=[spec] * (1 + len(deps)),
        out_specs=spec,
        out_shape=struct(array.shape, array.dtype),
        input_output_aliases={0: 0},
        cost_estimate=cost(span),
        name="after",
    )(array, *deps)


def together(*arrays, span=0):
    def body(*refs):
        del refs

    spec = pl.BlockSpec(memory_space=pl.ANY)
    return pl.pallas_call(
        body,
        in_specs=[spec] * len(arrays),
        out_specs=[spec] * len(arrays),
        out_shape=[struct(a.shape, a.dtype) for a in arrays],
        input_output_aliases={i: i for i in range(len(arrays))},
        cost_estimate=cost(span),
        name="together",
    )(*arrays)


def pile(*arrays):
    def body(*refs):
        for i, ref in enumerate(refs[:-1]):
            refs[-1][i] = ref[...]

    shape = arrays[0].shape
    return pl.pallas_call(
        body,
        in_specs=[whole(*shape)] * len(arrays),
        out_specs=whole(len(arrays), *shape),
        out_shape=struct((len(arrays),) + shape, arrays[0].dtype),
        grid=(1,),
        compiler_params=params(),
        cost_estimate=cost(2),
        name="pile",
    )(*arrays)


def project_kernel(
    experts,
    head_dim,
    mem_steps,
    scale,
    mem_ref,
    tok_ref,
    gain_ref,
    bias_ref,
    key_w_ref,
    vsel_ref,
    value_w_ref,
    query_w_ref,
    osel_ref,
    vroute_ref,
    oroute_ref,
    cb_ref,
    pb_ref,
    w_out_ref,
    normed_ref,
    key_ref,
    val_ref,
    every_ref,
    vgate_ref,
    qc_ref,
    qp_ref,
    ogate_ref,
    w_ref,
):
    step = pl.program_id(0)
    query = (1 + experts) * LANES

    @pl.when(step == 0)
    def _():
        w_ref[...] = jnp.zeros_like(w_ref)
        w_ref[:head_dim, :] = key_w_ref[...]
        w_ref[head_dim : head_dim + experts, :] = vsel_ref[...]
        for e in range(experts):
            w_ref[(1 + e) * LANES : (1 + e) * LANES + head_dim, :] = value_w_ref[
                e * head_dim : (e + 1) * head_dim, :
            ]
        w_ref[query : query + head_dim, :] = query_w_ref[...]
        w_ref[query + head_dim : query + head_dim + experts, :] = osel_ref[...]

    size = w_out_ref.shape[0]
    w_out_ref[...] = w_ref[pl.ds(pl.multiple_of(step * size, size), size), :]

    def rows_part():
        blocks = [slice(i * ROWS, (i + 1) * ROWS) for i in range(tok_ref.shape[0] // ROWS)]
        normed, outs = [], []
        for rows in blocks:
            block = jnp.where(step < mem_steps, mem_ref[rows, :], tok_ref[rows, :])
            normal, _ = norm_parts(block.astype(F32))
            normed.append((normal * gain_ref[...] + bias_ref[...]).astype(BF16))
            outs.append(mm_nt(normed[-1], w_ref[: query + LANES, :]))
        lane = lane_of(ROWS)
        real = lane < head_dim
        for rows, norm, out in zip(blocks, normed, outs):
            normed_ref[rows, :] = norm
            first = out[:, :LANES]
            key_ref[rows, :] = jnp.where(real, first, 0.0).astype(BF16)
            every_ref[rows, :] = out[:, LANES:query].astype(BF16)
            gate = jnp.where(picked(vroute_ref[:, rows], head_dim), jax.nn.sigmoid(first), 0.0)
            vgate_ref[rows, :] = gate
            value = jnp.zeros((ROWS, LANES), F32)
            for e in range(experts):
                value = value + gate[:, head_dim + e : head_dim + e + 1] * (
                    out[:, (1 + e) * LANES : (2 + e) * LANES]
                )
            val_ref[rows, :] = value.astype(BF16)
            q = out[:, query:]
            qc_ref[rows, :] = jnp.where(real, (q + cb_ref[...]) * scale, 0.0).astype(BF16)
            qp_ref[rows, :] = jnp.where(real, (q + pb_ref[...]) * scale, 0.0).astype(BF16)
            ogate_ref[rows, :] = jnp.where(
                picked(oroute_ref[:, rows], head_dim), jax.nn.sigmoid(q), 0.0
            )

    rows_part()


def project(memory, tokens, gain, bias, weights, vroutes, oroutes, cb, pb, experts, head_dim):
    mem, width = memory.shape
    toks = tokens.shape[0]
    big = 2 * ROWS
    mem_steps, tok_steps = mem // big, toks // big
    steps = mem_steps + tok_steps
    keys = mem + toks
    cols = width
    mem_row = lambda i: (jnp.minimum(i, mem_steps - 1), 0)
    tok_row = lambda i: (jnp.maximum(i - mem_steps, 0), 0)
    row = lambda i: (i, 0)
    return pl.pallas_call(
        functools.partial(project_kernel, experts, head_dim, mem_steps, head_dim ** (-0.5)),
        grid=(steps,),
        in_specs=[
            pl.BlockSpec((big, width), mem_row),
            pl.BlockSpec((big, width), tok_row),
            whole(1, width),
            whole(1, width),
        ]
        + [whole(*w.shape) for w in weights]
        + [
            pl.BlockSpec((vroutes.shape[0], big), lambda i: (0, i)),
            pl.BlockSpec((oroutes.shape[0], big), lambda i: (0, jnp.maximum(i - mem_steps, 0))),
            whole(1, LANES),
            whole(1, LANES),
        ],
        out_specs=[
            pl.BlockSpec((cols // steps, width), row),
            pl.BlockSpec((big, width), row),
            pl.BlockSpec((big, LANES), row),
            pl.BlockSpec((big, LANES), row),
            pl.BlockSpec((big, experts * LANES), row),
            pl.BlockSpec((big, LANES), row),
            pl.BlockSpec((big, LANES), tok_row),
            pl.BlockSpec((big, LANES), tok_row),
            pl.BlockSpec((big, LANES), tok_row),
        ],
        out_shape=[
            struct((cols, width), BF16),
            struct((keys, width), BF16),
            struct((keys, LANES), BF16),
            struct((keys, LANES), BF16),
            struct((keys, experts * LANES), BF16),
            struct((keys, LANES), F32),
            struct((toks, LANES), BF16),
            struct((toks, LANES), BF16),
            struct((toks, LANES), F32),
        ],
        scratch_shapes=[pltpu.VMEM((cols, width), BF16)],
        compiler_params=params(),
        cost_estimate=cost(12),
        name="project",
    )(memory, tokens, gain, bias, *weights, vroutes, oroutes, cb, pb)


def attend_kernel(
    span,
    head_dim,
    count,
    z_ref,
    qc_ref,
    qp_ref,
    key_ref,
    val_ref,
    rel_ref,
    segk_ref,
    segq_ref,
    ogate_ref,
    heads_ref,
    probs_ref,
    *pack_refs,
):
    step = pl.program_id(0)
    wide = span + ROWS
    column = lax.broadcasted_iota(jnp.int32, (ROWS, ROWS), 1)
    causal = column <= lax.broadcasted_iota(jnp.int32, (ROWS, ROWS), 0)
    for b in range(count):
        rows = slice(b * ROWS, (b + 1) * ROWS)
        window = pl.ds((step * count + b) * ROWS, wide)
        content = mm_nt(qc_ref[rows, :], key_ref[window, :])
        reverse = mm_nt(qp_ref[rows, :], rel_ref[...])
        reverse = jnp.concatenate([reverse, jnp.zeros((ROWS, ROWS), F32)], axis=1)
        scores = content + pltpu.roll(reverse, 1, 1, stride=1, stride_axis=0)
        same = segk_ref[b] == segq_ref[rows, :]
        allowed = jnp.concatenate([same[:, :span], same[:, span:] & causal], axis=1)
        scores = jnp.where(allowed, scores, -1e30)
        expo = jnp.exp(scores - jnp.max(scores, axis=1, keepdims=True))
        probs = (expo * (1.0 / jnp.sum(expo, axis=1, keepdims=True))).astype(BF16)
        probs_ref[rows, :] = probs
        heads = mm(probs, val_ref[window, :])
        heads_ref[rows, :] = heads
        packed = jnp.where(lane_of(ROWS) < head_dim, heads, ogate_ref[rows, :]).astype(BF16)
        slot = (step * count + b) ^ z_ref[0]
        for side, pack_ref in enumerate(pack_refs):

            @pl.when(slot // 2 == side)
            def _():
                pack_ref[slot % 2] = packed


def attend(rank, qc, qp, key_vecs, value_vecs, rel_reverse, seg_keys, seg_query, ogate, head_dim):
    toks = qc.shape[0]
    keys = key_vecs.shape[0]
    span = rel_reverse.shape[0]
    steps = toks // ROWS
    count = 1
    big = count * ROWS
    wide = span + ROWS
    row = lambda i, z: (i, 0)
    return pl.pallas_call(
        functools.partial(attend_kernel, span, head_dim, count),
        grid_spec=pltpu.PrefetchScalarGridSpec(
            num_scalar_prefetch=1,
            grid=(steps // count,),
            in_specs=[
                pl.BlockSpec((big, LANES), row),
                pl.BlockSpec((big, LANES), row),
                whole(keys, LANES),
                whole(keys, LANES),
                whole(span, LANES),
                pl.BlockSpec((count, 1, wide), lambda i, z: (i, 0, 0)),
                pl.BlockSpec((big, 1), row),
                pl.BlockSpec((big, LANES), row),
            ],
            out_specs=[
                pl.BlockSpec((big, LANES), row),
                pl.BlockSpec((big, wide), row),
            ]
            + [whole(2, ROWS, LANES)] * (steps // 2),
        ),
        out_shape=[struct((toks, LANES), F32), struct((toks, wide), BF16)]
        + [struct((2, ROWS, LANES), BF16)] * (steps // 2),
        compiler_params=params(),
        cost_estimate=cost(8),
        name="attend",
    )(rank, qc, qp, key_vecs, value_vecs, rel_reverse, seg_keys, seg_query, ogate)


def attend_back_kernel(
    span,
    experts,
    head_dim,
    parts,
    z_ref,
    qc_ref,
    qp_ref,
    key_ref,
    val_ref,
    rel_ref,
    probs_ref,
    heads_ref,
    ogate_ref,
    every_ref,
    vgate_ref,
    *refs,
):
    back_refs, refs = refs[: parts // 2], refs[parts // 2 :]
    key_grad_ref, value_grad_ref, query_grad_ref, rel_grad_ref, bias_ref = refs[:5]
    pack_refs, refs = refs[5 : 5 + parts // 2], refs[5 + parts // 2 :]
    keys_scr, values_scr, rel_scr, query_scr, back_scr = refs
    step = pl.program_id(0)
    steps = pl.num_programs(0)
    wide = span + ROWS
    mem = keys_scr.shape[0] - steps * ROWS
    scale = head_dim ** (-0.5)
    real = lane_of(ROWS) < head_dim

    @pl.when(step == 0)
    def _():
        keys_scr[...] = jnp.zeros_like(keys_scr)
        values_scr[...] = jnp.zeros_like(values_scr)
        rel_scr[...] = jnp.zeros_like(rel_scr)
        bias_ref[...] = jnp.zeros_like(bias_ref)

    slot = step ^ z_ref[0]
    for side, back_ref in enumerate(back_refs):

        @pl.when(slot // 2 == side)
        def _():
            back_scr[...] = back_ref[slot % 2]

    window = pl.ds(step * ROWS, wide)
    keys = key_ref[window, :]
    vals = val_ref[window, :]
    back = back_scr[...].astype(F32)
    out_grad = jnp.where(real, back, 0.0)
    delta = jnp.sum(out_grad * heads_ref[...], axis=1, keepdims=True)
    out_grad = out_grad.astype(BF16)
    probs = probs_ref[...]
    probs_grad = mm_nt(out_grad, vals)
    score_grad = (probs.astype(F32) * (probs_grad - delta)).astype(BF16)
    content_grad = mm(score_grad, keys).astype(BF16).astype(F32) * scale
    keys_scr[window, :] += mm_tn(score_grad, qc_ref[...])
    values_scr[window, :] += mm_tn(probs, out_grad)
    flip = (
        lax.broadcasted_iota(jnp.int32, (ROWS, ROWS), 0)
        + lax.broadcasted_iota(jnp.int32, (ROWS, ROWS), 1)
        == ROWS - 1
    ).astype(BF16)
    turned = mm(flip, score_grad)
    turned = pltpu.roll(turned, span, 1, stride=1, stride_axis=0)[:, :span].astype(BF16)
    place_grad = mm(turned, rel_ref[...]).astype(BF16)
    position_grad = mm(flip, place_grad) * scale
    rel_scr[...] += mm_tn(turned, mm(flip, qp_ref[...]).astype(BF16))
    bias_ref[0:1, :] += jnp.sum(content_grad, axis=0, keepdims=True)
    bias_ref[1:2, :] += jnp.sum(position_grad, axis=0, keepdims=True)
    gate = ogate_ref[...]
    query_grad = jnp.where(real, content_grad + position_grad, back * gate * (1.0 - gate))
    query_grad = query_grad.astype(BF16)
    query_grad_ref[...] = query_grad
    query_scr[pl.ds(step * ROWS, ROWS), :] = query_grad

    @pl.when(step == steps - 1)
    def _():
        rel_grad_ref[...] = rel_scr[...].astype(BF16)

        @pl.loop(0, (mem + steps * ROWS) // ROWS)
        def _(block):
            rows = pl.ds(block * ROWS, ROWS)
            value_grad = values_scr[rows, :]
            gates = vgate_ref[rows, :]
            value_grad_ref[rows, :] = value_grad
            logit = keys_scr[rows, :]
            lane = lane_of(ROWS)
            for e in range(experts):
                part = every_ref[rows, e * LANES : (e + 1) * LANES].astype(F32)
                total = jnp.sum(value_grad * part, axis=1, keepdims=True)
                logit = jnp.where(lane == head_dim + e, total, logit)
            key_grad = jnp.where(real, logit, logit * gates * (1.0 - gates)).astype(BF16)
            key_grad_ref[rows, :] = key_grad

            @pl.when(block * ROWS >= mem)
            def _():
                place = block - mem // ROWS
                slot = place ^ z_ref[0]
                value_pack = jnp.where(real, value_grad, gates).astype(BF16)
                for side, pack_ref in enumerate(pack_refs):

                    @pl.when(slot // 2 == side)
                    def _():
                        pack_ref[slot % 2, 0] = key_grad
                        pack_ref[slot % 2, 1] = value_pack
                        pack_ref[slot % 2, 2] = query_scr[pl.ds(place * ROWS, ROWS), :]


def attend_back(
    rank,
    qc,
    qp,
    key_vecs,
    value_vecs,
    rel_reverse,
    probs,
    heads,
    ogate,
    every,
    vgate,
    backs,
    head_dim,
):
    toks = qc.shape[0]
    keys = key_vecs.shape[0]
    span = rel_reverse.shape[0]
    steps = toks // ROWS
    wide = span + ROWS
    experts = every.shape[1] // LANES
    row = lambda i, z: (i, 0)
    return pl.pallas_call(
        functools.partial(attend_back_kernel, span, experts, head_dim, steps),
        grid_spec=pltpu.PrefetchScalarGridSpec(
            num_scalar_prefetch=1,
            grid=(steps,),
            in_specs=[
                pl.BlockSpec((ROWS, LANES), row),
                pl.BlockSpec((ROWS, LANES), row),
                whole(keys, LANES),
                whole(keys, LANES),
                whole(span, LANES),
                pl.BlockSpec((ROWS, wide), row),
                pl.BlockSpec((ROWS, LANES), row),
                pl.BlockSpec((ROWS, LANES), row),
                whole(keys, experts * LANES),
                whole(keys, LANES),
            ]
            + [whole(2, ROWS, LANES)] * (steps // 2),
            out_specs=[
                whole(keys, LANES),
                whole(keys, LANES),
                pl.BlockSpec((ROWS, LANES), row),
                whole(span, LANES),
                whole(2, LANES),
            ]
            + [whole(2, 3, ROWS, LANES)] * (steps // 2),
            scratch_shapes=[
                pltpu.VMEM((keys, LANES), F32),
                pltpu.VMEM((keys, LANES), F32),
                pltpu.VMEM((span, LANES), F32),
                pltpu.VMEM((toks, LANES), BF16),
                pltpu.VMEM((ROWS, LANES), BF16),
            ],
        ),
        out_shape=[
            struct((keys, LANES), BF16),
            struct((keys, LANES), F32),
            struct((toks, LANES), BF16),
            struct((span, LANES), BF16),
            struct((2, LANES), F32),
        ]
        + [struct((2, 3, ROWS, LANES), BF16)] * (steps // 2),
        compiler_params=params(),
        cost_estimate=cost(15),
        name="attend_back",
    )(rank, qc, qp, key_vecs, value_vecs, rel_reverse, probs, heads, ogate, every, vgate, *backs)


def mix_kernel(experts, head_dim, where_ref, *refs):
    pack_refs, refs = refs[:2], refs[2:]
    own_ref, even_ref, odd_ref, full_ref, own_part_ref, near_part_ref, mixed_scr = refs
    step = pl.program_id(0)

    @pl.when(step == 0)
    def _():
        real = lane_of(ROWS) < head_dim
        for h in range(2):
            for block in range(2):
                pack = pack_refs[h][block].astype(F32)
                out = jnp.where(real, pack, 0.0)
                rows = slice(block * ROWS, (block + 1) * ROWS)
                for e in range(experts):
                    gate = pack[:, head_dim + e : head_dim + e + 1]
                    mixed_scr[h, rows, e * LANES : (e + 1) * LANES] = (gate * out).astype(BF16)

    turned = where_ref[1] == 1
    even, odd = even_ref[0], odd_ref[0]
    far = jnp.concatenate([jnp.where(turned, odd, even), jnp.where(turned, even, odd)], axis=1)
    total = None
    for h, weight in enumerate((own_ref[...], far)):
        for e in range(experts):
            full_ref[h, e * LANES : e * LANES + head_dim, :] = weight[
                e * head_dim : (e + 1) * head_dim
            ]
            full_ref[h, e * LANES + head_dim : (e + 1) * LANES, :] = jnp.zeros(
                (LANES - head_dim, weight.shape[1]), BF16
            )
        part = mm(mixed_scr[h], full_ref[h])
        total = part if total is None else total + part
    own_part_ref[...] = total[:ROWS]
    near_part_ref[...] = total[ROWS:].astype(BF16)


def mix(where, packs, own_weight, even, odd, experts, head_dim):
    depth, width = own_weight.shape
    steps = even.shape[0]
    size = width // steps
    column = lambda s, w: (0, w[0] ^ s)
    return pl.pallas_call(
        functools.partial(mix_kernel, experts, head_dim),
        grid_spec=pltpu.PrefetchScalarGridSpec(
            num_scalar_prefetch=1,
            grid=(steps,),
            in_specs=[whole(2, ROWS, LANES)] * 2
            + [
                pl.BlockSpec((depth, size), column),
                pl.BlockSpec((1,) + even.shape[1:], lambda s, w: (s, 0, 0)),
                pl.BlockSpec((1,) + odd.shape[1:], lambda s, w: (s, 0, 0)),
            ],
            out_specs=[
                pl.BlockSpec((2, experts * LANES, size), lambda s, w: (0, 0, w[0] ^ s)),
                pl.BlockSpec((ROWS, size), column),
                pl.BlockSpec((ROWS, size), column),
            ],
            scratch_shapes=[pltpu.VMEM((2, 2 * ROWS, experts * LANES), BF16)],
        ),
        out_shape=[
            struct((2, experts * LANES, width), BF16),
            struct((ROWS, width), F32),
            struct((ROWS, width), BF16),
        ],
        compiler_params=params(),
        cost_estimate=cost(7),
        name="mix",
    )(where, *packs, own_weight, even, odd)


def middle_kernel(z_ref, tok_ref, own_ref, near_ref, gain_ref, bias_ref, middle_ref, up_ref):
    middle = tok_ref[...].astype(F32) + (own_ref[...] + near_ref[...].astype(F32))
    middle_ref[...] = middle
    normal, _ = norm_parts(middle)
    up_ref[...] = (normal * gain_ref[...] + bias_ref[...]).astype(BF16)


def middle_rows(rank, tokens, own, near, gain, bias):
    rows, width = own.shape
    steps = 2
    block = pl.BlockSpec((rows // steps, width), lambda i, z: (i, 0))
    return pl.pallas_call(
        middle_kernel,
        grid_spec=pltpu.PrefetchScalarGridSpec(
            num_scalar_prefetch=1,
            grid=(steps,),
            in_specs=[
                pl.BlockSpec((rows // steps, width), lambda i, z: (z[0] * steps + i, 0)),
                block,
                block,
                whole(1, width),
                whole(1, width),
            ],
            out_specs=[block, block],
        ),
        out_shape=[struct((rows, width), F32), struct((rows, width), BF16)],
        compiler_params=params(),
        cost_estimate=cost(3),
        name="middle",
    )(rank, tokens, own, near, gain, bias)


def middle_back_kernel(
    own_ref, near_ref, cot_ref, middle_ref, gain_ref, grad_ref, low_ref, sums_ref
):
    upstream = own_ref[...].astype(F32) + near_ref[...].astype(F32)
    normal, inv_std = norm_parts(middle_ref[...])

    @pl.when(pl.program_id(0) == 0)
    def _():
        sums_ref[...] = jnp.zeros_like(sums_ref)

    sums_ref[0:1, :] += jnp.sum(upstream * normal, axis=0, keepdims=True)
    sums_ref[1:2, :] += jnp.sum(upstream, axis=0, keepdims=True)
    grad = cot_ref[...].astype(F32) + norm_back(upstream, normal, inv_std, gain_ref[...])
    grad_ref[...] = grad
    low_ref[...] = grad.astype(BF16)


def middle_back(own, near, cot, middle, gain):
    rows, width = middle.shape
    steps = 2
    block = pl.BlockSpec((rows // steps, width), lambda i: (i, 0))
    return pl.pallas_call(
        middle_back_kernel,
        grid=(steps,),
        in_specs=[block] * 4 + [whole(1, width)],
        out_specs=[block, block, whole(2, width)],
        out_shape=[
            struct((rows, width), F32),
            struct((rows, width), BF16),
            struct((2, width), F32),
        ],
        compiler_params=params(),
        cost_estimate=cost(4),
        name="middle_back",
    )(own, near, cot, middle, gain)


def heads_back_kernel(experts, head_dim, own_ref, near_ref, full_ref, *refs):
    pack_refs, out_refs = refs[:2], refs[2:]
    lane = lane_of(ROWS)
    real = lane < head_dim
    grads = [mm_nt(ref[...], full_ref[0]) for ref in (own_ref, near_ref)]
    for h in range(2):

        @pl.when(pl.program_id(0) == h)
        def _():
            for block, grad in enumerate(grads):
                grad = grad.astype(BF16).astype(F32)
                pack = pack_refs[h][block].astype(F32)
                total = jnp.zeros((ROWS, LANES), F32)
                gates = jnp.zeros((ROWS, LANES), F32)
                for e in range(experts):
                    part = grad[:, e * LANES : (e + 1) * LANES]
                    total = total + pack[:, head_dim + e : head_dim + e + 1] * part
                    inner = jnp.sum(part * pack, axis=1, keepdims=True)
                    gates = jnp.where(lane == head_dim + e, inner, gates)
                out_refs[h][block] = jnp.where(real, total, gates).astype(BF16)


def heads_back(own, near, full, packs, experts, head_dim):
    heads, depth, width = full.shape
    rows = own.shape[0]
    return pl.pallas_call(
        functools.partial(heads_back_kernel, experts, head_dim),
        grid=(heads,),
        in_specs=[whole(rows, width)] * 2
        + [pl.BlockSpec((1, depth, width), lambda m: (m, 0, 0))]
        + [whole(2, ROWS, LANES)] * 2,
        out_specs=[whole(2, ROWS, LANES)] * 2,
        out_shape=[struct((2, ROWS, LANES), BF16)] * 2,
        compiler_params=params(),
        cost_estimate=cost(6),
        name="heads_back",
    )(own, near, full, *packs)


def feed_kernel(half, up_ref, cot_ref, wu_ref, wd_ref, far_u_ref, far_d_ref, *refs):
    refs = refs[-6:]
    hidden_ref, pre_grad_ref, out_ref, up_grad_ref, out_scr, up_scr = refs
    step = pl.program_id(0)
    steps = pl.num_programs(0)
    width = up_ref.shape[1]
    count = wu_ref.shape[1] // ROWS

    @pl.when(step == 0)
    def _():
        out_scr[...] = jnp.zeros_like(out_scr)
        up_scr[...] = jnp.zeros_like(up_scr)

    def part(w_up, w_down):
        pres, grads = [], []
        for b in range(count):
            cols = slice(b * ROWS, (b + 1) * ROWS)
            pres.append(mm(up_ref[...], w_up[:, cols]))
            grads.append(mm_nt(cot_ref[...], w_down[cols, :]))
        out, up_grad = None, None
        for b in range(count):
            cols = slice(b * ROWS, (b + 1) * ROWS)
            pre = pres[b]
            hidden_grad = grads[b].astype(BF16).astype(F32)
            phi = 0.5 * (1.0 + lax.erf(pre * ROOT_HALF))
            hidden = (pre * phi).astype(BF16)
            slope = phi + pre * jnp.exp(-0.5 * pre * pre) * INVERSE_ROOT_TAU
            pre_grad = (hidden_grad * slope).astype(BF16)
            hidden_ref[:, cols] = hidden
            pre_grad_ref[:, cols] = pre_grad
            out_part, up_part = mm(hidden, w_down[cols, :]), mm_nt(pre_grad, w_up[:, cols])
            out = out_part if out is None else out + out_part
            up_grad = up_part if up_grad is None else up_grad + up_part
        out_scr[...] += out
        up_scr[...] += up_grad

    @pl.when(step < half)
    def _():
        part(wu_ref[...], wd_ref[...])

    @pl.when(step >= half)
    def _():
        part(far_u_ref[...].reshape(width, -1), far_d_ref[...].reshape(-1, width))

    @pl.when(step == steps - 1)
    def _():
        out_ref[...] = out_scr[...].astype(out_ref.dtype)
        up_grad_ref[...] = up_scr[...].astype(up_grad_ref.dtype)


def feed(up_in, cot, w_up, w_down, far, dtype, *deps):
    rows, width = up_in.shape
    hidden = w_up.shape[1]
    size = 2 * ROWS
    half = hidden // size
    pieces, _, depth, _ = far.shape
    count = size // depth
    own = lambda i: jnp.minimum(i, half - 1)
    other = lambda i: jnp.maximum(i - half, 0)
    return pl.pallas_call(
        functools.partial(feed_kernel, half),
        grid=(2 * half,),
        in_specs=[
            whole(rows, width),
            whole(rows, width),
            pl.BlockSpec((width, size), lambda i: (0, own(i))),
            pl.BlockSpec((size, width), lambda i: (own(i), 0)),
            pl.BlockSpec((pieces, 1, depth, size), lambda i: (0, 0, 0, other(i))),
            pl.BlockSpec((count, 1, depth, width), lambda i: (other(i), 1, 0, 0)),
        ]
        + [pl.BlockSpec(memory_space=pl.ANY)] * len(deps),
        out_specs=[
            pl.BlockSpec((rows, size), lambda i: (0, i)),
            pl.BlockSpec((rows, size), lambda i: (0, i)),
            whole(rows, width),
            whole(rows, width),
        ],
        out_shape=[
            struct((rows, 2 * hidden), BF16),
            struct((rows, 2 * hidden), BF16),
            struct((rows, width), dtype),
            struct((rows, width), dtype),
        ],
        scratch_shapes=[pltpu.VMEM((rows, width), F32), pltpu.VMEM((rows, width), F32)],
        compiler_params=params(),
        cost_estimate=cost(10),
        name="feed",
    )(up_in, cot, w_up, w_down, far, far, *deps)


def feed_weights_kernel(count, half, *refs):
    lefts, refs = refs[: 2 * count], refs[2 * count :]
    rights, out_ref = refs[: 2 * count], refs[2 * count]
    step = pl.program_id(0)

    for which in range(2):

        @pl.when((step // half) % 2 == which)
        def _():
            total = None
            for m in range(which * count, (which + 1) * count):
                part = mm_tn(lefts[m][...], rights[m][...])
                total = part if total is None else total + part
            out_ref[...] = total.astype(BF16)


def feed_weights(ups, cots, pre_grads, hiddens):
    count = len(ups)
    rows, width = ups[0].shape
    hidden = hiddens[0].shape[1] // 2
    size = 512
    half = hidden // size

    def columns(which):
        def at(i):
            shard, inner = i // (2 * half), i % (2 * half)
            return (0, shard * half + jnp.clip(inner - which * half, 0, half - 1))

        return pl.BlockSpec((rows, size), at)

    return pl.pallas_call(
        functools.partial(feed_weights_kernel, count, half),
        grid=(4 * half,),
        in_specs=[whole(rows, width)] * (2 * count)
        + [columns(0)] * count
        + [columns(1)] * count,
        out_specs=pl.BlockSpec((width, size), lambda i: (0, i)),
        out_shape=struct((width, 4 * hidden), BF16),
        compiler_params=params(),
        cost_estimate=cost(11),
        name="feed_weights",
    )(*ups, *cots, *pre_grads, *hiddens)


def out_weights_kernel(experts, head_dim, heads, where_ref, *refs):
    pack_refs, refs = refs[:heads], refs[heads:]
    grad_ref, near_grad_ref, keep_ref, send_ref, mixed_scr, scr = refs
    real = lane_of(ROWS) < head_dim

    def fill(begin, pack):
        pack = pack.astype(F32)
        out = jnp.where(real, pack, 0.0)
        for e in range(experts):
            gate = pack[:, head_dim + e : head_dim + e + 1]
            mixed_scr[begin : begin + ROWS, e * LANES : (e + 1) * LANES] = (gate * out).astype(
                BF16
            )

    for m in range(heads):

        @pl.when(pl.program_id(0) == m)
        def _():
            fill(0, pack_refs[m][0])
            fill(ROWS, pack_refs[m][1])

    scr[...] = mm_tn(mixed_scr[:ROWS], grad_ref[...]) + mm_tn(
        mixed_scr[ROWS:], near_grad_ref[...]
    )
    for k in range(GROUP):
        target = send_ref if k % 2 else keep_ref
        lanes = pl.ds(pl.multiple_of((where_ref[0] ^ k) * LANES, LANES), LANES)
        for e in range(experts):
            target[k // 2, e * head_dim : (e + 1) * head_dim, :] = scr[
                e * LANES : e * LANES + head_dim, lanes
            ].astype(BF16)


def out_weights(where, packs, grad, near_grad, experts, head_dim):
    heads = len(packs)
    rows, width = grad.shape
    depth = experts * head_dim
    shape = (GROUP // 2, heads * depth, width // GROUP)
    spec = pl.BlockSpec((GROUP // 2, depth, width // GROUP), lambda m, w: (0, m, 0))
    return pl.pallas_call(
        functools.partial(out_weights_kernel, experts, head_dim, heads),
        grid_spec=pltpu.PrefetchScalarGridSpec(
            num_scalar_prefetch=1,
            grid=(heads,),
            in_specs=[whole(2, rows, LANES)] * heads + [whole(rows, width)] * 2,
            out_specs=[spec] * 2,
            scratch_shapes=[
                pltpu.VMEM((2 * rows, experts * LANES), BF16),
                pltpu.VMEM((experts * LANES, width), F32),
            ],
        ),
        out_shape=[struct(shape, BF16)] * 2,
        compiler_params=params(),
        cost_estimate=cost(5),
        name="out_weights",
    )(where, *packs, grad, near_grad)


def weights_kernel(
    experts,
    head_dim,
    counts,
    where_ref,
    normed_ref,
    key_ref,
    value_ref,
    gate_ref,
    query_ref,
    table_ref,
    rel_ref,
    w_ref,
    gain_ref,
    bias_ref,
    sums_ref,
    biases_ref,
    keep_ref,
    send_ref,
    small_ref,
    grads_scr,
    sum_scr,
    main_scr,
    rel_scr,
):
    step = pl.program_id(0)
    mem_steps, key_steps, rel_steps = counts
    query = (1 + experts) * LANES

    @pl.when(step == 0)
    def _():
        main_scr[...] = jnp.zeros_like(main_scr)
        sum_scr[...] = jnp.zeros_like(sum_scr)
        rel_scr[...] = jnp.zeros_like(rel_scr)

    def add(columns):
        grads = grads_scr[:, :columns]
        main_scr[:columns, :] += mm_tn(grads, normed_ref[...])
        sum_scr[0:1, :columns] += jnp.sum(grads.astype(F32), axis=0, keepdims=True)

    @pl.when(step < key_steps)
    def _():
        value_grad = value_ref[...]
        grads_scr[:, :LANES] = key_ref[...]
        for e in range(experts):
            gate = gate_ref[:, head_dim + e : head_dim + e + 1]
            grads_scr[:, LANES * (1 + e) : LANES * (2 + e)] = (gate * value_grad).astype(BF16)

    @pl.when(step < mem_steps)
    def _():
        add(query)

    @pl.when((step >= mem_steps) & (step < key_steps))
    def _():
        grads_scr[:, query:] = query_ref[...]
        add(query + LANES)

    @pl.when(step >= key_steps)
    def _():
        rel_scr[...] += mm_tn(rel_ref[...], table_ref[...])

    @pl.when(step == key_steps + rel_steps - 1)
    def _():
        weights = w_ref[...].astype(F32)
        sums = sum_scr[...].T
        bias_one = jnp.sum(weights * sums[:, 0:1], axis=0, keepdims=True)
        inner = jnp.sum(weights * main_scr[...], axis=0, keepdims=True)
        small_ref[...] = jnp.zeros_like(small_ref)
        small_ref[0:1, :] = (inner - bias_ref[...] * bias_one) / gain_ref[...]
        small_ref[1:2, :] = bias_one
        small_ref[2:4, :] = sums_ref[...]
        small_ref[4:6, pl.ds(pl.multiple_of(where_ref[1] * LANES, LANES), LANES)] = biases_ref[...]
        for k in range(GROUP):
            target = send_ref if k % 2 else keep_ref
            at = k // 2
            lanes = pl.ds(pl.multiple_of((where_ref[0] ^ k) * LANES, LANES), LANES)
            row = 0

            def put(source, begin, size):
                target[at, row : row + size, :] = source[begin : begin + size, lanes].astype(BF16)
                return row + size

            for section in range(2 + experts):
                row = put(main_scr, section * LANES, head_dim)
            row = put(rel_scr, 0, head_dim)
            target[at, row:, :] = jnp.concatenate(
                [
                    main_scr[head_dim : head_dim + 8, lanes],
                    main_scr[query + head_dim : query + head_dim + 8, lanes],
                ],
                axis=0,
            ).astype(BF16)


def weight_grads(
    where,
    normed,
    key_grad,
    value_grad,
    gates,
    query_grad,
    table,
    rel_grad,
    w_all,
    gain,
    bias,
    sums_two,
    bias_sums,
    mem,
    head_dim,
    experts,
):
    keys, width = normed.shape
    cols = (2 + experts) * LANES
    big = 4 * ROWS
    mem_steps, key_steps = mem // big, keys // big
    rel_steps = table.shape[0] // big
    counts = (mem_steps, key_steps, rel_steps)
    rows = (3 + experts) * head_dim + 16
    key_row = lambda i, w: (jnp.minimum(i, key_steps - 1), 0)
    tok_row = lambda i, w: (jnp.clip(i - mem_steps, 0, key_steps - mem_steps - 1), 0)
    rel_row = lambda i, w: (jnp.clip(i - key_steps, 0, rel_steps - 1), 0)
    half = GROUP // 2
    return pl.pallas_call(
        functools.partial(weights_kernel, experts, head_dim, counts),
        grid_spec=pltpu.PrefetchScalarGridSpec(
            num_scalar_prefetch=1,
            grid=(key_steps + rel_steps,),
            in_specs=[
                pl.BlockSpec((big, width), key_row),
                pl.BlockSpec((big, LANES), key_row),
                pl.BlockSpec((big, LANES), key_row),
                pl.BlockSpec((big, LANES), key_row),
                pl.BlockSpec((big, LANES), tok_row),
                pl.BlockSpec((big, width), rel_row),
                pl.BlockSpec((big, LANES), rel_row),
                whole(cols, width),
                whole(1, width),
                whole(1, width),
                whole(2, width),
                whole(2, LANES),
            ],
            out_specs=[
                whole(half, rows, LANES),
                whole(half, rows, LANES),
                whole(8, width),
            ],
            scratch_shapes=[
                pltpu.VMEM((big, cols), BF16),
                pltpu.VMEM((8, cols), F32),
                pltpu.VMEM((cols, width), F32),
                pltpu.VMEM((LANES, width), F32),
            ],
        ),
        out_shape=[
            struct((half, rows, LANES), BF16),
            struct((half, rows, LANES), BF16),
            struct((8, width), F32),
        ],
        compiler_params=params(),
        cost_estimate=cost(15),
        name="weight_grads",
    )(
        where,
        normed,
        key_grad,
        value_grad,
        gates,
        query_grad,
        table,
        rel_grad,
        w_all,
        gain,
        bias,
        sums_two,
        bias_sums,
    )


def token_kernel(experts, head_dim, own_ref, far_ref, w_own_ref, w_far_ref, *refs):
    out_refs, grads_scr, total_scr = refs[:2], refs[2], refs[3]
    step = pl.program_id(0)
    query = (1 + experts) * LANES
    cols = query + LANES
    real = lane_of(ROWS) < head_dim

    def part(pack_ref, weights):
        for block in range(2):
            rows = slice(block * ROWS, (block + 1) * ROWS)
            value_pack = pack_ref[block, 1].astype(F32)
            value_grad = jnp.where(real, value_pack, 0.0)
            grads_scr[rows, :LANES] = pack_ref[block, 0]
            for e in range(experts):
                gate = value_pack[:, head_dim + e : head_dim + e + 1]
                grads_scr[rows, LANES * (1 + e) : LANES * (2 + e)] = (gate * value_grad).astype(
                    BF16
                )
            grads_scr[rows, query:] = pack_ref[block, 2]
        return mm(grads_scr[...], weights)

    @pl.when(step == 0)
    def _():
        total_scr[...] = part(own_ref, w_own_ref[:cols, :])

    @pl.when(step == 1)
    def _():
        weights = w_far_ref[...].reshape(-1, w_far_ref.shape[2])
        total = total_scr[...] + part(far_ref, weights[:cols, :])
        out_refs[0][...] = total[:ROWS]
        out_refs[1][...] = total[ROWS:].astype(BF16)


def token_parts(own_pack, far_pack, own_w, far_w, head_dim, experts):
    width = own_w.shape[1]
    rows = 2 * ROWS
    cols = (2 + experts) * LANES
    return pl.pallas_call(
        functools.partial(token_kernel, experts, head_dim),
        grid=(2,),
        in_specs=[
            whole(*own_pack.shape),
            whole(*far_pack.shape),
            whole(*own_w.shape),
            whole(*far_w.shape),
        ],
        out_specs=[whole(ROWS, width)] * 2,
        out_shape=[struct((ROWS, width), F32), struct((ROWS, width), BF16)],
        scratch_shapes=[pltpu.VMEM((rows, cols), BF16), pltpu.VMEM((rows, width), F32)],
        compiler_params=params(),
        cost_estimate=cost(6),
        name="token_parts",
    )(own_pack, far_pack, own_w, far_w)


def token_sum_kernel(z_ref, tok_ref, mid_ref, gain_ref, own_ref, near_ref, out_ref):
    total = own_ref[...] + near_ref[...].astype(F32)
    normal, inv_std = norm_parts(tok_ref[...].astype(F32))
    out_ref[...] = mid_ref[...] + norm_back(total, normal, inv_std, gain_ref[...])


def token_sum(rank, tokens, middle_grad, gain, own, near):
    rows, width = middle_grad.shape
    return pl.pallas_call(
        token_sum_kernel,
        grid_spec=pltpu.PrefetchScalarGridSpec(
            num_scalar_prefetch=1,
            grid=(1,),
            in_specs=[
                pl.BlockSpec((rows, width), lambda i, z: (z[0], 0)),
                whole(rows, width),
                whole(1, width),
                whole(rows, width),
                whole(rows, width),
            ],
            out_specs=whole(rows, width),
        ),
        out_shape=struct((rows, width), F32),
        compiler_params=params(),
        cost_estimate=cost(4),
        name="token_sum",
    )(rank, tokens, middle_grad, gain, own, near)


def swap(array, axis, mask):
    size = lax.axis_size(axis)
    return lax.ppermute(array, axis, [(i, i ^ mask) for i in range(size)])


def plus(left, right):
    return (left.astype(F32) + right.astype(F32)).astype(BF16)


def scatter_first(keep, far):
    return [plus(keep[m], far[m]) for m in range(keep.shape[0])]


def scatter_sends(blocks, unit):
    return [swap(blocks[m], "dp", 2 * m * unit) for m in range(1, len(blocks))]


def scatter_done(own, fars, unit, axis):
    out = own.astype(F32)
    for far in fars:
        out = out + far.astype(F32)
    mask = unit // 2
    while mask:
        size = out.shape[axis] // 2
        bit = (lax.axis_index("dp") // mask) % 2
        mine = lax.dynamic_slice_in_dim(out, bit * size, size, axis)
        theirs = lax.dynamic_slice_in_dim(out, (1 - bit) * size, size, axis)
        out = mine + swap(theirs.astype(BF16), "dp", mask).astype(F32)
        mask //= 2
    return out


def spread(far, *gates):
    pieces = [swap(far, "dp", 2 * m) for m in range(1, GROUP // 2)]
    even = after(pile(far, *pieces), *gates)
    odd = swap(even, "dp", 1)
    return even, odd


def on_device(
    tokens,
    memory,
    segments,
    value_routes,
    output_routes,
    first_gain,
    first_bias,
    second_gain,
    second_bias,
    query_head_weight,
    key_weight,
    position_weight,
    value_weight,
    value_select,
    output_expert_selector,
    output_expert_weight,
    content_bias,
    position_bias,
    up_projection_weight,
    down_projection_weight,
    cotangent,
):
    mem_len = memory.shape[1]
    toks, width = tokens.shape
    head_dim = query_head_weight.shape[2]
    experts = value_select.shape[2]
    hidden = up_projection_weight.shape[1]
    parts = lax.axis_size("tensor")
    rank = lax.axis_index("tensor")
    dp = lax.axis_size("dp")
    at = lax.axis_index("dp")
    others = range(1, parts)
    near, far_shard = 1, 2
    rank_ref = rank.reshape(1).astype(jnp.int32)
    row = lambda v: v.reshape(1, -1)
    lanes = lambda v: jnp.pad(v, ((0, 0), (0, LANES - head_dim)))

    own_out = output_expert_weight[0]
    size = width // GROUP
    own_block = lax.dynamic_slice_in_dim(own_out, (at % GROUP) * size, size, 1)
    far_out = swap(own_block, "tensor", far_shard)
    span = mem_len
    fine = 32
    rates = jnp.exp(jnp.arange(width // 2).astype(F32) * (-2.0 * math.log(10000.0) / width))
    coarse_at = (span - 1 - fine * jnp.arange(span // fine)).astype(F32)[:, None] * rates[None, :]
    fine_at = jnp.arange(fine).astype(F32)[:, None] * rates[None, :]
    sin_a, cos_a = jnp.sin(coarse_at)[:, None, :], jnp.cos(coarse_at)[:, None, :]
    sin_b, cos_b = jnp.sin(fine_at)[None, :, :], jnp.cos(fine_at)[None, :, :]
    sin_table = jnp.concatenate(
        [sin_a * cos_b - cos_a * sin_b, cos_a * cos_b + sin_a * sin_b], axis=2
    )
    sin_table = lax.optimization_barrier(sin_table.reshape(span, width).astype(BF16))
    rel_weight = jnp.concatenate(
        [position_weight[0].T, jnp.zeros((LANES - head_dim, width), BF16)]
    )
    rel_reverse = mm_nt(sin_table, rel_weight).astype(BF16)

    w_all, normed, key_vecs, value_vecs, every, vgate, qc, qp, ogate = project(
        memory[0],
        tokens,
        row(first_gain),
        row(first_bias),
        (
            key_weight[0].T,
            value_select[0].T,
            value_weight[0].T,
            query_head_weight[0].T,
            output_expert_selector[0].T,
        ),
        value_routes[0, :, 0].T,
        output_routes[:, 0].T,
        lanes(content_bias),
        lanes(position_bias),
        experts,
        head_dim,
    )
    steps = toks // ROWS
    seg = segments[0]
    seg_keys = jnp.stack([seg[i * ROWS : i * ROWS + span + ROWS] for i in range(steps)])[:, None]
    seg_keys = after(seg_keys, far_out)
    heads, probs, *packs = attend(
        rank_ref,
        qc,
        qp,
        key_vecs,
        value_vecs,
        rel_reverse,
        seg_keys,
        seg[mem_len:, None],
        ogate,
        head_dim,
    )

    depth = width // dp
    feed_piece = jnp.stack(
        [
            lax.dynamic_slice_in_dim(up_projection_weight, at * depth, depth, 0),
            lax.dynamic_slice_in_dim(down_projection_weight, at * (hidden // dp), hidden // dp, 0),
        ]
    )
    far_feed = swap(feed_piece, "tensor", far_shard)
    far_feed = lax.all_gather(after(far_feed, packs[0]), "dp", axis=0)
    packs = [packs[0], swap(packs[1], "tensor", far_shard)]
    even, odd = spread(after(far_out, qc), packs[1])
    cots = [cotangent, swap(after(cotangent, packs[1]), "tensor", near)]
    piece = w_all.shape[0] // dp
    own_piece = lax.dynamic_slice_in_dim(w_all, at * piece, piece, 0)
    far_w = swap(after(own_piece, packs[1]), "tensor", far_shard)
    group_at = at % GROUP
    where = jnp.stack([group_at // 2, group_at % 2, rank]).astype(jnp.int32)
    full, own_part, near_part = mix(where, packs, own_out, even, odd, experts, head_dim)
    middle, up_in = middle_rows(
        rank_ref,
        tokens,
        after(own_part, far_w, cots[1]),
        swap(near_part, "tensor", near),
        row(second_gain),
        row(second_bias),
    )

    ups = [up_in, swap(up_in, "tensor", near)]
    unit = dp // GROUP
    where_grads = jnp.stack([at // unit, rank]).astype(jnp.int32)
    far_w = lax.all_gather(after(far_w, up_in), "dp", axis=0)
    shards = (up_projection_weight, down_projection_weight, far_feed)
    own_hidden, own_pre, own_result, own_up = feed(ups[0], cots[0], *shards, F32)
    near_hidden, near_pre, near_result, near_up = feed(ups[1], cots[1], *shards, BF16, own_pre)
    back_up = swap(near_up, "tensor", near)
    feed_sums = feed_weights(ups, cots, (own_pre, near_pre), (own_hidden, near_hidden))
    feed_sums = after(feed_sums, far_w, back_up)
    own_up = after(own_up, feed_sums)
    feed_sums = lax.psum_scatter(feed_sums, "dp", scatter_dimension=0, tiled=True)

    middle_grad, attn_grad, sums_two = middle_back(
        own_up, back_up, cotangent, middle, row(second_gain)
    )
    near_grad = swap(attn_grad, "tensor", near)
    backs = heads_back(attn_grad, near_grad, full, packs, experts, head_dim)
    out_keep, out_send = out_weights(where_grads, packs, attn_grad, near_grad, experts, head_dim)
    backs = [after(backs[0], out_keep), swap(backs[1], "tensor", far_shard)]
    back_out = swap(after(near_result, backs[1]), "tensor", near)

    key_grad, value_grad, query_grad, rel_grad, bias_sums, *grad_packs = attend_back(
        rank_ref,
        qc,
        qp,
        key_vecs,
        value_vecs,
        rel_reverse,
        probs,
        heads,
        ogate,
        every,
        vgate,
        backs,
        head_dim,
    )
    out_part = scatter_first(out_keep, swap(out_send, "dp", unit))
    rel_grad = after(rel_grad, *out_part, back_out)
    out_fars = scatter_sends(out_part, unit)
    far_pack = swap(grad_packs[1], "tensor", far_shard)
    keep, send, small = weight_grads(
        where_grads,
        normed,
        key_grad,
        value_grad,
        vgate,
        query_grad,
        sin_table,
        rel_grad,
        w_all,
        row(first_gain),
        row(first_bias),
        sums_two,
        bias_sums,
        mem_len,
        head_dim,
        experts,
    )
    token_own, token_near = token_parts(
        grad_packs[0], far_pack, w_all, after(far_w, keep), head_dim, experts
    )
    send, small = (after(each, token_near, span=20) for each in (send, small))
    token_near = swap(token_near, "tensor", near)
    kept_far = swap(send, "dp", unit)
    small_fars = [swap(small, "tensor", m) for m in others]
    out_fars = [after(far, send) for far in out_fars]
    out_sums = scatter_done(out_part[0], out_fars, unit, 1).reshape(2, experts * head_dim, -1)
    out_low = out_sums[1].astype(BF16)
    feed_own, feed_far = feed_sums[:, : 2 * hidden], feed_sums[:, 2 * hidden :]
    kept_far, feed_far, *small_fars = together(kept_far, feed_far, *small_fars)
    feed_far = swap(feed_far, "tensor", far_shard)
    out_far = swap(out_low, "tensor", far_shard)
    kept = scatter_first(keep, kept_far)
    for far in small_fars:
        small = small + far
    kept_fars = scatter_sends(kept, unit)
    small_fars = [swap(small, "dp", m) for m in range(2, GROUP, 2)]
    feed_far, *fars = together(feed_far, *kept_fars, *small_fars)
    kept_fars, small_fars = fars[: len(fars) // 2], fars[len(fars) // 2 :]
    for far in small_fars:
        small = small + far
    mask = GROUP
    while mask < dp:
        small = small + swap(small, "dp", mask)
        mask *= 2
    small = small + swap(small, "dp", 1)
    kept = scatter_done(kept[0], kept_fars, unit, 1)
    tokens_grad = token_sum(
        rank_ref, tokens, middle_grad, row(first_gain), token_own, token_near
    )
    result = (middle + own_result + after(back_out, keep).astype(F32)).astype(BF16)
    out_w = out_sums[0] + after(out_far, *kept_fars).astype(F32)
    feed_grads = feed_own.astype(F32) + feed_far.astype(F32)
    up_total = feed_grads[:, :hidden]
    down_total = feed_grads[:, hidden:].T
    biases = small[4:6, : parts * LANES].reshape(2, parts, LANES)[:, :, :head_dim]
    marks = [0, 1, 1 + experts, 2 + experts, 3 + experts]
    key_w, value_w, query_w, rel_w = (
        kept[a * head_dim : b * head_dim] for a, b in zip(marks, marks[1:])
    )
    select = marks[-1] * head_dim
    turn = lambda part: part.T[None]
    return (
        result,
        tokens_grad,
        small[0],
        small[1],
        small[2],
        small[3],
        turn(query_w),
        turn(key_w),
        turn(rel_w),
        turn(value_w),
        turn(kept[select : select + experts]),
        turn(kept[select + 8 : select + 8 + experts]),
        out_w[None],
        biases[0],
        biases[1],
        up_total,
        down_total,
    )


def solution(mesh):
    placed = (
        P("dp", None),
        P("dp", None, None),
        P("dp", None),
        P("dp", None, "tensor", None),
        P("dp", "tensor", None),
        P(),
        P(),
        P(),
        P(),
        P("tensor", None, None),
        P("tensor", None, None),
        P("tensor", None, None),
        P("tensor", None, None),
        P("tensor", None, None),
        P("tensor", None, None),
        P("tensor", None, None),
        P("tensor", None),
        P("tensor", None),
        P(None, "tensor"),
        P("tensor", None),
        P(("dp", "tensor"), None),
    )
    return jax.shard_map(
        on_device,
        mesh=mesh,
        in_specs=placed,
        out_specs=(
            P(("dp", "tensor"), None),
            P(("dp", "tensor"), None),
            P(),
            P(),
            P(),
            P(),
            P("tensor", "dp", None),
            P("tensor", "dp", None),
            P("tensor", "dp", None),
            P("tensor", "dp", None),
            P("tensor", "dp", None),
            P("tensor", "dp", None),
            P("tensor", None, "dp"),
            P(),
            P(),
            P("dp", "tensor"),
            P("tensor", "dp"),
        ),
        check_vma=False,
    )
```

```python
import functools
import math

import jax
import jax.numpy as jnp
from jax import lax
from jax.experimental import pallas as pl
from jax.experimental.pallas import tpu as pltpu
from jax.sharding import PartitionSpec as P

EPSILON = 1e-05
ROOT_HALF = 0.7071067811865476
INVERSE_ROOT_TAU = 0.3989422804014327
ROWS = 256
GROUP = 8
MIB = 1024 * 1024
BF16 = jnp.bfloat16
F32 = jnp.float32


def mm(left, right):
    return jnp.dot(left, right, preferred_element_type=F32)


def mm_nt(left, right):
    return lax.dot_general(left, right, (((1,), (1,)), ((), ())), preferred_element_type=F32)


def mm_tn(left, right):
    return lax.dot_general(left, right, (((0,), (0,)), ((), ())), preferred_element_type=F32)


def norm_parts(values):
    center = values - jnp.mean(values, axis=-1, keepdims=True)
    inv_std = lax.rsqrt(jnp.mean(center * center, axis=-1, keepdims=True) + EPSILON)
    return center * inv_std, inv_std


def norm_back(upstream, normal, inv_std, gain):
    scaled = upstream * gain
    return inv_std * (
        scaled
        - jnp.mean(scaled, axis=-1, keepdims=True)
        - normal * jnp.mean(scaled * normal, axis=-1, keepdims=True)
    )


def params():
    return pltpu.CompilerParams(vmem_limit_bytes=63 * MIB)


def cost(microseconds):
    return pl.CostEstimate(
        flops=int(microseconds * 1.15e9), bytes_accessed=0, transcendentals=0
    )


def struct(shape, dtype):
    return jax.ShapeDtypeStruct(shape, dtype)


def whole(*shape):
    return pl.BlockSpec(shape, lambda *_: (0,) * len(shape))

LANES = 128


def lane_of(rows):
    return lax.broadcasted_iota(jnp.int32, (rows, LANES), 1)


def picked(routes, head_dim):
    rows = routes.shape[1]
    routes = jnp.concatenate([routes, jnp.zeros((6, rows), jnp.int32)], axis=0).astype(F32).T
    lane = (lane_of(rows) - head_dim).astype(F32)
    return (lane == routes[:, 0:1]) | (lane == routes[:, 1:2])


def after(array, *deps, span=0):
    def body(*refs):
        del refs

    spec = pl.BlockSpec(memory_space=pl.ANY)
    return pl.pallas_call(
        body,
        in_specs=[spec] * (1 + len(deps)),
        out_specs=spec,
        out_shape=struct(array.shape, array.dtype),
        input_output_aliases={0: 0},
        cost_estimate=cost(span),
        name="after",
    )(array, *deps)


def together(*arrays, span=0):
    def body(*refs):
        del refs

    spec = pl.BlockSpec(memory_space=pl.ANY)
    return pl.pallas_call(
        body,
        in_specs=[spec] * len(arrays),
        out_specs=[spec] * len(arrays),
        out_shape=[struct(a.shape, a.dtype) for a in arrays],
        input_output_aliases={i: i for i in range(len(arrays))},
        cost_estimate=cost(span),
        name="together",
    )(*arrays)


def pile(*arrays):
    def body(*refs):
        for i, ref in enumerate(refs[:-1]):
            refs[-1][i] = ref[...]

    shape = arrays[0].shape
    return pl.pallas_call(
        body,
        in_specs=[whole(*shape)] * len(arrays),
        out_specs=whole(len(arrays), *shape),
        out_shape=struct((len(arrays),) + shape, arrays[0].dtype),
        grid=(1,),
        compiler_params=params(),
        cost_estimate=cost(2),
        name="pile",
    )(*arrays)


def project_kernel(
    experts,
    head_dim,
    mem_steps,
    scale,
    mem_ref,
    tok_ref,
    gain_ref,
    bias_ref,
    key_w_ref,
    vsel_ref,
    value_w_ref,
    query_w_ref,
    osel_ref,
    vroute_ref,
    oroute_ref,
    cb_ref,
    pb_ref,
    w_out_ref,
    normed_ref,
    key_ref,
    val_ref,
    every_ref,
    vgate_ref,
    qc_ref,
    qp_ref,
    ogate_ref,
    w_ref,
):
    step = pl.program_id(0)
    query = (1 + experts) * LANES

    @pl.when(step == 0)
    def _():
        w_ref[...] = jnp.zeros_like(w_ref)
        w_ref[:head_dim, :] = key_w_ref[...]
        w_ref[head_dim : head_dim + experts, :] = vsel_ref[...]
        for e in range(experts):
            w_ref[(1 + e) * LANES : (1 + e) * LANES + head_dim, :] = value_w_ref[
                e * head_dim : (e + 1) * head_dim, :
            ]
        w_ref[query : query + head_dim, :] = query_w_ref[...]
        w_ref[query + head_dim : query + head_dim + experts, :] = osel_ref[...]

    size = w_out_ref.shape[0]
    w_out_ref[...] = w_ref[pl.ds(pl.multiple_of(step * size, size), size), :]

    def rows_part():
        blocks = [slice(i * ROWS, (i + 1) * ROWS) for i in range(tok_ref.shape[0] // ROWS)]
        normed, outs = [], []
        for rows in blocks:
            block = jnp.where(step < mem_steps, mem_ref[rows, :], tok_ref[rows, :])
            normal, _ = norm_parts(block.astype(F32))
            normed.append((normal * gain_ref[...] + bias_ref[...]).astype(BF16))
            outs.append(mm_nt(normed[-1], w_ref[: query + LANES, :]))
        lane = lane_of(ROWS)
        real = lane < head_dim
        for rows, norm, out in zip(blocks, normed, outs):
            normed_ref[rows, :] = norm
            first = out[:, :LANES]
            key_ref[rows, :] = jnp.where(real, first, 0.0).astype(BF16)
            every_ref[rows, :] = out[:, LANES:query].astype(BF16)
            gate = jnp.where(picked(vroute_ref[:, rows], head_dim), jax.nn.sigmoid(first), 0.0)
            vgate_ref[rows, :] = gate
            value = jnp.zeros((ROWS, LANES), F32)
            for e in range(experts):
                value = value + gate[:, head_dim + e : head_dim + e + 1] * (
                    out[:, (1 + e) * LANES : (2 + e) * LANES]
                )
            val_ref[rows, :] = value.astype(BF16)
            q = out[:, query:]
            qc_ref[rows, :] = jnp.where(real, (q + cb_ref[...]) * scale, 0.0).astype(BF16)
            qp_ref[rows, :] = jnp.where(real, (q + pb_ref[...]) * scale, 0.0).astype(BF16)
            ogate_ref[rows, :] = jnp.where(
                picked(oroute_ref[:, rows], head_dim), jax.nn.sigmoid(q), 0.0
            )

    rows_part()


def project(memory, tokens, gain, bias, weights, vroutes, oroutes, cb, pb, experts, head_dim):
    mem, width = memory.shape
    toks = tokens.shape[0]
    big = 2 * ROWS
    mem_steps, tok_steps = mem // big, toks // big
    steps = mem_steps + tok_steps
    keys = mem + toks
    cols = width
    mem_row = lambda i: (jnp.minimum(i, mem_steps - 1), 0)
    tok_row = lambda i: (jnp.maximum(i - mem_steps, 0), 0)
    row = lambda i: (i, 0)
    return pl.pallas_call(
        functools.partial(project_kernel, experts, head_dim, mem_steps, head_dim ** (-0.5)),
        grid=(steps,),
        in_specs=[
            pl.BlockSpec((big, width), mem_row),
            pl.BlockSpec((big, width), tok_row),
            whole(1, width),
            whole(1, width),
        ]
        + [whole(*w.shape) for w in weights]
        + [
            pl.BlockSpec((vroutes.shape[0], big), lambda i: (0, i)),
            pl.BlockSpec((oroutes.shape[0], big), lambda i: (0, jnp.maximum(i - mem_steps, 0))),
            whole(1, LANES),
            whole(1, LANES),
        ],
        out_specs=[
            pl.BlockSpec((cols // steps, width), row),
            pl.BlockSpec((big, width), row),
            pl.BlockSpec((big, LANES), row),
            pl.BlockSpec((big, LANES), row),
            pl.BlockSpec((big, experts * LANES), row),
            pl.BlockSpec((big, LANES), row),
            pl.BlockSpec((big, LANES), tok_row),
            pl.BlockSpec((big, LANES), tok_row),
            pl.BlockSpec((big, LANES), tok_row),
        ],
        out_shape=[
            struct((cols, width), BF16),
            struct((keys, width), BF16),
            struct((keys, LANES), BF16),
            struct((keys, LANES), BF16),
            struct((keys, experts * LANES), BF16),
            struct((keys, LANES), F32),
            struct((toks, LANES), BF16),
            struct((toks, LANES), BF16),
            struct((toks, LANES), F32),
        ],
        scratch_shapes=[pltpu.VMEM((cols, width), BF16)],
        compiler_params=params(),
        cost_estimate=cost(12),
        name="project",
    )(memory, tokens, gain, bias, *weights, vroutes, oroutes, cb, pb)


def attend_kernel(
    span,
    head_dim,
    count,
    z_ref,
    qc_ref,
    qp_ref,
    key_ref,
    val_ref,
    rel_ref,
    segk_ref,
    segq_ref,
    ogate_ref,
    heads_ref,
    probs_ref,
    *pack_refs,
):
    step = pl.program_id(0)
    wide = span + ROWS
    column = lax.broadcasted_iota(jnp.int32, (ROWS, ROWS), 1)
    causal = column <= lax.broadcasted_iota(jnp.int32, (ROWS, ROWS), 0)
    for b in range(count):
        rows = slice(b * ROWS, (b + 1) * ROWS)
        window = pl.ds((step * count + b) * ROWS, wide)
        content = mm_nt(qc_ref[rows, :], key_ref[window, :])
        reverse = mm_nt(qp_ref[rows, :], rel_ref[...])
        reverse = jnp.concatenate([reverse, jnp.zeros((ROWS, ROWS), F32)], axis=1)
        scores = content + pltpu.roll(reverse, 1, 1, stride=1, stride_axis=0)
        own = jnp.concatenate([segq_ref[:, rows], jnp.zeros((7, ROWS), jnp.int32)], axis=0)
        same = segk_ref[b].astype(F32) == own.astype(F32).T[:, 0:1]
        allowed = jnp.concatenate([same[:, :span], same[:, span:] & causal], axis=1)
        scores = jnp.where(allowed, scores, -1e30)
        expo = jnp.exp(scores - jnp.max(scores, axis=1, keepdims=True))
        probs = (expo * (1.0 / jnp.sum(expo, axis=1, keepdims=True))).astype(BF16)
        probs_ref[rows, :] = probs
        heads = mm(probs, val_ref[window, :])
        heads_ref[rows, :] = heads
        packed = jnp.where(lane_of(ROWS) < head_dim, heads, ogate_ref[rows, :]).astype(BF16)
        slot = (step * count + b) ^ z_ref[0]
        for side, pack_ref in enumerate(pack_refs):

            @pl.when(slot // 2 == side)
            def _():
                pack_ref[slot % 2] = packed


def attend(rank, qc, qp, key_vecs, value_vecs, rel_reverse, seg_keys, seg_query, ogate, head_dim):
    toks = qc.shape[0]
    keys = key_vecs.shape[0]
    span = rel_reverse.shape[0]
    steps = toks // ROWS
    count = 1
    big = count * ROWS
    wide = span + ROWS
    row = lambda i, z: (i, 0)
    return pl.pallas_call(
        functools.partial(attend_kernel, span, head_dim, count),
        grid_spec=pltpu.PrefetchScalarGridSpec(
            num_scalar_prefetch=1,
            grid=(steps // count,),
            in_specs=[
                pl.BlockSpec((big, LANES), row),
                pl.BlockSpec((big, LANES), row),
                whole(keys, LANES),
                whole(keys, LANES),
                whole(span, LANES),
                pl.BlockSpec((count, 1, wide), lambda i, z: (i, 0, 0)),
                pl.BlockSpec((1, big), lambda i, z: (0, i)),
                pl.BlockSpec((big, LANES), row),
            ],
            out_specs=[
                pl.BlockSpec((big, LANES), row),
                pl.BlockSpec((big, wide), row),
            ]
            + [whole(2, ROWS, LANES)] * (steps // 2),
        ),
        out_shape=[struct((toks, LANES), F32), struct((toks, wide), BF16)]
        + [struct((2, ROWS, LANES), BF16)] * (steps // 2),
        compiler_params=params(),
        cost_estimate=cost(8),
        name="attend",
    )(rank, qc, qp, key_vecs, value_vecs, rel_reverse, seg_keys, seg_query, ogate)


def attend_back_kernel(
    span,
    experts,
    head_dim,
    parts,
    z_ref,
    qc_ref,
    qp_ref,
    key_ref,
    val_ref,
    rel_ref,
    probs_ref,
    heads_ref,
    ogate_ref,
    every_ref,
    vgate_ref,
    *refs,
):
    back_refs, refs = refs[: parts // 2], refs[parts // 2 :]
    key_grad_ref, value_grad_ref, query_grad_ref, rel_grad_ref, bias_ref = refs[:5]
    pack_refs, refs = refs[5 : 5 + parts // 2], refs[5 + parts // 2 :]
    keys_scr, values_scr, rel_scr, query_scr, back_scr = refs
    step = pl.program_id(0)
    steps = pl.num_programs(0)
    wide = span + ROWS
    mem = keys_scr.shape[0] - steps * ROWS
    scale = head_dim ** (-0.5)
    real = lane_of(ROWS) < head_dim

    @pl.when(step == 0)
    def _():
        keys_scr[...] = jnp.zeros_like(keys_scr)
        values_scr[...] = jnp.zeros_like(values_scr)
        rel_scr[...] = jnp.zeros_like(rel_scr)
        bias_ref[...] = jnp.zeros_like(bias_ref)

    slot = step ^ z_ref[0]
    for side, back_ref in enumerate(back_refs):

        @pl.when(slot // 2 == side)
        def _():
            back_scr[...] = back_ref[slot % 2]

    window = pl.ds(step * ROWS, wide)
    keys = key_ref[window, :]
    vals = val_ref[window, :]
    back = back_scr[...].astype(F32)
    out_grad = jnp.where(real, back, 0.0)
    delta = jnp.sum(out_grad * heads_ref[...], axis=1, keepdims=True)
    out_grad = out_grad.astype(BF16)
    probs = probs_ref[...]
    probs_grad = mm_nt(out_grad, vals)
    score_grad = (probs.astype(F32) * (probs_grad - delta)).astype(BF16)
    content_grad = mm(score_grad, keys).astype(BF16).astype(F32) * scale
    keys_scr[window, :] += mm_tn(score_grad, qc_ref[...])
    values_scr[window, :] += mm_tn(probs, out_grad)
    flip = (
        lax.broadcasted_iota(jnp.int32, (ROWS, ROWS), 0)
        + lax.broadcasted_iota(jnp.int32, (ROWS, ROWS), 1)
        == ROWS - 1
    ).astype(BF16)
    turned = mm(flip, score_grad)
    turned = pltpu.roll(turned, span, 1, stride=1, stride_axis=0)[:, :span].astype(BF16)
    place_grad = mm(turned, rel_ref[...]).astype(BF16)
    position_grad = mm(flip, place_grad) * scale
    rel_scr[...] += mm_tn(turned, mm(flip, qp_ref[...]).astype(BF16))
    bias_ref[0:1, :] += jnp.sum(content_grad, axis=0, keepdims=True)
    bias_ref[1:2, :] += jnp.sum(position_grad, axis=0, keepdims=True)
    gate = ogate_ref[...]
    query_grad = jnp.where(real, content_grad + position_grad, back * gate * (1.0 - gate))
    query_grad = query_grad.astype(BF16)
    query_grad_ref[...] = query_grad
    query_scr[pl.ds(step * ROWS, ROWS), :] = query_grad

    @pl.when(step == steps - 1)
    def _():
        rel_grad_ref[...] = rel_scr[...].astype(BF16)

        @pl.loop(0, (mem + steps * ROWS) // ROWS)
        def _(block):
            rows = pl.ds(block * ROWS, ROWS)
            value_grad = values_scr[rows, :]
            gates = vgate_ref[rows, :]
            value_grad_ref[rows, :] = value_grad
            logit = keys_scr[rows, :]
            lane = lane_of(ROWS)
            for e in range(experts):
                part = every_ref[rows, e * LANES : (e + 1) * LANES].astype(F32)
                total = jnp.sum(value_grad * part, axis=1, keepdims=True)
                logit = jnp.where(lane == head_dim + e, total, logit)
            key_grad = jnp.where(real, logit, logit * gates * (1.0 - gates)).astype(BF16)
            key_grad_ref[rows, :] = key_grad

            @pl.when(block * ROWS >= mem)
            def _():
                place = block - mem // ROWS
                slot = place ^ z_ref[0]
                value_pack = jnp.where(real, value_grad, gates).astype(BF16)
                for side, pack_ref in enumerate(pack_refs):

                    @pl.when(slot // 2 == side)
                    def _():
                        pack_ref[slot % 2, 0] = key_grad
                        pack_ref[slot % 2, 1] = value_pack
                        pack_ref[slot % 2, 2] = query_scr[pl.ds(place * ROWS, ROWS), :]


def attend_back(
    rank,
    qc,
    qp,
    key_vecs,
    value_vecs,
    rel_reverse,
    probs,
    heads,
    ogate,
    every,
    vgate,
    backs,
    head_dim,
):
    toks = qc.shape[0]
    keys = key_vecs.shape[0]
    span = rel_reverse.shape[0]
    steps = toks // ROWS
    wide = span + ROWS
    experts = every.shape[1] // LANES
    row = lambda i, z: (i, 0)
    return pl.pallas_call(
        functools.partial(attend_back_kernel, span, experts, head_dim, steps),
        grid_spec=pltpu.PrefetchScalarGridSpec(
            num_scalar_prefetch=1,
            grid=(steps,),
            in_specs=[
                pl.BlockSpec((ROWS, LANES), row),
                pl.BlockSpec((ROWS, LANES), row),
                whole(keys, LANES),
                whole(keys, LANES),
                whole(span, LANES),
                pl.BlockSpec((ROWS, wide), row),
                pl.BlockSpec((ROWS, LANES), row),
                pl.BlockSpec((ROWS, LANES), row),
                whole(keys, experts * LANES),
                whole(keys, LANES),
            ]
            + [whole(2, ROWS, LANES)] * (steps // 2),
            out_specs=[
                whole(keys, LANES),
                whole(keys, LANES),
                pl.BlockSpec((ROWS, LANES), row),
                whole(span, LANES),
                whole(2, LANES),
            ]
            + [whole(2, 3, ROWS, LANES)] * (steps // 2),
            scratch_shapes=[
                pltpu.VMEM((keys, LANES), F32),
                pltpu.VMEM((keys, LANES), F32),
                pltpu.VMEM((span, LANES), F32),
                pltpu.VMEM((toks, LANES), BF16),
                pltpu.VMEM((ROWS, LANES), BF16),
            ],
        ),
        out_shape=[
            struct((keys, LANES), BF16),
            struct((keys, LANES), F32),
            struct((toks, LANES), BF16),
            struct((span, LANES), BF16),
            struct((2, LANES), F32),
        ]
        + [struct((2, 3, ROWS, LANES), BF16)] * (steps // 2),
        compiler_params=params(),
        cost_estimate=cost(15),
        name="attend_back",
    )(rank, qc, qp, key_vecs, value_vecs, rel_reverse, probs, heads, ogate, every, vgate, *backs)


def mix_kernel(experts, head_dim, where_ref, *refs):
    pack_refs, refs = refs[:2], refs[2:]
    own_ref, even_ref, odd_ref, full_ref, own_part_ref, near_part_ref, mixed_scr = refs
    step = pl.program_id(0)

    @pl.when(step == 0)
    def _():
        real = lane_of(ROWS) < head_dim
        for h in range(2):
            for block in range(2):
                pack = pack_refs[h][block].astype(F32)
                out = jnp.where(real, pack, 0.0)
                rows = slice(block * ROWS, (block + 1) * ROWS)
                for e in range(experts):
                    gate = pack[:, head_dim + e : head_dim + e + 1]
                    mixed_scr[h, rows, e * LANES : (e + 1) * LANES] = (gate * out).astype(BF16)

    turned = where_ref[1] == 1
    even, odd = even_ref[0], odd_ref[0]
    far = jnp.concatenate([jnp.where(turned, odd, even), jnp.where(turned, even, odd)], axis=1)
    total = None
    for h, weight in enumerate((own_ref[...], far)):
        for e in range(experts):
            full_ref[h, e * LANES : e * LANES + head_dim, :] = weight[
                e * head_dim : (e + 1) * head_dim
            ]
            full_ref[h, e * LANES + head_dim : (e + 1) * LANES, :] = jnp.zeros(
                (LANES - head_dim, weight.shape[1]), BF16
            )
        part = mm(mixed_scr[h], full_ref[h])
        total = part if total is None else total + part
    own_part_ref[...] = total[:ROWS]
    near_part_ref[...] = total[ROWS:].astype(BF16)


def mix(where, packs, own_weight, even, odd, experts, head_dim):
    depth, width = own_weight.shape
    steps = even.shape[0]
    size = width // steps
    column = lambda s, w: (0, w[0] ^ s)
    return pl.pallas_call(
        functools.partial(mix_kernel, experts, head_dim),
        grid_spec=pltpu.PrefetchScalarGridSpec(
            num_scalar_prefetch=1,
            grid=(steps,),
            in_specs=[whole(2, ROWS, LANES)] * 2
            + [
                pl.BlockSpec((depth, size), column),
                pl.BlockSpec((1,) + even.shape[1:], lambda s, w: (s, 0, 0)),
                pl.BlockSpec((1,) + odd.shape[1:], lambda s, w: (s, 0, 0)),
            ],
            out_specs=[
                pl.BlockSpec((2, experts * LANES, size), lambda s, w: (0, 0, w[0] ^ s)),
                pl.BlockSpec((ROWS, size), column),
                pl.BlockSpec((ROWS, size), column),
            ],
            scratch_shapes=[pltpu.VMEM((2, 2 * ROWS, experts * LANES), BF16)],
        ),
        out_shape=[
            struct((2, experts * LANES, width), BF16),
            struct((ROWS, width), F32),
            struct((ROWS, width), BF16),
        ],
        compiler_params=params(),
        cost_estimate=cost(7),
        name="mix",
    )(where, *packs, own_weight, even, odd)


def middle_kernel(z_ref, tok_ref, own_ref, near_ref, gain_ref, bias_ref, middle_ref, up_ref):
    middle = tok_ref[...].astype(F32) + (own_ref[...] + near_ref[...].astype(F32))
    middle_ref[...] = middle
    normal, _ = norm_parts(middle)
    up_ref[...] = (normal * gain_ref[...] + bias_ref[...]).astype(BF16)


def middle_rows(rank, tokens, own, near, gain, bias):
    rows, width = own.shape
    steps = 2
    block = pl.BlockSpec((rows // steps, width), lambda i, z: (i, 0))
    return pl.pallas_call(
        middle_kernel,
        grid_spec=pltpu.PrefetchScalarGridSpec(
            num_scalar_prefetch=1,
            grid=(steps,),
            in_specs=[
                pl.BlockSpec((rows // steps, width), lambda i, z: (z[0] * steps + i, 0)),
                block,
                block,
                whole(1, width),
                whole(1, width),
            ],
            out_specs=[block, block],
        ),
        out_shape=[struct((rows, width), F32), struct((rows, width), BF16)],
        compiler_params=params(),
        cost_estimate=cost(3),
        name="middle",
    )(rank, tokens, own, near, gain, bias)


def middle_back_kernel(
    own_ref, near_ref, cot_ref, middle_ref, gain_ref, grad_ref, low_ref, sums_ref
):
    upstream = own_ref[...].astype(F32) + near_ref[...].astype(F32)
    normal, inv_std = norm_parts(middle_ref[...])

    @pl.when(pl.program_id(0) == 0)
    def _():
        sums_ref[...] = jnp.zeros_like(sums_ref)

    sums_ref[0:1, :] += jnp.sum(upstream * normal, axis=0, keepdims=True)
    sums_ref[1:2, :] += jnp.sum(upstream, axis=0, keepdims=True)
    grad = cot_ref[...].astype(F32) + norm_back(upstream, normal, inv_std, gain_ref[...])
    grad_ref[...] = grad
    low_ref[...] = grad.astype(BF16)


def middle_back(own, near, cot, middle, gain):
    rows, width = middle.shape
    steps = 2
    block = pl.BlockSpec((rows // steps, width), lambda i: (i, 0))
    return pl.pallas_call(
        middle_back_kernel,
        grid=(steps,),
        in_specs=[block] * 4 + [whole(1, width)],
        out_specs=[block, block, whole(2, width)],
        out_shape=[
            struct((rows, width), F32),
            struct((rows, width), BF16),
            struct((2, width), F32),
        ],
        compiler_params=params(),
        cost_estimate=cost(4),
        name="middle_back",
    )(own, near, cot, middle, gain)


def heads_back_kernel(experts, head_dim, own_ref, near_ref, full_ref, *refs):
    pack_refs, out_refs = refs[:2], refs[2:]
    lane = lane_of(ROWS)
    real = lane < head_dim
    grads = [mm_nt(ref[...], full_ref[0]) for ref in (own_ref, near_ref)]
    for h in range(2):

        @pl.when(pl.program_id(0) == h)
        def _():
            for block, grad in enumerate(grads):
                grad = grad.astype(BF16).astype(F32)
                pack = pack_refs[h][block].astype(F32)
                total = jnp.zeros((ROWS, LANES), F32)
                gates = jnp.zeros((ROWS, LANES), F32)
                for e in range(experts):
                    part = grad[:, e * LANES : (e + 1) * LANES]
                    total = total + pack[:, head_dim + e : head_dim + e + 1] * part
                    inner = jnp.sum(part * pack, axis=1, keepdims=True)
                    gates = jnp.where(lane == head_dim + e, inner, gates)
                out_refs[h][block] = jnp.where(real, total, gates).astype(BF16)


def heads_back(own, near, full, packs, experts, head_dim):
    heads, depth, width = full.shape
    rows = own.shape[0]
    return pl.pallas_call(
        functools.partial(heads_back_kernel, experts, head_dim),
        grid=(heads,),
        in_specs=[whole(rows, width)] * 2
        + [pl.BlockSpec((1, depth, width), lambda m: (m, 0, 0))]
        + [whole(2, ROWS, LANES)] * 2,
        out_specs=[whole(2, ROWS, LANES)] * 2,
        out_shape=[struct((2, ROWS, LANES), BF16)] * 2,
        compiler_params=params(),
        cost_estimate=cost(6),
        name="heads_back",
    )(own, near, full, *packs)


def feed_kernel(half, up_ref, cot_ref, wu_ref, wd_ref, far_u_ref, far_d_ref, *refs):
    refs = refs[-6:]
    hidden_ref, pre_grad_ref, out_ref, up_grad_ref, out_scr, up_scr = refs
    step = pl.program_id(0)
    steps = pl.num_programs(0)
    width = up_ref.shape[1]
    count = wu_ref.shape[1] // ROWS

    @pl.when(step == 0)
    def _():
        out_scr[...] = jnp.zeros_like(out_scr)
        up_scr[...] = jnp.zeros_like(up_scr)

    def part(w_up, w_down):
        pres, grads = [], []
        for b in range(count):
            cols = slice(b * ROWS, (b + 1) * ROWS)
            pres.append(mm(up_ref[...], w_up[:, cols]))
            grads.append(mm_nt(cot_ref[...], w_down[cols, :]))
        out, up_grad = None, None
        for b in range(count):
            cols = slice(b * ROWS, (b + 1) * ROWS)
            pre = pres[b]
            hidden_grad = grads[b].astype(BF16).astype(F32)
            phi = 0.5 * (1.0 + lax.erf(pre * ROOT_HALF))
            hidden = (pre * phi).astype(BF16)
            slope = phi + pre * jnp.exp(-0.5 * pre * pre) * INVERSE_ROOT_TAU
            pre_grad = (hidden_grad * slope).astype(BF16)
            hidden_ref[:, cols] = hidden
            pre_grad_ref[:, cols] = pre_grad
            out_part, up_part = mm(hidden, w_down[cols, :]), mm_nt(pre_grad, w_up[:, cols])
            out = out_part if out is None else out + out_part
            up_grad = up_part if up_grad is None else up_grad + up_part
        out_scr[...] += out
        up_scr[...] += up_grad

    @pl.when(step < half)
    def _():
        part(wu_ref[...], wd_ref[...])

    @pl.when(step >= half)
    def _():
        part(far_u_ref[...].reshape(width, -1), far_d_ref[...].reshape(-1, width))

    @pl.when(step == steps - 1)
    def _():
        out_ref[...] = out_scr[...].astype(out_ref.dtype)
        up_grad_ref[...] = up_scr[...].astype(up_grad_ref.dtype)


def feed(up_in, cot, w_up, w_down, far, dtype, *deps):
    rows, width = up_in.shape
    hidden = w_up.shape[1]
    size = 2 * ROWS
    half = hidden // size
    pieces, _, depth, _ = far.shape
    count = size // depth
    own = lambda i: jnp.minimum(i, half - 1)
    other = lambda i: jnp.maximum(i - half, 0)
    return pl.pallas_call(
        functools.partial(feed_kernel, half),
        grid=(2 * half,),
        in_specs=[
            whole(rows, width),
            whole(rows, width),
            pl.BlockSpec((width, size), lambda i: (0, own(i))),
            pl.BlockSpec((size, width), lambda i: (own(i), 0)),
            pl.BlockSpec((pieces, 1, depth, size), lambda i: (0, 0, 0, other(i))),
            pl.BlockSpec((count, 1, depth, width), lambda i: (other(i), 1, 0, 0)),
        ]
        + [pl.BlockSpec(memory_space=pl.ANY)] * len(deps),
        out_specs=[
            pl.BlockSpec((rows, size), lambda i: (0, i)),
            pl.BlockSpec((rows, size), lambda i: (0, i)),
            whole(rows, width),
            whole(rows, width),
        ],
        out_shape=[
            struct((rows, 2 * hidden), BF16),
            struct((rows, 2 * hidden), BF16),
            struct((rows, width), dtype),
            struct((rows, width), dtype),
        ],
        scratch_shapes=[pltpu.VMEM((rows, width), F32), pltpu.VMEM((rows, width), F32)],
        compiler_params=params(),
        cost_estimate=cost(10),
        name="feed",
    )(up_in, cot, w_up, w_down, far, far, *deps)


def feed_weights_kernel(count, half, *refs):
    lefts, refs = refs[: 2 * count], refs[2 * count :]
    rights, out_ref = refs[: 2 * count], refs[2 * count]
    step = pl.program_id(0)

    for which in range(2):

        @pl.when((step // half) % 2 == which)
        def _():
            total = None
            for m in range(which * count, (which + 1) * count):
                part = mm_tn(lefts[m][...], rights[m][...])
                total = part if total is None else total + part
            out_ref[...] = total.astype(BF16)


def feed_weights(ups, cots, pre_grads, hiddens):
    count = len(ups)
    rows, width = ups[0].shape
    hidden = hiddens[0].shape[1] // 2
    size = 512
    half = hidden // size

    def columns(which):
        def at(i):
            shard, inner = i // (2 * half), i % (2 * half)
            return (0, shard * half + jnp.clip(inner - which * half, 0, half - 1))

        return pl.BlockSpec((rows, size), at)

    return pl.pallas_call(
        functools.partial(feed_weights_kernel, count, half),
        grid=(4 * half,),
        in_specs=[whole(rows, width)] * (2 * count)
        + [columns(0)] * count
        + [columns(1)] * count,
        out_specs=pl.BlockSpec((width, size), lambda i: (0, i)),
        out_shape=struct((width, 4 * hidden), BF16),
        compiler_params=params(),
        cost_estimate=cost(11),
        name="feed_weights",
    )(*ups, *cots, *pre_grads, *hiddens)


def out_weights_kernel(experts, head_dim, heads, where_ref, *refs):
    pack_refs, refs = refs[:heads], refs[heads:]
    grad_ref, near_grad_ref, keep_ref, send_ref, mixed_scr, scr = refs
    real = lane_of(ROWS) < head_dim

    def fill(begin, pack):
        pack = pack.astype(F32)
        out = jnp.where(real, pack, 0.0)
        for e in range(experts):
            gate = pack[:, head_dim + e : head_dim + e + 1]
            mixed_scr[begin : begin + ROWS, e * LANES : (e + 1) * LANES] = (gate * out).astype(
                BF16
            )

    for m in range(heads):

        @pl.when(pl.program_id(0) == m)
        def _():
            fill(0, pack_refs[m][0])
            fill(ROWS, pack_refs[m][1])

    scr[...] = mm_tn(mixed_scr[:ROWS], grad_ref[...]) + mm_tn(
        mixed_scr[ROWS:], near_grad_ref[...]
    )
    for k in range(GROUP):
        target = send_ref if k % 2 else keep_ref
        lanes = pl.ds(pl.multiple_of((where_ref[0] ^ k) * LANES, LANES), LANES)
        for e in range(experts):
            target[k // 2, e * head_dim : (e + 1) * head_dim, :] = scr[
                e * LANES : e * LANES + head_dim, lanes
            ].astype(BF16)


def out_weights(where, packs, grad, near_grad, experts, head_dim):
    heads = len(packs)
    rows, width = grad.shape
    depth = experts * head_dim
    shape = (GROUP // 2, heads * depth, width // GROUP)
    spec = pl.BlockSpec((GROUP // 2, depth, width // GROUP), lambda m, w: (0, m, 0))
    return pl.pallas_call(
        functools.partial(out_weights_kernel, experts, head_dim, heads),
        grid_spec=pltpu.PrefetchScalarGridSpec(
            num_scalar_prefetch=1,
            grid=(heads,),
            in_specs=[whole(2, rows, LANES)] * heads + [whole(rows, width)] * 2,
            out_specs=[spec] * 2,
            scratch_shapes=[
                pltpu.VMEM((2 * rows, experts * LANES), BF16),
                pltpu.VMEM((experts * LANES, width), F32),
            ],
        ),
        out_shape=[struct(shape, BF16)] * 2,
        compiler_params=params(),
        cost_estimate=cost(5),
        name="out_weights",
    )(where, *packs, grad, near_grad)


def weights_kernel(
    experts,
    head_dim,
    counts,
    where_ref,
    normed_ref,
    key_ref,
    value_ref,
    gate_ref,
    query_ref,
    table_ref,
    rel_ref,
    w_ref,
    gain_ref,
    bias_ref,
    sums_ref,
    biases_ref,
    keep_ref,
    send_ref,
    small_ref,
    grads_scr,
    sum_scr,
    main_scr,
    rel_scr,
):
    step = pl.program_id(0)
    mem_steps, key_steps, rel_steps = counts
    query = (1 + experts) * LANES

    @pl.when(step == 0)
    def _():
        main_scr[...] = jnp.zeros_like(main_scr)
        sum_scr[...] = jnp.zeros_like(sum_scr)
        rel_scr[...] = jnp.zeros_like(rel_scr)

    def add(columns):
        grads = grads_scr[:, :columns]
        main_scr[:columns, :] += mm_tn(grads, normed_ref[...])
        sum_scr[0:1, :columns] += jnp.sum(grads.astype(F32), axis=0, keepdims=True)

    @pl.when(step < key_steps)
    def _():
        value_grad = value_ref[...]
        grads_scr[:, :LANES] = key_ref[...]
        for e in range(experts):
            gate = gate_ref[:, head_dim + e : head_dim + e + 1]
            grads_scr[:, LANES * (1 + e) : LANES * (2 + e)] = (gate * value_grad).astype(BF16)

    @pl.when(step < mem_steps)
    def _():
        add(query)

    @pl.when((step >= mem_steps) & (step < key_steps))
    def _():
        grads_scr[:, query:] = query_ref[...]
        add(query + LANES)

    @pl.when(step >= key_steps)
    def _():
        rel_scr[...] += mm_tn(rel_ref[...], table_ref[...])

    @pl.when(step == key_steps + rel_steps - 1)
    def _():
        weights = w_ref[...].astype(F32)
        sums = sum_scr[...].T
        bias_one = jnp.sum(weights * sums[:, 0:1], axis=0, keepdims=True)
        inner = jnp.sum(weights * main_scr[...], axis=0, keepdims=True)
        small_ref[...] = jnp.zeros_like(small_ref)
        small_ref[0:1, :] = (inner - bias_ref[...] * bias_one) / gain_ref[...]
        small_ref[1:2, :] = bias_one
        small_ref[2:4, :] = sums_ref[...]
        small_ref[4:6, pl.ds(pl.multiple_of(where_ref[1] * LANES, LANES), LANES)] = biases_ref[...]
        for k in range(GROUP):
            target = send_ref if k % 2 else keep_ref
            at = k // 2
            lanes = pl.ds(pl.multiple_of((where_ref[0] ^ k) * LANES, LANES), LANES)
            row = 0

            def put(source, begin, size):
                target[at, row : row + size, :] = source[begin : begin + size, lanes].astype(BF16)
                return row + size

            for section in range(2 + experts):
                row = put(main_scr, section * LANES, head_dim)
            row = put(rel_scr, 0, head_dim)
            target[at, row:, :] = jnp.concatenate(
                [
                    main_scr[head_dim : head_dim + 8, lanes],
                    main_scr[query + head_dim : query + head_dim + 8, lanes],
                ],
                axis=0,
            ).astype(BF16)


def weight_grads(
    where,
    normed,
    key_grad,
    value_grad,
    gates,
    query_grad,
    table,
    rel_grad,
    w_all,
    gain,
    bias,
    sums_two,
    bias_sums,
    mem,
    head_dim,
    experts,
):
    keys, width = normed.shape
    cols = (2 + experts) * LANES
    big = 4 * ROWS
    mem_steps, key_steps = mem // big, keys // big
    rel_steps = table.shape[0] // big
    counts = (mem_steps, key_steps, rel_steps)
    rows = (3 + experts) * head_dim + 16
    key_row = lambda i, w: (jnp.minimum(i, key_steps - 1), 0)
    tok_row = lambda i, w: (jnp.clip(i - mem_steps, 0, key_steps - mem_steps - 1), 0)
    rel_row = lambda i, w: (jnp.clip(i - key_steps, 0, rel_steps - 1), 0)
    half = GROUP // 2
    return pl.pallas_call(
        functools.partial(weights_kernel, experts, head_dim, counts),
        grid_spec=pltpu.PrefetchScalarGridSpec(
            num_scalar_prefetch=1,
            grid=(key_steps + rel_steps,),
            in_specs=[
                pl.BlockSpec((big, width), key_row),
                pl.BlockSpec((big, LANES), key_row),
                pl.BlockSpec((big, LANES), key_row),
                pl.BlockSpec((big, LANES), key_row),
                pl.BlockSpec((big, LANES), tok_row),
                pl.BlockSpec((big, width), rel_row),
                pl.BlockSpec((big, LANES), rel_row),
                whole(cols, width),
                whole(1, width),
                whole(1, width),
                whole(2, width),
                whole(2, LANES),
            ],
            out_specs=[
                whole(half, rows, LANES),
                whole(half, rows, LANES),
                whole(8, width),
            ],
            scratch_shapes=[
                pltpu.VMEM((big, cols), BF16),
                pltpu.VMEM((8, cols), F32),
                pltpu.VMEM((cols, width), F32),
                pltpu.VMEM((LANES, width), F32),
            ],
        ),
        out_shape=[
            struct((half, rows, LANES), BF16),
            struct((half, rows, LANES), BF16),
            struct((8, width), F32),
        ],
        compiler_params=params(),
        cost_estimate=cost(15),
        name="weight_grads",
    )(
        where,
        normed,
        key_grad,
        value_grad,
        gates,
        query_grad,
        table,
        rel_grad,
        w_all,
        gain,
        bias,
        sums_two,
        bias_sums,
    )


def token_kernel(experts, head_dim, own_ref, far_ref, w_own_ref, w_far_ref, *refs):
    out_refs, grads_scr, total_scr = refs[:2], refs[2], refs[3]
    step = pl.program_id(0)
    query = (1 + experts) * LANES
    cols = query + LANES
    real = lane_of(ROWS) < head_dim

    def part(pack_ref, weights):
        for block in range(2):
            rows = slice(block * ROWS, (block + 1) * ROWS)
            value_pack = pack_ref[block, 1].astype(F32)
            value_grad = jnp.where(real, value_pack, 0.0)
            grads_scr[rows, :LANES] = pack_ref[block, 0]
            for e in range(experts):
                gate = value_pack[:, head_dim + e : head_dim + e + 1]
                grads_scr[rows, LANES * (1 + e) : LANES * (2 + e)] = (gate * value_grad).astype(
                    BF16
                )
            grads_scr[rows, query:] = pack_ref[block, 2]
        return mm(grads_scr[...], weights)

    @pl.when(step == 0)
    def _():
        total_scr[...] = part(own_ref, w_own_ref[:cols, :])

    @pl.when(step == 1)
    def _():
        weights = w_far_ref[...].reshape(-1, w_far_ref.shape[2])
        total = total_scr[...] + part(far_ref, weights[:cols, :])
        out_refs[0][...] = total[:ROWS]
        out_refs[1][...] = total[ROWS:].astype(BF16)


def token_parts(own_pack, far_pack, own_w, far_w, head_dim, experts):
    width = own_w.shape[1]
    rows = 2 * ROWS
    cols = (2 + experts) * LANES
    return pl.pallas_call(
        functools.partial(token_kernel, experts, head_dim),
        grid=(2,),
        in_specs=[
            whole(*own_pack.shape),
            whole(*far_pack.shape),
            whole(*own_w.shape),
            whole(*far_w.shape),
        ],
        out_specs=[whole(ROWS, width)] * 2,
        out_shape=[struct((ROWS, width), F32), struct((ROWS, width), BF16)],
        scratch_shapes=[pltpu.VMEM((rows, cols), BF16), pltpu.VMEM((rows, width), F32)],
        compiler_params=params(),
        cost_estimate=cost(6),
        name="token_parts",
    )(own_pack, far_pack, own_w, far_w)


def token_sum_kernel(z_ref, tok_ref, mid_ref, gain_ref, own_ref, near_ref, out_ref):
    total = own_ref[...] + near_ref[...].astype(F32)
    normal, inv_std = norm_parts(tok_ref[...].astype(F32))
    out_ref[...] = mid_ref[...] + norm_back(total, normal, inv_std, gain_ref[...])


def token_sum(rank, tokens, middle_grad, gain, own, near):
    rows, width = middle_grad.shape
    return pl.pallas_call(
        token_sum_kernel,
        grid_spec=pltpu.PrefetchScalarGridSpec(
            num_scalar_prefetch=1,
            grid=(1,),
            in_specs=[
                pl.BlockSpec((rows, width), lambda i, z: (z[0], 0)),
                whole(rows, width),
                whole(1, width),
                whole(rows, width),
                whole(rows, width),
            ],
            out_specs=whole(rows, width),
        ),
        out_shape=struct((rows, width), F32),
        compiler_params=params(),
        cost_estimate=cost(4),
        name="token_sum",
    )(rank, tokens, middle_grad, gain, own, near)


def swap(array, axis, mask):
    size = lax.axis_size(axis)
    return lax.ppermute(array, axis, [(i, i ^ mask) for i in range(size)])


def plus(left, right):
    return (left.astype(F32) + right.astype(F32)).astype(BF16)


def scatter_first(keep, far):
    return [plus(keep[m], far[m]) for m in range(keep.shape[0])]


def scatter_sends(blocks, unit):
    return [swap(blocks[m], "dp", 2 * m * unit) for m in range(1, len(blocks))]


def scatter_done(own, fars, unit, axis):
    out = own.astype(F32)
    for far in fars:
        out = out + far.astype(F32)
    mask = unit // 2
    while mask:
        size = out.shape[axis] // 2
        bit = (lax.axis_index("dp") // mask) % 2
        mine = lax.dynamic_slice_in_dim(out, bit * size, size, axis)
        theirs = lax.dynamic_slice_in_dim(out, (1 - bit) * size, size, axis)
        out = mine + swap(theirs.astype(BF16), "dp", mask).astype(F32)
        mask //= 2
    return out


def spread(far, *gates):
    pieces = [swap(far, "dp", 2 * m) for m in range(1, GROUP // 2)]
    even = after(pile(far, *pieces), *gates)
    odd = swap(even, "dp", 1)
    return even, odd


def on_device(
    tokens,
    memory,
    segments,
    value_routes,
    output_routes,
    first_gain,
    first_bias,
    second_gain,
    second_bias,
    query_head_weight,
    key_weight,
    position_weight,
    value_weight,
    value_select,
    output_expert_selector,
    output_expert_weight,
    content_bias,
    position_bias,
    up_projection_weight,
    down_projection_weight,
    cotangent,
):
    mem_len = memory.shape[1]
    toks, width = tokens.shape
    head_dim = query_head_weight.shape[2]
    experts = value_select.shape[2]
    hidden = up_projection_weight.shape[1]
    parts = lax.axis_size("tensor")
    rank = lax.axis_index("tensor")
    dp = lax.axis_size("dp")
    at = lax.axis_index("dp")
    others = range(1, parts)
    near, far_shard = 1, 2
    rank_ref = rank.reshape(1).astype(jnp.int32)
    row = lambda v: v.reshape(1, -1)
    lanes = lambda v: jnp.pad(v, ((0, 0), (0, LANES - head_dim)))

    own_out = output_expert_weight[0]
    size = width // GROUP
    own_block = lax.dynamic_slice_in_dim(own_out, (at % GROUP) * size, size, 1)
    far_out = swap(own_block, "tensor", far_shard)
    span = mem_len
    fine = 32
    rates = jnp.exp(jnp.arange(width // 2).astype(F32) * (-2.0 * math.log(10000.0) / width))
    coarse_at = (span - 1 - fine * jnp.arange(span // fine)).astype(F32)[:, None] * rates[None, :]
    fine_at = jnp.arange(fine).astype(F32)[:, None] * rates[None, :]
    sin_a, cos_a = jnp.sin(coarse_at)[:, None, :], jnp.cos(coarse_at)[:, None, :]
    sin_b, cos_b = jnp.sin(fine_at)[None, :, :], jnp.cos(fine_at)[None, :, :]
    sin_table = jnp.concatenate(
        [sin_a * cos_b - cos_a * sin_b, cos_a * cos_b + sin_a * sin_b], axis=2
    )
    sin_table = lax.optimization_barrier(sin_table.reshape(span, width).astype(BF16))
    rel_weight = jnp.concatenate(
        [position_weight[0].T, jnp.zeros((LANES - head_dim, width), BF16)]
    )
    rel_reverse = mm_nt(sin_table, rel_weight).astype(BF16)

    w_all, normed, key_vecs, value_vecs, every, vgate, qc, qp, ogate = project(
        memory[0],
        tokens,
        row(first_gain),
        row(first_bias),
        (
            key_weight[0].T,
            value_select[0].T,
            value_weight[0].T,
            query_head_weight[0].T,
            output_expert_selector[0].T,
        ),
        value_routes[0, :, 0].T,
        output_routes[:, 0].T,
        lanes(content_bias),
        lanes(position_bias),
        experts,
        head_dim,
    )
    steps = toks // ROWS
    seg = segments[0]
    seg_keys = jnp.stack([seg[i * ROWS : i * ROWS + span + ROWS] for i in range(steps)])[:, None]
    seg_keys = after(seg_keys, far_out)
    heads, probs, *packs = attend(
        rank_ref,
        qc,
        qp,
        key_vecs,
        value_vecs,
        rel_reverse,
        seg_keys,
        seg[None, mem_len:],
        ogate,
        head_dim,
    )

    depth = width // dp
    feed_piece = jnp.stack(
        [
            lax.dynamic_slice_in_dim(up_projection_weight, at * depth, depth, 0),
            lax.dynamic_slice_in_dim(down_projection_weight, at * (hidden // dp), hidden // dp, 0),
        ]
    )
    far_feed = swap(feed_piece, "tensor", far_shard)
    far_feed = lax.all_gather(after(far_feed, packs[0]), "dp", axis=0)
    packs = [packs[0], swap(packs[1], "tensor", far_shard)]
    even, odd = spread(after(far_out, qc), packs[1])
    cots = [cotangent, swap(after(cotangent, packs[1]), "tensor", near)]
    piece = w_all.shape[0] // dp
    own_piece = lax.dynamic_slice_in_dim(w_all, at * piece, piece, 0)
    far_w = swap(after(own_piece, packs[1]), "tensor", far_shard)
    group_at = at % GROUP
    where = jnp.stack([group_at // 2, group_at % 2, rank]).astype(jnp.int32)
    full, own_part, near_part = mix(where, packs, own_out, even, odd, experts, head_dim)
    middle, up_in = middle_rows(
        rank_ref,
        tokens,
        after(own_part, far_w, cots[1]),
        swap(near_part, "tensor", near),
        row(second_gain),
        row(second_bias),
    )

    ups = [up_in, swap(up_in, "tensor", near)]
    unit = dp // GROUP
    where_grads = jnp.stack([at // unit, rank]).astype(jnp.int32)
    far_w = lax.all_gather(after(far_w, up_in), "dp", axis=0)
    shards = (up_projection_weight, down_projection_weight, far_feed)
    own_hidden, own_pre, own_result, own_up = feed(ups[0], cots[0], *shards, F32)
    near_hidden, near_pre, near_result, near_up = feed(ups[1], cots[1], *shards, BF16, own_pre)
    back_up = swap(near_up, "tensor", near)
    feed_sums = feed_weights(ups, cots, (own_pre, near_pre), (own_hidden, near_hidden))
    feed_sums = after(feed_sums, far_w, back_up)
    own_up = after(own_up, feed_sums)
    feed_sums = lax.psum_scatter(feed_sums, "dp", scatter_dimension=0, tiled=True)

    middle_grad, attn_grad, sums_two = middle_back(
        own_up, back_up, cotangent, middle, row(second_gain)
    )
    near_grad = swap(attn_grad, "tensor", near)
    backs = heads_back(attn_grad, near_grad, full, packs, experts, head_dim)
    out_keep, out_send = out_weights(where_grads, packs, attn_grad, near_grad, experts, head_dim)
    backs = [after(backs[0], out_keep), swap(backs[1], "tensor", far_shard)]
    back_out = swap(after(near_result, backs[1]), "tensor", near)

    key_grad, value_grad, query_grad, rel_grad, bias_sums, *grad_packs = attend_back(
        rank_ref,
        qc,
        qp,
        key_vecs,
        value_vecs,
        rel_reverse,
        probs,
        heads,
        ogate,
        every,
        vgate,
        backs,
        head_dim,
    )
    out_part = scatter_first(out_keep, swap(out_send, "dp", unit))
    rel_grad = after(rel_grad, *out_part, back_out)
    out_fars = scatter_sends(out_part, unit)
    far_pack = swap(grad_packs[1], "tensor", far_shard)
    keep, send, small = weight_grads(
        where_grads,
        normed,
        key_grad,
        value_grad,
        vgate,
        query_grad,
        sin_table,
        rel_grad,
        w_all,
        row(first_gain),
        row(first_bias),
        sums_two,
        bias_sums,
        mem_len,
        head_dim,
        experts,
    )
    token_own, token_near = token_parts(
        grad_packs[0], far_pack, w_all, after(far_w, keep), head_dim, experts
    )
    send, small = (after(each, token_near, span=20) for each in (send, small))
    token_near = swap(token_near, "tensor", near)
    kept_far = swap(send, "dp", unit)
    small_fars = [swap(small, "tensor", m) for m in others]
    out_fars = [after(far, send) for far in out_fars]
    out_sums = scatter_done(out_part[0], out_fars, unit, 1).reshape(2, experts * head_dim, -1)
    out_low = out_sums[1].astype(BF16)
    feed_own, feed_far = feed_sums[:, : 2 * hidden], feed_sums[:, 2 * hidden :]
    kept_far, feed_far, *small_fars = together(kept_far, feed_far, *small_fars)
    feed_far = swap(feed_far, "tensor", far_shard)
    out_far = swap(out_low, "tensor", far_shard)
    kept = scatter_first(keep, kept_far)
    for far in small_fars:
        small = small + far
    kept_fars = scatter_sends(kept, unit)
    small_fars = [swap(small, "dp", m) for m in range(2, GROUP, 2)]
    feed_far, *fars = together(feed_far, *kept_fars, *small_fars)
    kept_fars, small_fars = fars[: len(fars) // 2], fars[len(fars) // 2 :]
    for far in small_fars:
        small = small + far
    mask = GROUP
    while mask < dp:
        small = small + swap(small, "dp", mask)
        mask *= 2
    small = small + swap(small, "dp", 1)
    kept = scatter_done(kept[0], kept_fars, unit, 1)
    tokens_grad = token_sum(
        rank_ref, tokens, middle_grad, row(first_gain), token_own, token_near
    )
    result = (middle + own_result + after(back_out, keep).astype(F32)).astype(BF16)
    out_w = out_sums[0] + after(out_far, *kept_fars).astype(F32)
    feed_grads = feed_own.astype(F32) + feed_far.astype(F32)
    up_total = feed_grads[:, :hidden]
    down_total = feed_grads[:, hidden:].T
    biases = small[4:6, : parts * LANES].reshape(2, parts, LANES)[:, :, :head_dim]
    marks = [0, 1, 1 + experts, 2 + experts, 3 + experts]
    key_w, value_w, query_w, rel_w = (
        kept[a * head_dim : b * head_dim] for a, b in zip(marks, marks[1:])
    )
    select = marks[-1] * head_dim
    turn = lambda part: part.T[None]
    return (
        result,
        tokens_grad,
        small[0],
        small[1],
        small[2],
        small[3],
        turn(query_w),
        turn(key_w),
        turn(rel_w),
        turn(value_w),
        turn(kept[select : select + experts]),
        turn(kept[select + 8 : select + 8 + experts]),
        out_w[None],
        biases[0],
        biases[1],
        up_total,
        down_total,
    )


def solution(mesh):
    placed = (
        P("dp", None),
        P("dp", None, None),
        P("dp", None),
        P("dp", None, "tensor", None),
        P("dp", "tensor", None),
        P(),
        P(),
        P(),
        P(),
        P("tensor", None, None),
        P("tensor", None, None),
        P("tensor", None, None),
        P("tensor", None, None),
        P("tensor", None, None),
        P("tensor", None, None),
        P("tensor", None, None),
        P("tensor", None),
        P("tensor", None),
        P(None, "tensor"),
        P("tensor", None),
        P(("dp", "tensor"), None),
    )
    return jax.shard_map(
        on_device,
        mesh=mesh,
        in_specs=placed,
        out_specs=(
            P(("dp", "tensor"), None),
            P(("dp", "tensor"), None),
            P(),
            P(),
            P(),
            P(),
            P("tensor", "dp", None),
            P("tensor", "dp", None),
            P("tensor", "dp", None),
            P("tensor", "dp", None),
            P("tensor", "dp", None),
            P("tensor", "dp", None),
            P("tensor", None, "dp"),
            P(),
            P(),
            P("dp", "tensor"),
            P("tensor", "dp"),
        ),
        check_vma=False,
    )
```
